32 devices in a mesh: depth: 8 (over z, x), batch: 4 (over y, core).
Axes of the slice: x: 2, y: 2, z: 4, core: 2. Of those that a mesh axis runs over, the one named last changes fastest.
Arguments:
- cpoint_guess: float32 [8, 4, 32, 4096], P('depth', 'batch'), may hold values from -6 to 6
- adjoint_guess: float32 [8, 4, 32, 4096], P('depth', 'batch'), may hold values from -6 to 6
- weights: float32 [64, 32, 32], P('depth'), may hold values from -0.5 to 0.5
- biases: float32 [64, 32], P('depth'), may hold values from -3 to 3
- diffusion: float32 [32], replicated, may hold values from 0.02 to 0.25
- section_len: int32 [8], replicated, may hold values from 1 to 8, 24 in all
Outputs:
- states_out: float32 [8, 4, 32, 4096], P('depth', 'batch')
- adjoint_out: float32 [8, 4, 32, 4096], P('depth', 'batch')
- grad_weights: float32 [64, 32, 32], P('depth')
- grad_biases: float32 [64, 32], P('depth')
The draws below stay inside these ranges and needn't reach their ends.
Inputs may be any that keep to these rules, and one draw needn't show every extreme that they name: `section_len`: each of the 8 sections holds 1 to 8 layers, 24 in all, and one section holds exactly 8.
All inputs are finite; a program needn't handle non-finite values.
Results may differ from the reference program's by a relative error of at most 0.0003.
Values sent between devices are 32-bit elements; how exact they have to be, the bound alone decides.
No kernel may reach another device: no remote copies, remote signals or barrier semaphores. Data moves between devices by JAX's collectives and lax.ppermute only.
A program may use at most 128 MiB of HBM per device.

```python
import math
import jax
import jax.numpy as jnp
import numpy as np
from jax import lax

C = 32
IMG_H = 64
IMG_W = 64
PIX = 4096
MOST = 8
LAYERS = 24
IMAGES = 4
N_DEPTH = 8


def steps_of(stream_key, shape, shards, smallest, top_value):
    gain, own = 1.0, jax.random.fold_in(stream_key, 6)
    for axis_at, parts in shards:
        steps = jnp.exp(jax.random.uniform(jax.random.fold_in(own, axis_at), (parts,), jnp.float32, smallest / len(shards), top_value / len(shards)))
        gain = gain * jnp.repeat(steps, shape[axis_at] // parts).reshape([-1 if axis == axis_at else 1 for axis in range(len(shape))])
    return gain


def length_profile(count, total, bound, slope):
    weights = [(1 << 20) // math.isqrt(rank ** slope) + 1 for rank in range(2, count + 1)]
    surplus, holding = total - bound - (count - 1), [1] * (count - 1)
    while surplus > 0:
        free = [i for i in range(count - 1) if holding[i] < bound]
        pool, budget = sum([weights[i] for i in free]), surplus
        for i in free:
            addition = min(bound - holding[i], max(1, budget * weights[i] // pool), surplus)
            holding[i] = holding[i] + addition
            surplus = surplus - addition
    return np.array([bound] + holding)


def uneven(key, number_of, total, reach, slope):
    if number_of == 2:
        one = jax.random.randint(key, (), max(1, total - reach), min(reach, total - 1) + 1)
        return jnp.stack([one, total - one])
    tallies = jnp.asarray(length_profile(number_of, total, reach, slope), jnp.int32)
    couples = (number_of - 1) // 2
    giver, taker = tallies[1:1 + 2 * couples:2], tallies[2:2 + 2 * couples:2]
    slack = jnp.minimum(giver - 1, reach - taker)
    moved = jax.random.randint(jax.random.fold_in(key, 1), (couples,), 0, 1 << 20) % (slack + 1)
    tallies = tallies.at[1:1 + 2 * couples:2].set(giver - moved).at[2:2 + 2 * couples:2].set(taker + moved)
    return tallies[jax.random.permutation(jax.random.fold_in(key, 2), number_of)]


def normal_values(stream_key, dims, scale, reach, cuts=(), dtype=jnp.bfloat16):
    array = scale * jax.random.normal(stream_key, dims, jnp.float32)
    if cuts:
        array = array * steps_of(stream_key, dims, cuts, -0.22, 0.18)
    return jnp.clip(array, -reach, reach).astype(dtype)


def setup_inputs(seed: int = 0) -> dict:
    arg_keys = jax.random.split(jax.random.key(seed), 7)
    cpoint_guess = normal_values(arg_keys[0], (N_DEPTH, IMAGES, C, PIX), 1.0, 6.0, ((0, 8), (1, 4)), jnp.float32)
    adjoint_guess = normal_values(arg_keys[1], (N_DEPTH, IMAGES, C, PIX), 1.0, 6.0, ((0, 8), (1, 4)), jnp.float32)
    weights = normal_values(arg_keys[2], (N_DEPTH * MOST, C, C), (4 * C) ** -0.5, 0.5, ((0, 8),), jnp.float32)
    biases = normal_values(arg_keys[3], (N_DEPTH * MOST, C), 0.5, 3.0, ((0, 8),), jnp.float32)
    diffusion = jnp.clip(jnp.exp(jax.random.uniform(arg_keys[4], (C,), jnp.float32, math.log(0.02), math.log(0.25))), 0.02, 0.25)
    section_len = uneven(arg_keys[5], N_DEPTH, LAYERS, MOST, 2).astype(jnp.int32)
    return dict(cpoint_guess=cpoint_guess, adjoint_guess=adjoint_guess, weights=weights, biases=biases, diffusion=diffusion, section_len=section_len)


def laplace(states):
    shaped = states.reshape(states.shape[:-1] + (IMG_H, IMG_W))
    padded = jnp.pad(shaped, [(0, 0)] * (shaped.ndim - 2) + [(1, 1), (1, 1)])
    beside_all = padded[..., 2:, 1:-1] + padded[..., :-2, 1:-1] + padded[..., 1:-1, 2:] + padded[..., 1:-1, :-2]
    return (beside_all - 4.0 * shaped).reshape(states.shape)

def apply_layer(states, matrix, offset, diffusion, factor):
    pre_act = jnp.einsum('ij,bjp->bip', matrix, states, precision=lax.Precision.HIGHEST) + offset[None, :, None]
    mixed = jnp.einsum('ji,bjp->bip', matrix, jnp.tanh(pre_act), precision=lax.Precision.HIGHEST)
    return states + (factor * diffusion)[None, :, None] * laplace(states) - factor * mixed

def fine_factor():
    return jnp.asarray(1.0, jnp.float32) / MOST

def section(states, matrices, offsets, diffusion, layer_count):
    factor = fine_factor()

    def advance(position, current):
        changed = apply_layer(current, matrices[position], offsets[position], diffusion, factor)
        return jnp.where(position < layer_count - 1, changed, current)
    relaxed = lax.fori_loop(0, MOST - 1, advance, states)
    final_slot = layer_count - 1
    return apply_layer(relaxed, matrices[final_slot], offsets[final_slot], diffusion, factor)

def coarse(states, matrix, offset, diffusion, layer_count):
    factor = layer_count.astype(jnp.float32) / MOST
    return apply_layer(states, matrix, offset, diffusion, factor)

def reference(cpoint_guess, adjoint_guess, weights, biases, diffusion, section_len):
    sections = N_DEPTH
    matrices = weights.reshape(sections, MOST, C, C)
    offsets = biases.reshape(sections, MOST, C)

    def forward_one(packed):
        states, mats, offs, layer_count = packed
        return section(states, mats, offs, diffusion, layer_count)
    pushed = lax.map(forward_one, (cpoint_guess, matrices, offsets, section_len))
    cpoints = jnp.concatenate([cpoint_guess[:1], pushed[:-1]], 0)
    second = lax.map(forward_one, (cpoints, matrices, offsets, section_len))

    def tau_one(packed):
        states, mat, off, layer_count = packed
        return coarse(states, mat, off, diffusion, layer_count)
    anchors = lax.map(tau_one, (cpoints, matrices[:, 0], offsets[:, 0], section_len))
    taus = second - anchors

    def coarse_step(current, packed):
        mat, off, layer_count, tau_here = packed
        return (coarse(current, mat, off, diffusion, layer_count) + tau_here, current)
    _, states_out = lax.scan(coarse_step, cpoints[0], (matrices[:, 0], offsets[:, 0], section_len, taus))

    def back_start(packed):
        states, mats, offs, layer_count, cotangent = packed
        _, pullback = jax.vjp(lambda start_state: section(start_state, mats, offs, diffusion, layer_count), states)
        return pullback(cotangent)[0]
    lam_start = lax.map(back_start, (cpoints, matrices, offsets, section_len, adjoint_guess))
    lam_end = jnp.concatenate([lam_start[1:], adjoint_guess[-1:]], 0)

    def back_full(packed):
        states, mats, offs, layer_count, cotangent = packed
        _, pullback = jax.vjp(lambda start_state, mat_all, off_all: section(start_state, mat_all, off_all, diffusion, layer_count), states, mats, offs)
        return pullback(cotangent)
    adjoint_out, grad_mats, grad_offs = lax.map(back_full, (cpoints, matrices, offsets, section_len, lam_end))
    return (states_out, adjoint_out, grad_mats.reshape(sections * MOST, C, C), grad_offs.reshape(sections * MOST, C))
```

```python
import functools

import jax
import jax.numpy as jnp
from jax import lax
from jax.experimental import pallas as pl
from jax.experimental.pallas import tpu as pltpu
from jax.sharding import PartitionSpec as P

IMG = 64
LANES = 128
CHUNK = 512
F32 = jnp.float32
BF16 = jnp.bfloat16


def split(x):
    hi = x.astype(BF16)
    lo = (x - hi.astype(F32)).astype(BF16)
    return hi, lo


def stack3(hi, lo):
    return jnp.concatenate([hi, lo, hi], axis=0)


def left_factor(matrix):
    hi = matrix.astype(BF16).astype(F32)
    return jnp.concatenate([hi, hi, matrix - hi], axis=1).astype(BF16)


def mm(a, b):
    return jnp.dot(a, b, preferred_element_type=F32)


def mm_nt(a, b):
    return lax.dot_general(a, b, (((1,), (1,)), ((), ())), preferred_element_type=F32)


def lane_masks(rows):
    lane = lax.broadcasted_iota(jnp.int32, (rows, LANES), 1)
    col = lane % IMG
    return col > 0, col < IMG - 1, lane < IMG


def neighbours(left, mid, right, masks):
    not_first, not_last, upper = masks
    pieces = [left] + [mid[:, k : k + LANES] for k in range(0, mid.shape[1], LANES)] + [right]
    swapped = [pltpu.roll(piece, IMG, 1) for piece in pieces]
    sums = []
    for k in range(1, len(pieces) - 1):
        piece = pieces[k]
        beside = jnp.where(not_first, pltpu.roll(piece, 1, 1), 0.0)
        beside += jnp.where(not_last, pltpu.roll(piece, LANES - 1, 1), 0.0)
        beside += swapped[k] + jnp.where(upper, swapped[k - 1], swapped[k + 1])
        sums.append(beside)
    return jnp.concatenate(sums, axis=1)


def sweep(buf, width, step):
    rows = buf.shape[0]
    masks = lane_masks(rows)
    before = buf[:, 0:LANES]
    for start in range(0, width, CHUNK):
        size = min(CHUNK, width - start)
        at = LANES + start
        mid = buf[:, at : at + size]
        after = buf[:, at + size : at + size + LANES]
        around = neighbours(before, mid, after, masks)
        before = mid[:, size - LANES :]
        buf[:, at : at + size] = step(start, size, mid, around)


def prepare(w_ref, wl_ref, wt_ref, factor):
    for slot in range(w_ref.shape[0]):
        matrix = w_ref[slot]
        wl_ref[slot] = left_factor(matrix)
        wt_ref[slot] = left_factor((factor * matrix).T)


def bias_of(bt_ref, slot):
    table = bt_ref[...]
    pick = lax.broadcasted_iota(jnp.int32, table.shape, 1) == slot
    return jnp.sum(jnp.where(pick, table, 0.0), axis=1, keepdims=True)


def forward_layer(buf, width, wl, wt, bias, spread, t_out=None, u_out=None):
    keep = 1.0 - 4.0 * spread

    def step(start, size, mid, around):
        hi, lo = split(mid)
        t_hi, t_lo = split(jnp.tanh(mm(wl, stack3(hi, lo)) + bias))
        if t_out is not None:
            t_out(start, size, t_hi, t_lo)
        if u_out is not None:
            u_out(start, size, hi, lo)
        return mid * keep + around * spread - mm(wt, stack3(t_hi, t_lo))

    sweep(buf, width, step)


def run_forward(buf, width, wl_ref, wt_ref, bt_ref, spread, count, t_refs=None, u_refs=None):
    def saver(refs, slot):
        if refs is None:
            return None

        def save(start, size, hi, lo):
            refs[0][slot, :, start : start + size] = hi
            refs[1][slot, :, start : start + size] = lo

        return save

    @pl.loop(0, count)
    def _(slot):
        forward_layer(
            buf, width, wl_ref[slot], wt_ref[slot], bias_of(bt_ref, slot), spread,
            saver(t_refs, slot), saver(u_refs, slot),
        )


def run_backward(buf, width, wl_ref, wt_ref, spread, count, t_refs, u_refs=None, grads=None):
    keep = 1.0 - 4.0 * spread

    @pl.loop(0, count)
    def _(passed):
        slot = count - 1 - passed
        wl, wt = wl_ref[slot], wt_ref[slot]
        rows = buf.shape[0]
        total = [None, None]

        def step(start, size, mid, around):
            hi, lo = split(mid)
            t_hi = t_refs[0][slot, :, start : start + size]
            t_lo = t_refs[1][slot, :, start : start + size]
            t = t_hi.astype(F32) + t_lo.astype(F32)
            q = (1.0 - t * t) * mm(wl, stack3(hi, lo))
            q_hi, q_lo = split(q)
            if grads is not None:
                u_hi = u_refs[0][slot, :, start : start + size]
                u_lo = u_refs[1][slot, :, start : start + size]
                left = jnp.concatenate([t_hi, t_lo, q_hi, q_lo], axis=0)
                right = jnp.concatenate([hi, lo, u_hi, u_lo], axis=0)
                part = mm_nt(left, right)
                part_b = sum(q[:, k : k + LANES] for k in range(0, size, LANES))
                total[0] = part if total[0] is None else total[0] + part
                total[1] = part_b if total[1] is None else total[1] + part_b
            return mid * keep + around * spread - mm(wt, stack3(q_hi, q_lo))

        sweep(buf, width, step)
        if grads is not None:
            gw_ref, gb_ref, factor = grads
            g = total[0]
            a, b, c, d = rows, 2 * rows, 3 * rows, 4 * rows
            gw = g[0:a, 0:a] + g[0:a, a:b] + g[a:b, 0:a]
            gw += g[b:c, b:c] + g[b:c, c:d] + g[c:d, b:c]
            gw_ref[slot] = -factor * gw
            column = jnp.sum(total[1], axis=1, keepdims=True)
            pick = lax.broadcasted_iota(jnp.int32, gb_ref.shape, 1) == slot
            gb_ref[...] = jnp.where(pick, -factor * column, gb_ref[...])


def fill(buf, value):
    rows, width = value.shape
    zero = jnp.zeros((rows, LANES), F32)
    buf[:, 0:LANES] = zero
    buf[:, LANES + width :] = zero
    buf[:, LANES : LANES + width] = value


def inner(buf):
    return buf[:, LANES : buf.shape[1] - LANES]


def push_kernel(len_ref, guess_ref, w_ref, bt_ref, diff_ref, out_ref, buf, wl, wt):
    most = w_ref.shape[0]
    factor = 1.0 / most
    own = lax.axis_index("depth")
    prepare(w_ref, wl, wt, factor)
    fill(buf, guess_ref[...])
    run_forward(buf, guess_ref.shape[1], wl, wt, bt_ref, factor * diff_ref[...], len_ref[own])
    out_ref[...] = inner(buf)


def tau_kernel(len_ref, point_ref, w_ref, bt_ref, diff_ref, out_ref, buf, wl, wt):
    most = w_ref.shape[0]
    factor = 1.0 / most
    own = lax.axis_index("depth")
    count = len_ref[jnp.minimum(own + 1, lax.axis_size("depth") - 1)]
    width = point_ref.shape[1]
    prepare(w_ref, wl, wt, factor)
    point = point_ref[...]
    fill(buf, point)
    run_forward(buf, width, wl, wt, bt_ref, factor * diff_ref[...], count)
    out_ref[...] = inner(buf)

    @pl.when(own > 0)
    def _():
        coarse_factor = count.astype(F32) * factor
        buf[:, LANES : LANES + width] = point_ref[...]
        forward_layer(
            buf, width, wl[0], left_factor((coarse_factor * w_ref[0]).T), bias_of(bt_ref, 0),
            coarse_factor * diff_ref[...],
        )
        out_ref[...] = out_ref[...] - inner(buf)


def adjoint_kernel(
    len_ref, guess_ref, before_ref, after_ref, adj_ref, adj_after_ref,
    w_ref, bt_ref, w_before_ref, bt_before_ref, w_after_ref, bt_after_ref, diff_ref,
    point_ref, adj_out_ref, gw_ref, gb_ref,
    buf, wl, wt, t_hi, t_lo, u_hi, u_lo,
):
    most = w_ref.shape[0]
    factor = 1.0 / most
    own = lax.axis_index("depth")
    last = lax.axis_size("depth") - 1
    width = guess_ref.shape[1]
    spread = factor * diff_ref[...]
    gw_ref[...] = jnp.zeros_like(gw_ref)
    gb_ref[...] = jnp.zeros_like(gb_ref)

    @pl.when(own < last)
    def _():
        count = len_ref[jnp.minimum(own + 1, last)]
        prepare(w_after_ref, wl, wt, factor)
        fill(buf, after_ref[...])
        run_forward(buf, width, wl, wt, bt_after_ref, spread, count, (t_hi, t_lo))
        fill(buf, adj_after_ref[...])
        run_backward(buf, width, wl, wt, spread, count, (t_hi, t_lo))
        adj_out_ref[...] = inner(buf)

    @pl.when(own == last)
    def _():
        adj_out_ref[...] = adj_ref[...]

    @pl.when(own > 0)
    def _():
        count = len_ref[jnp.maximum(own - 1, 0)]
        prepare(w_before_ref, wl, wt, factor)
        fill(buf, before_ref[...])
        run_forward(buf, width, wl, wt, bt_before_ref, spread, count)
        point_ref[...] = inner(buf)

    @pl.when(own == 0)
    def _():
        point_ref[...] = guess_ref[...]

    count = len_ref[own]
    prepare(w_ref, wl, wt, factor)
    fill(buf, point_ref[...])
    run_forward(buf, width, wl, wt, bt_ref, spread, count, (t_hi, t_lo), (u_hi, u_lo))
    fill(buf, adj_out_ref[...])
    run_backward(
        buf, width, wl, wt, spread, count, (t_hi, t_lo), (u_hi, u_lo), (gw_ref, gb_ref, factor)
    )
    adj_out_ref[...] = inner(buf)


def chain_kernel(sources, most, len_ref, point_ref, w0_ref, bt0_ref, diff_ref, *rest):
    items = rest[: len(sources)]
    out_ref, buf, held, sem = rest[len(sources) :]
    own = lax.axis_index("depth")
    count = held.shape[0]
    width = point_ref.shape[1]
    copies = [
        pltpu.make_async_copy(item, held.at[source(own)], sem.at[k])
        for k, (item, source) in enumerate(zip(items, sources))
    ]
    for copy in copies:
        copy.start()
    for copy in copies:
        copy.wait()
    fill(buf, held[0])

    @pl.loop(2, own)
    def _(section):
        factor = len_ref[section].astype(F32) * (1.0 / most)
        entry = lax.rem(section - own + count, count)
        matrix = w0_ref[entry]
        forward_layer(
            buf, width, left_factor(matrix), left_factor((factor * matrix).T),
            bias_of(bt0_ref, entry), factor * diff_ref[...],
        )
        buf[:, LANES : LANES + width] = inner(buf) + held[section - 1]

    @pl.when(own < 2)
    def _():
        out_ref[...] = point_ref[...]

    @pl.when(own >= 2)
    def _():
        out_ref[...] = inner(buf)


SMEM = pl.BlockSpec(memory_space=pltpu.SMEM)
VMEM = pl.BlockSpec(memory_space=pltpu.VMEM)
ANY = pl.BlockSpec(memory_space=pl.ANY)


def call(kernel, out_shape, in_specs, scratch, flops, name):
    return pl.pallas_call(
        kernel,
        out_shape=out_shape,
        in_specs=in_specs,
        out_specs=jax.tree.map(lambda _: VMEM, out_shape),
        scratch_shapes=scratch,
        compiler_params=pltpu.CompilerParams(vmem_limit_bytes=48 * 2**20),
        cost_estimate=pl.CostEstimate(flops=flops, bytes_accessed=2**21, transcendentals=0),
        name=name,
    )


def shifted(value, steps):
    count = lax.axis_size("depth")
    first, end = max(0, -steps), min(count, count - steps)
    return lax.ppermute(value, "depth", [(s, s + steps) for s in range(first, end)])


def gather_small(value):
    count = lax.axis_size("depth")
    have, held = 1, value[None]
    while have < count:
        take = min(have, count - have)
        more = lax.ppermute(held[:take], "depth", [((s + have) % count, s) for s in range(count)])
        held = jnp.concatenate([held, more], axis=0)
        have += take
    return held


def batch_sum(values):
    count = lax.axis_size("batch")
    if count & (count - 1):
        return lax.psum(values, "batch")
    gap = 1
    while gap < count:
        pairs = [(s, s ^ gap) for s in range(count)]
        values = jax.tree.map(lambda v: v + lax.ppermute(v, "batch", pairs), values)
        gap *= 2
    return values


def body(cpoint_guess, adjoint_guess, weights, biases, diffusion, section_len):
    count = lax.axis_size("depth")
    most, rows, _ = weights.shape
    width = cpoint_guess.shape[-1]
    guess, adjoint = cpoint_guess[0, 0], adjoint_guess[0, 0]
    diff = diffusion[:, None]
    state = jax.ShapeDtypeStruct((rows, width), F32)
    buffer = pltpu.VMEM((rows, width + 2 * LANES), F32)
    factors = [pltpu.VMEM((most, rows, 3 * rows), BF16)] * 2

    packed = jnp.concatenate([weights, biases[:, None, :]], axis=1)
    packed_after = shifted(packed, -1)
    packed_before = shifted(packed, 1)
    adj_after = shifted(adjoint, -1)
    before = shifted(guess, 1)
    packed0 = gather_small(packed[0])

    def parts(array):
        return array[:, :rows, :], array[:, rows, :].T

    w_after, bt_after = parts(packed_after)
    w_before, bt_before = parts(packed_before)
    w_zero, bt_zero = parts(packed0)
    bt = biases.T

    layer = 16 * rows * rows * width
    after = call(push_kernel, state, [SMEM, VMEM, VMEM, VMEM, VMEM], [buffer, *factors], 4 * layer, "push")(
        section_len, guess, weights, bt, diff
    )
    item = call(tau_kernel, state, [SMEM, VMEM, VMEM, VMEM, VMEM], [buffer, *factors], 4 * layer, "tau")(
        section_len, after, w_after, bt_after, diff
    )

    ring = list(range(0, count, 2)) + list(range(1, count, 2))[::-1]
    place = {device: k for k, device in enumerate(ring)}
    forth = [(ring[k], ring[(k + 1) % count]) for k in range(count)]
    back = [(b, a) for a, b in forth]

    def source(shift):
        table = [ring[(place[d] - shift) % count] for d in range(count)]

        def at(own):
            found = jnp.int32(0)
            for d in range(count):
                found = jnp.where(own == d, table[d], found)
            return found

        return at

    items, sources = [item], [source(0)]
    ahead = behind = item
    for k in range(1, count // 2 + 1):
        ahead = lax.ppermute(ahead, "depth", forth)
        items.append(ahead)
        sources.append(source(k))
        if 2 * k < count:
            behind = lax.ppermute(behind, "depth", back)
            items.append(behind)
            sources.append(source(-k))

    saved = [pltpu.VMEM((most, rows, width), BF16)] * 4
    point, adjoint_out, gw, gbt = call(
        adjoint_kernel,
        [state, state, jax.ShapeDtypeStruct(weights.shape, F32), jax.ShapeDtypeStruct((rows, most), F32)],
        [SMEM] + [VMEM] * 12, [buffer, *factors, *saved], 20 * layer, "adjoint",
    )(
        section_len, guess, before, after, adjoint, adj_after,
        weights, bt, w_before, bt_before, w_after, bt_after, diff,
    )
    gw, gbt = batch_sum((gw, gbt))

    states = call(
        functools.partial(chain_kernel, sources, most), state,
        [SMEM, VMEM, VMEM, VMEM, VMEM] + [ANY] * count,
        [buffer, pltpu.VMEM((count, rows, width), F32), pltpu.SemaphoreType.DMA((count,))],
        4 * layer, "chain",
    )(section_len, point, w_zero, bt_zero, diff, *items)
    return states[None, None], adjoint_out[None, None], gw, gbt.T


def solution(mesh):
    state = P("depth", "batch", None, None)
    return jax.shard_map(
        body,
        mesh=mesh,
        in_specs=(state, state, P("depth", None, None), P("depth", None), P(), P()),
        out_specs=(state, state, P("depth", None, None), P("depth", None)),
        check_vma=False,
    )
```

```python
import functools

import jax
import jax.numpy as jnp
from jax import lax
from jax.experimental import pallas as pl
from jax.experimental.pallas import tpu as pltpu
from jax.sharding import PartitionSpec as P

IMG = 64
LANES = 128
CHUNK = 256
GRAD_CHUNK = 2048
F32 = jnp.float32
BF16 = jnp.bfloat16


def split(x):
    hi = x.astype(BF16)
    lo = (x - hi.astype(F32)).astype(BF16)
    return hi, lo


def stack3(hi, lo):
    return jnp.concatenate([hi, lo, hi], axis=0)


def left_factor(matrix):
    hi = matrix.astype(BF16).astype(F32)
    return jnp.concatenate([hi, hi, matrix - hi], axis=1).astype(BF16)


def mm(a, b):
    return jnp.dot(a, b, preferred_element_type=F32)


def mm_nt(a, b):
    return lax.dot_general(a, b, (((1,), (1,)), ((), ())), preferred_element_type=F32)


def lane_masks(rows):
    lane = lax.broadcasted_iota(jnp.int32, (rows, LANES), 1)
    col = lane % IMG
    return col > 0, col < IMG - 1, lane < IMG


def neighbours(left, mid, right, masks):
    not_first, not_last, upper = masks
    pieces = [left] + [mid[:, k : k + LANES] for k in range(0, mid.shape[1], LANES)] + [right]
    swapped = [pltpu.roll(piece, IMG, 1) for piece in pieces]
    sums = []
    for k in range(1, len(pieces) - 1):
        piece = pieces[k]
        beside = jnp.where(not_first, pltpu.roll(piece, 1, 1), 0.0)
        beside += jnp.where(not_last, pltpu.roll(piece, LANES - 1, 1), 0.0)
        beside += swapped[k] + jnp.where(upper, swapped[k - 1], swapped[k + 1])
        sums.append(beside)
    return jnp.concatenate(sums, axis=1)


def sweep(buf, width, step, chunk=CHUNK):
    rows = buf.shape[0]
    masks = lane_masks(rows)
    before = buf[:, 0:LANES]
    for start in range(0, width, chunk):
        size = min(chunk, width - start)
        at = LANES + start
        mid = buf[:, at : at + size]
        after = buf[:, at + size : at + size + LANES]
        around = neighbours(before, mid, after, masks)
        before = mid[:, size - LANES :]
        buf[:, at : at + size] = step(start, size, mid, around)


def prepare(p_ref, wl_ref, wt_ref, factor):
    rows = p_ref.shape[2]
    for slot in range(p_ref.shape[0]):
        matrix = p_ref[slot, :rows, :]
        wl_ref[slot] = left_factor(matrix)
        wt_ref[slot] = left_factor((factor * matrix).T)


def column(row):
    n = row.shape[1]
    same = lax.broadcasted_iota(jnp.int32, (n, n), 0) == lax.broadcasted_iota(jnp.int32, (n, n), 1)
    return jnp.sum(jnp.where(same, row, 0.0), axis=1, keepdims=True)


def bias_of(p_ref, slot):
    rows = p_ref.shape[2]
    return column(p_ref[slot, rows : rows + 1, :])


def forward_layer(buf, width, wl, wt, bias, spread, t_out=None, u_out=None):
    keep = 1.0 - 4.0 * spread

    def step(start, size, mid, around):
        hi, lo = split(mid)
        t_hi, t_lo = split(jnp.tanh(mm(wl, stack3(hi, lo)) + bias))
        if t_out is not None:
            t_out(start, size, t_hi, t_lo)
        if u_out is not None:
            u_out(start, size, hi, lo)
        return mid * keep + around * spread - mm(wt, stack3(t_hi, t_lo))

    sweep(buf, width, step)


def run_forward(buf, width, p_ref, wl_ref, wt_ref, spread, count, t_refs=None, u_refs=None):
    def saver(refs, slot):
        if refs is None:
            return None

        def save(start, size, hi, lo):
            refs[0][slot, :, start : start + size] = hi
            refs[1][slot, :, start : start + size] = lo

        return save

    @pl.loop(0, count)
    def _(slot):
        forward_layer(
            buf, width, wl_ref[slot], wt_ref[slot], bias_of(p_ref, slot), spread,
            saver(t_refs, slot), saver(u_refs, slot),
        )


def run_backward(buf, width, wl_ref, wt_ref, spread, count, t_refs, u_refs=None, grads=None):
    keep = 1.0 - 4.0 * spread

    @pl.loop(0, count)
    def _(passed):
        slot = count - 1 - passed
        wl, wt = wl_ref[slot], wt_ref[slot]
        rows = buf.shape[0]
        total = [None, None]

        def step(start, size, mid, around):
            hi, lo = split(mid)
            t_hi = t_refs[0][slot, :, start : start + size]
            t_lo = t_refs[1][slot, :, start : start + size]
            t = t_hi.astype(F32) + t_lo.astype(F32)
            q = (1.0 - t * t) * mm(wl, stack3(hi, lo))
            q_hi, q_lo = split(q)
            if grads is not None:
                u_hi = u_refs[0][slot, :, start : start + size]
                u_lo = u_refs[1][slot, :, start : start + size]
                left = jnp.concatenate([t_hi, t_lo, q_hi, q_lo], axis=0)
                right = jnp.concatenate([hi, lo, u_hi, u_lo], axis=0)
                part = mm_nt(left, right)
                part_b = sum(q[:, k : k + LANES] for k in range(0, size, LANES))
                total[0] = part if total[0] is None else total[0] + part
                total[1] = part_b if total[1] is None else total[1] + part_b
            return mid * keep + around * spread - mm(wt, stack3(q_hi, q_lo))

        sweep(buf, width, step, CHUNK if grads is None else GRAD_CHUNK)
        if grads is not None:
            g_ref, factor = grads
            g = total[0]
            a, b, c, d = rows, 2 * rows, 3 * rows, 4 * rows
            gw = g[0:a, 0:a] + g[0:a, a:b] + g[a:b, 0:a]
            gw += g[b:c, b:c] + g[b:c, c:d] + g[c:d, b:c]
            g_ref[slot, :, 0:rows] = -factor * gw
            g_ref[slot, :, rows : rows + 1] = -factor * jnp.sum(total[1], axis=1, keepdims=True)


def fill(buf, value):
    rows, width = value.shape
    zero = jnp.zeros((rows, LANES), F32)
    buf[:, 0:LANES] = zero
    buf[:, LANES + width :] = zero
    buf[:, LANES : LANES + width] = value


def inner(buf):
    return buf[:, LANES : buf.shape[1] - LANES]


class Plan:
    def __init__(self, count):
        self.count = count
        self.items = count - 2
        self.hosts = count // 2
        self.first = count // 4
        self.block = IMG // self.hosts
        self.rows = min(IMG, self.block + 2 * (count - 4))
        self.rows += self.rows % 2
        self.results = count - 3
        self.local = (self.first - 3) % self.results

    def window(self, host):
        start = host * self.block - (self.count - 4)
        return jnp.clip(start - start % 2, 0, IMG - self.rows)

    def in_pairs(self, shift):
        return [((h + shift) % self.items, h + self.first) for h in range(self.hosts)]

    def out_pairs(self, shift):
        pairs = [(h + self.first, 3 + (h + shift) % self.results) for h in range(self.hosts)]
        pairs = [(s, d) for s, d in pairs if s != d]
        return pairs + ([(0, 2)] if shift < self.hosts else [])


def lanes(row, size):
    return pl.ds(pl.multiple_of(row * IMG, LANES), size * IMG)


def push_kernel(len_ref, guess_ref, p_ref, diff_ref, out_ref, buf, wl, wt):
    factor = 1.0 / p_ref.shape[0]
    own = lax.axis_index("depth")
    prepare(p_ref, wl, wt, factor)
    fill(buf, guess_ref[...])
    run_forward(buf, guess_ref.shape[1], p_ref, wl, wt, factor * diff_ref[...], len_ref[own])
    out_ref[...] = inner(buf)


def tau_kernel(plan, len_ref, point_ref, p_ref, p2_ref, diff_ref, second_ref, *rest):
    msgs, (buf, wl, wt, whole) = rest[:-4], rest[-4:]
    most, _, rows = p_ref.shape
    factor = 1.0 / most
    own = lax.axis_index("depth")
    count = len_ref[jnp.minimum(own + 1, plan.count - 1)]
    width = point_ref.shape[1]
    prepare(p_ref, wl, wt, factor)
    fill(buf, point_ref[...])
    run_forward(buf, width, p_ref, wl, wt, factor * diff_ref[...], count)
    second_ref[...] = inner(buf)

    def coarse(q_ref, length):
        scale = length.astype(F32) * factor
        matrix = q_ref[0, :rows, :]
        forward_layer(
            buf, width, left_factor(matrix), left_factor((scale * matrix).T), bias_of(q_ref, 0),
            scale * diff_ref[...],
        )

    @pl.when(own > 0)
    def _():
        buf[:, LANES : LANES + width] = point_ref[...]
        coarse(p_ref, count)
        whole[...] = second_ref[...] - inner(buf)

    @pl.when(own == 0)
    def _():
        coarse(p2_ref, len_ref[2])
        whole[...] = inner(buf)

    size = plan.rows * IMG
    bias = bias_of(p_ref, 0)
    for shift, msg in enumerate(msgs):
        host = lax.rem(own - shift + 2 * plan.items, plan.items)
        start = plan.window(jnp.minimum(host, plan.hosts - 1))
        msg[:, 0:size] = whole[:, lanes(start, plan.rows)]
        msg[:, size : size + rows] = p_ref[0, :rows, :]
        msg[:, size + rows : size + rows + 1] = bias


def adjoint_kernel(
    len_ref, _, guess_ref, before_ref, after_ref, adj_ref, adj_after_ref,
    p_ref, p_before_ref, p_after_ref, diff_ref,
    point_ref, adj_out_ref, g_ref,
    buf, wl, wt, t_hi, t_lo, u_hi, u_lo,
):
    factor = 1.0 / p_ref.shape[0]
    own = lax.axis_index("depth")
    last = lax.axis_size("depth") - 1
    width = guess_ref.shape[1]
    spread = factor * diff_ref[...]
    g_ref[...] = jnp.zeros_like(g_ref)

    @pl.when(own < last)
    def _():
        count = len_ref[jnp.minimum(own + 1, last)]
        prepare(p_after_ref, wl, wt, factor)
        fill(buf, after_ref[...])
        run_forward(buf, width, p_after_ref, wl, wt, spread, count, (t_hi, t_lo))
        fill(buf, adj_after_ref[...])
        run_backward(buf, width, wl, wt, spread, count, (t_hi, t_lo))
        adj_out_ref[...] = inner(buf)

    @pl.when(own == last)
    def _():
        adj_out_ref[...] = adj_ref[...]

    @pl.when(own > 0)
    def _():
        count = len_ref[jnp.maximum(own - 1, 0)]
        prepare(p_before_ref, wl, wt, factor)
        fill(buf, before_ref[...])
        run_forward(buf, width, p_before_ref, wl, wt, spread, count)
        point_ref[...] = inner(buf)

    @pl.when(own == 0)
    def _():
        point_ref[...] = guess_ref[...]

    count = len_ref[own]
    prepare(p_ref, wl, wt, factor)
    fill(buf, point_ref[...])
    run_forward(buf, width, p_ref, wl, wt, spread, count, (t_hi, t_lo), (u_hi, u_lo))
    fill(buf, adj_out_ref[...])
    run_backward(
        buf, width, wl, wt, spread, count, (t_hi, t_lo), (u_hi, u_lo), (g_ref, factor)
    )
    adj_out_ref[...] = inner(buf)


def chain_kernel(plan, most, len_ref, _, second_ref, diff_ref, *rest):
    msgs, rest = rest[: plan.items], rest[plan.items :]
    outs, (buf, held, done, sem) = rest[: plan.results], rest[plan.results :]
    own = lax.axis_index("depth")
    host = own - plan.first
    rows = held.shape[1]
    size = plan.rows * IMG
    piece = plan.block * IMG

    @pl.when(jnp.logical_and(host >= 0, host < plan.hosts))
    def _():
        copies = [
            pltpu.make_async_copy(msg, held.at[lax.rem(host + shift, plan.items)], sem.at[shift])
            for shift, msg in enumerate(msgs)
        ]
        for copy in copies:
            copy.start()
        for copy in copies:
            copy.wait()
        offset = host * plan.block - plan.window(host)
        fill(buf, held[0, :, 0:size] + held[1, :, 0:size])

        def keep(result):
            done[result] = buf[:, pl.ds(pl.multiple_of(LANES + offset * IMG, LANES), piece)]

        keep(0)

        @pl.loop(2, plan.items)
        def _(item):
            scale = len_ref[item + 1].astype(F32) * (1.0 / most)
            matrix = held[item, :, size : size + rows]
            forward_layer(
                buf, size, left_factor(matrix), left_factor((scale * matrix).T),
                held[item, :, size + rows : size + rows + 1], scale * diff_ref[...],
            )
            buf[:, LANES : LANES + size] = inner(buf) + held[item, :, 0:size]
            keep(item - 1)

        for shift, out in enumerate(outs):
            out[...] = done[lax.rem(host + shift, plan.results)]

    @pl.when(own == 0)
    def _():
        for shift, out in enumerate(outs):
            if shift < plan.hosts:
                out[...] = second_ref[:, shift * piece : (shift + 1) * piece]


def collect_kernel(plan, point_ref, local_ref, *rest):
    received, out_ref = rest[:-1], rest[-1]
    own = lax.axis_index("depth")
    host = own - plan.first

    @pl.when(own < 2)
    def _():
        out_ref[...] = point_ref[...]

    @pl.when(own == 2)
    def _():
        for shift, block in enumerate(received):
            if shift < plan.hosts:
                out_ref[:, lanes(shift * plan.block, plan.block)] = block[...]

    for shift, block in enumerate(received):
        sender = lax.rem(own - 3 - shift + 2 * plan.results, plan.results)

        @pl.when(jnp.logical_and(own > 2, jnp.logical_and(sender < plan.hosts, sender != host)))
        def _():
            out_ref[:, lanes(sender * plan.block, plan.block)] = block[...]

    @pl.when(jnp.logical_and(own > 2, jnp.logical_and(host >= 0, host < plan.hosts)))
    def _():
        out_ref[:, lanes(host * plan.block, plan.block)] = local_ref[...]


SMEM = pl.BlockSpec(memory_space=pltpu.SMEM)
VMEM = pl.BlockSpec(memory_space=pltpu.VMEM)
ANY = pl.BlockSpec(memory_space=pl.ANY)


def call(kernel, out_shape, in_specs, scratch, micros, name):
    return pl.pallas_call(
        kernel,
        out_shape=out_shape,
        in_specs=in_specs,
        out_specs=jax.tree.map(lambda _: VMEM, out_shape),
        scratch_shapes=scratch,
        compiler_params=pltpu.CompilerParams(vmem_limit_bytes=48 * 2**20),
        cost_estimate=pl.CostEstimate(flops=int(micros * 1e9), bytes_accessed=2**21, transcendentals=0),
        name=name,
    )


def shifted(value, steps):
    count = lax.axis_size("depth")
    first, end = max(0, -steps), min(count, count - steps)
    return lax.ppermute(value, "depth", [(s, s + steps) for s in range(first, end)])


def batch_sum(value):
    count = lax.axis_size("batch")
    if count & (count - 1):
        return lax.psum(value, "batch")
    gap = 1
    while gap < count:
        value = value + lax.ppermute(value, "batch", [(s, s ^ gap) for s in range(count)])
        gap *= 2
    return value


def body(cpoint_guess, adjoint_guess, weights, biases, diffusion, section_len):
    plan = Plan(lax.axis_size("depth"))
    most, rows, _ = weights.shape
    width = cpoint_guess.shape[-1]
    guess, adjoint = cpoint_guess[0, 0], adjoint_guess[0, 0]
    diff = diffusion[:, None]

    def shape(*dims):
        return jax.ShapeDtypeStruct(dims, F32)

    state = shape(rows, width)
    buffer = pltpu.VMEM((rows, width + 2 * LANES), F32)
    factors = [pltpu.VMEM((most, rows, 3 * rows), BF16)] * 2

    packed = jnp.concatenate([weights, biases[:, None, :]], axis=1)
    packed_after = shifted(packed, -1)
    packed_second = lax.ppermute(packed[:1], "depth", [(2, 0)])
    before = shifted(guess, 1)
    adj_after = shifted(adjoint, -1)
    packed_before = shifted(packed, 1)

    after = call(push_kernel, state, [SMEM] + [VMEM] * 3, [buffer, *factors], 4, "push")(
        section_len, guess, packed, diff
    )
    window = shape(rows, plan.rows * IMG + LANES)
    second, *msgs = call(
        functools.partial(tau_kernel, plan), [state] + [window] * plan.items,
        [SMEM] + [VMEM] * 4, [buffer, *factors, pltpu.VMEM((rows, width), F32)], 3, "tau",
    )(section_len, after, packed_after, packed_second, diff)
    msgs = [
        msg if shift == plan.first else lax.ppermute(msg, "depth", plan.in_pairs(shift))
        for shift, msg in enumerate(msgs)
    ]

    saved = [pltpu.VMEM((most, rows, width), BF16)] * 4
    point, adjoint_out, grads = call(
        adjoint_kernel, [state, state, shape(most, rows, rows + 1)],
        [SMEM, ANY] + [VMEM] * 9, [buffer, *factors, *saved], 15, "adjoint",
    )(
        section_len, msgs[plan.first], guess, before, after, adjoint, adj_after,
        packed, packed_before, packed_after, diff,
    )

    blocks = call(
        functools.partial(chain_kernel, plan, most), [shape(rows, plan.block * IMG)] * plan.results,
        [SMEM, ANY, VMEM, VMEM] + [ANY] * plan.items,
        [
            pltpu.VMEM((rows, plan.rows * IMG + 2 * LANES), F32),
            pltpu.VMEM((plan.items, *window.shape), F32),
            pltpu.VMEM((plan.results, rows, plan.block * IMG), F32),
            pltpu.SemaphoreType.DMA((plan.items,)),
        ],
        1, "chain",
    )(section_len, grads, second, diff, *msgs)
    received = [lax.ppermute(block, "depth", plan.out_pairs(k)) for k, block in enumerate(blocks)]
    states = call(
        functools.partial(collect_kernel, plan), state, [VMEM] * (2 + plan.results), [], 0.5, "collect"
    )(point, blocks[plan.local], *received)

    grads = batch_sum(grads)
    return states[None, None], adjoint_out[None, None], grads[:, :, :rows], grads[:, :, rows]


def solution(mesh):
    state = P("depth", "batch", None, None)
    return jax.shard_map(
        body,
        mesh=mesh,
        in_specs=(state, state, P("depth", None, None), P("depth", None), P(), P()),
        out_specs=(state, state, P("depth", None, None), P("depth", None)),
        check_vma=False,
    )
```

```python
import functools

import jax
import jax.numpy as jnp
from jax import lax
from jax.experimental import pallas as pl
from jax.experimental.pallas import tpu as pltpu
from jax.sharding import PartitionSpec as P

IMG = 64
LANES = 128
CHUNK = 256
GRAD_CHUNK = 2048
AT_ONCE = 4
F32 = jnp.float32
BF16 = jnp.bfloat16


def split(x):
    hi = x.astype(BF16)
    lo = (x - hi.astype(F32)).astype(BF16)
    return hi, lo


def stack3(hi, lo):
    return jnp.concatenate([hi, lo, hi], axis=0)


def left_factor(matrix):
    hi = matrix.astype(BF16).astype(F32)
    return jnp.concatenate([hi, hi, matrix - hi], axis=1).astype(BF16)


def mm(a, b):
    return jnp.dot(a, b, preferred_element_type=F32)


def mm_nt(a, b):
    return lax.dot_general(a, b, (((1,), (1,)), ((), ())), preferred_element_type=F32)


def lane_masks(rows):
    lane = lax.broadcasted_iota(jnp.int32, (rows, LANES), 1)
    col = lane % IMG
    return col > 0, col < IMG - 1, lane < IMG


def neighbours(left, mid, right, masks):
    not_first, not_last, upper = masks
    pieces = [left] + [mid[:, k : k + LANES] for k in range(0, mid.shape[1], LANES)] + [right]
    swapped = [pltpu.roll(piece, IMG, 1) for piece in pieces]
    sums = []
    for k in range(1, len(pieces) - 1):
        piece = pieces[k]
        beside = jnp.where(not_first, pltpu.roll(piece, 1, 1), 0.0)
        beside += jnp.where(not_last, pltpu.roll(piece, LANES - 1, 1), 0.0)
        beside += swapped[k] + jnp.where(upper, swapped[k - 1], swapped[k + 1])
        sums.append(beside)
    return jnp.concatenate(sums, axis=1)


def sweep(buf, width, step, chunk=CHUNK):
    rows = buf.shape[0]
    masks = lane_masks(rows)
    before = buf[:, 0:LANES]
    for start in range(0, width, chunk):
        size = min(chunk, width - start)
        at = LANES + start
        mid = buf[:, at : at + size]
        after = buf[:, at + size : at + size + LANES]
        around = neighbours(before, mid, after, masks)
        before = mid[:, size - LANES :]
        buf[:, at : at + size] = step(start, size, mid, around)


def prepare(p_ref, wl_ref, wt_ref, factor):
    rows = p_ref.shape[2]
    for slot in range(p_ref.shape[0]):
        matrix = p_ref[slot, :rows, :]
        wl_ref[slot] = left_factor(matrix)
        wt_ref[slot] = left_factor((factor * matrix).T)


def column(row):
    n = row.shape[1]
    same = lax.broadcasted_iota(jnp.int32, (n, n), 0) == lax.broadcasted_iota(jnp.int32, (n, n), 1)
    return jnp.sum(jnp.where(same, row, 0.0), axis=1, keepdims=True)


def bias_of(p_ref, slot):
    rows = p_ref.shape[2]
    return column(p_ref[slot, rows : rows + 1, :])


def forward_layer(buf, width, wl, wt, bias, spread, t_out=None, u_out=None):
    keep = 1.0 - 4.0 * spread

    def step(start, size, mid, around):
        hi, lo = split(mid)
        t_hi, t_lo = split(jnp.tanh(mm(wl, stack3(hi, lo)) + bias))
        if t_out is not None:
            t_out(start, size, t_hi, t_lo)
        if u_out is not None:
            u_out(start, size, hi, lo)
        return mid * keep + around * spread - mm(wt, stack3(t_hi, t_lo))

    sweep(buf, width, step)


def run_forward(buf, width, p_ref, wl_ref, wt_ref, spread, count, t_refs=None, u_refs=None):
    def saver(refs, slot):
        if refs is None:
            return None

        def save(start, size, hi, lo):
            refs[0][slot, :, start : start + size] = hi
            refs[1][slot, :, start : start + size] = lo

        return save

    @pl.loop(0, count)
    def _(slot):
        forward_layer(
            buf, width, wl_ref[slot], wt_ref[slot], bias_of(p_ref, slot), spread,
            saver(t_refs, slot), saver(u_refs, slot),
        )


def run_backward(buf, width, wl_ref, wt_ref, spread, count, t_refs, u_refs=None, grads=None):
    keep = 1.0 - 4.0 * spread

    @pl.loop(0, count)
    def _(passed):
        slot = count - 1 - passed
        wl, wt = wl_ref[slot], wt_ref[slot]
        rows = buf.shape[0]
        total = [None, None]

        def step(start, size, mid, around):
            hi, lo = split(mid)
            t_hi = t_refs[0][slot, :, start : start + size]
            t_lo = t_refs[1][slot, :, start : start + size]
            t = t_hi.astype(F32) + t_lo.astype(F32)
            q = (1.0 - t * t) * mm(wl, stack3(hi, lo))
            q_hi, q_lo = split(q)
            if grads is not None:
                u_hi = u_refs[0][slot, :, start : start + size]
                u_lo = u_refs[1][slot, :, start : start + size]
                left = jnp.concatenate([t_hi, t_lo, q_hi, q_lo], axis=0)
                right = jnp.concatenate([hi, lo, u_hi, u_lo], axis=0)
                part = mm_nt(left, right)
                part_b = sum(q[:, k : k + LANES] for k in range(0, size, LANES))
                total[0] = part if total[0] is None else total[0] + part
                total[1] = part_b if total[1] is None else total[1] + part_b
            return mid * keep + around * spread - mm(wt, stack3(q_hi, q_lo))

        sweep(buf, width, step, CHUNK if grads is None else GRAD_CHUNK)
        if grads is not None:
            g_ref, factor = grads
            g = total[0]
            a, b, c, d = rows, 2 * rows, 3 * rows, 4 * rows
            gw = g[0:a, 0:a] + g[0:a, a:b] + g[a:b, 0:a]
            gw += g[b:c, b:c] + g[b:c, c:d] + g[c:d, b:c]
            g_ref[slot, :, 0:rows] = -factor * gw
            g_ref[slot, :, rows : rows + 1] = -factor * jnp.sum(total[1], axis=1, keepdims=True)


def fill(buf, value):
    rows, width = value.shape
    zero = jnp.zeros((rows, LANES), F32)
    buf[:, 0:LANES] = zero
    buf[:, LANES + width :] = zero
    buf[:, LANES : LANES + width] = value


def inner(buf):
    return buf[:, LANES : buf.shape[1] - LANES]


class Plan:
    def __init__(self, count):
        self.count = count
        self.items = count - 2
        self.hosts = count // 2
        self.first = count // 4
        self.block = IMG // self.hosts
        self.rows = min(IMG, self.block + 2 * (count - 4))
        self.rows += self.rows % 2
        self.results = count - 3
        self.local = (self.first - 3) % self.results

    def window(self, host):
        start = host * self.block - (self.count - 4)
        return jnp.clip(start - start % 2, 0, IMG - self.rows)

    def in_pairs(self, shift):
        return [((h + shift) % self.items, h + self.first) for h in range(self.hosts)]

    def out_pairs(self, shift):
        pairs = [(h + self.first, 3 + (h + shift) % self.results) for h in range(self.hosts)]
        pairs = [(s, d) for s, d in pairs if s != d]
        return pairs + ([(0, 2)] if shift < self.hosts else [])


def lanes(row, size):
    return pl.ds(pl.multiple_of(row * IMG, LANES), size * IMG)


def push_kernel(len_ref, guess_ref, p_ref, diff_ref, out_ref, buf, wl, wt):
    factor = 1.0 / p_ref.shape[0]
    own = lax.axis_index("depth")
    prepare(p_ref, wl, wt, factor)
    fill(buf, guess_ref[...])
    run_forward(buf, guess_ref.shape[1], p_ref, wl, wt, factor * diff_ref[...], len_ref[own])
    out_ref[...] = inner(buf)


def tau_kernel(plan, len_ref, point_ref, p_ref, p2_ref, diff_ref, second_ref, *rest):
    msgs, (buf, wl, wt, whole) = rest[:-4], rest[-4:]
    most, _, rows = p_ref.shape
    factor = 1.0 / most
    own = lax.axis_index("depth")
    count = len_ref[jnp.minimum(own + 1, plan.count - 1)]
    width = point_ref.shape[1]
    prepare(p_ref, wl, wt, factor)
    fill(buf, point_ref[...])
    run_forward(buf, width, p_ref, wl, wt, factor * diff_ref[...], count)
    second_ref[...] = inner(buf)

    def coarse(q_ref, length):
        scale = length.astype(F32) * factor
        matrix = q_ref[0, :rows, :]
        forward_layer(
            buf, width, left_factor(matrix), left_factor((scale * matrix).T), bias_of(q_ref, 0),
            scale * diff_ref[...],
        )

    @pl.when(own > 0)
    def _():
        buf[:, LANES : LANES + width] = point_ref[...]
        coarse(p_ref, count)
        whole[...] = second_ref[...] - inner(buf)

    @pl.when(own == 0)
    def _():
        coarse(p2_ref, len_ref[2])
        whole[...] = inner(buf)

    size = plan.rows * IMG
    bias = bias_of(p_ref, 0)
    for shift, msg in enumerate(msgs):
        host = lax.rem(own - shift + 2 * plan.items, plan.items)
        start = plan.window(jnp.minimum(host, plan.hosts - 1))
        msg[:, 0:size] = whole[:, lanes(start, plan.rows)]
        msg[:, size : size + rows] = p_ref[0, :rows, :]
        msg[:, size + rows : size + rows + 1] = bias


def point_kernel(
    len_ref, _, guess_ref, before_ref, p_ref, p_before_ref, diff_ref,
    point_ref, t_hi, t_lo, u_hi, u_lo, buf, wl, wt,
):
    factor = 1.0 / p_ref.shape[0]
    own = lax.axis_index("depth")
    width = guess_ref.shape[1]
    spread = factor * diff_ref[...]

    @pl.when(own > 0)
    def _():
        count = len_ref[jnp.maximum(own - 1, 0)]
        prepare(p_before_ref, wl, wt, factor)
        fill(buf, before_ref[...])
        run_forward(buf, width, p_before_ref, wl, wt, spread, count)
        point_ref[...] = inner(buf)

    @pl.when(own == 0)
    def _():
        point_ref[...] = guess_ref[...]
        fill(buf, guess_ref[...])

    prepare(p_ref, wl, wt, factor)
    run_forward(buf, width, p_ref, wl, wt, spread, len_ref[own], (t_hi, t_lo), (u_hi, u_lo))


def adjoint_kernel(
    len_ref, after_ref, adj_ref, adj_after_ref, p_ref, p_after_ref, diff_ref, t_hi, t_lo, u_hi, u_lo,
    adj_out_ref, g_ref, buf, wl, wt, t_next_hi, t_next_lo,
):
    factor = 1.0 / p_ref.shape[0]
    own = lax.axis_index("depth")
    last = lax.axis_size("depth") - 1
    width = after_ref.shape[1]
    spread = factor * diff_ref[...]
    g_ref[...] = jnp.zeros_like(g_ref)

    @pl.when(own < last)
    def _():
        count = len_ref[jnp.minimum(own + 1, last)]
        prepare(p_after_ref, wl, wt, factor)
        fill(buf, after_ref[...])
        run_forward(buf, width, p_after_ref, wl, wt, spread, count, (t_next_hi, t_next_lo))
        fill(buf, adj_after_ref[...])
        run_backward(buf, width, wl, wt, spread, count, (t_next_hi, t_next_lo))

    @pl.when(own == last)
    def _():
        fill(buf, adj_ref[...])

    prepare(p_ref, wl, wt, factor)
    run_backward(
        buf, width, wl, wt, spread, len_ref[own], (t_hi, t_lo), (u_hi, u_lo), (g_ref, factor)
    )
    adj_out_ref[...] = inner(buf)


def chain_kernel(plan, most, len_ref, _, second_ref, diff_ref, *rest):
    msgs, rest = rest[: plan.items], rest[plan.items :]
    outs, (buf, held, done, sem) = rest[: plan.results], rest[plan.results :]
    own = lax.axis_index("depth")
    host = own - plan.first
    rows = held.shape[1]
    size = plan.rows * IMG
    piece = plan.block * IMG

    @pl.when(jnp.logical_and(host >= 0, host < plan.hosts))
    def _():
        copies = [
            pltpu.make_async_copy(msg, held.at[lax.rem(host + shift, plan.items)], sem.at[shift])
            for shift, msg in enumerate(msgs)
        ]
        for copy in copies:
            copy.start()
        for copy in copies:
            copy.wait()
        offset = host * plan.block - plan.window(host)
        fill(buf, held[0, :, 0:size] + held[1, :, 0:size])

        def keep(result):
            done[result] = buf[:, pl.ds(pl.multiple_of(LANES + offset * IMG, LANES), piece)]

        keep(0)

        @pl.loop(2, plan.items)
        def _(item):
            scale = len_ref[item + 1].astype(F32) * (1.0 / most)
            matrix = held[item, :, size : size + rows]
            forward_layer(
                buf, size, left_factor(matrix), left_factor((scale * matrix).T),
                held[item, :, size + rows : size + rows + 1], scale * diff_ref[...],
            )
            buf[:, LANES : LANES + size] = inner(buf) + held[item, :, 0:size]
            keep(item - 1)

        for shift, out in enumerate(outs):
            out[...] = done[lax.rem(host + shift, plan.results)]

    @pl.when(own == 0)
    def _():
        for shift, out in enumerate(outs):
            if shift < plan.hosts:
                out[...] = second_ref[:, shift * piece : (shift + 1) * piece]


def collect_kernel(plan, point_ref, local_ref, *rest):
    received, out_ref = rest[:-1], rest[-1]
    own = lax.axis_index("depth")
    host = own - plan.first

    @pl.when(own < 2)
    def _():
        out_ref[...] = point_ref[...]

    @pl.when(own == 2)
    def _():
        for shift, block in enumerate(received):
            if shift < plan.hosts:
                out_ref[:, lanes(shift * plan.block, plan.block)] = block[...]

    for shift, block in enumerate(received):
        sender = lax.rem(own - 3 - shift + 2 * plan.results, plan.results)

        @pl.when(jnp.logical_and(own > 2, jnp.logical_and(sender < plan.hosts, sender != host)))
        def _():
            out_ref[:, lanes(sender * plan.block, plan.block)] = block[...]

    @pl.when(jnp.logical_and(own > 2, jnp.logical_and(host >= 0, host < plan.hosts)))
    def _():
        out_ref[:, lanes(host * plan.block, plan.block)] = local_ref[...]


SMEM = pl.BlockSpec(memory_space=pltpu.SMEM)
VMEM = pl.BlockSpec(memory_space=pltpu.VMEM)
ANY = pl.BlockSpec(memory_space=pl.ANY)


def call(kernel, out_shape, in_specs, scratch, micros, name):
    return pl.pallas_call(
        kernel,
        out_shape=out_shape,
        in_specs=in_specs,
        out_specs=jax.tree.map(lambda _: VMEM, out_shape),
        scratch_shapes=scratch,
        compiler_params=pltpu.CompilerParams(vmem_limit_bytes=32 * 2**20),
        cost_estimate=pl.CostEstimate(flops=int(micros * 1e8), bytes_accessed=2**21, transcendentals=0),
        name=name,
    )


def shifted(value, steps):
    count = lax.axis_size("depth")
    first, end = max(0, -steps), min(count, count - steps)
    return lax.ppermute(value, "depth", [(s, s + steps) for s in range(first, end)])


def batch_sum(value):
    count = lax.axis_size("batch")
    if count & (count - 1):
        return lax.psum(value, "batch")
    gap = 1
    while gap < count:
        value = value + lax.ppermute(value, "batch", [(s, s ^ gap) for s in range(count)])
        gap *= 2
    return value


def body(cpoint_guess, adjoint_guess, weights, biases, diffusion, section_len):
    plan = Plan(lax.axis_size("depth"))
    most, rows, _ = weights.shape
    width = cpoint_guess.shape[-1]
    guess, adjoint = cpoint_guess[0, 0], adjoint_guess[0, 0]
    diff = diffusion[:, None]

    def shape(*dims):
        return jax.ShapeDtypeStruct(dims, F32)

    state = shape(rows, width)
    buffer = pltpu.VMEM((rows, width + 2 * LANES), F32)
    factors = [pltpu.VMEM((most, rows, 3 * rows), BF16)] * 2

    packed = jnp.concatenate([weights, biases[:, None, :]], axis=1)
    packed_after = shifted(packed, -1)
    before = shifted(guess, 1)

    after = call(push_kernel, state, [SMEM] + [VMEM] * 3, [buffer, *factors], 40, "push")(
        section_len, guess, packed, diff
    )
    after, packed_after, packed_later, adjoint_later = lax.optimization_barrier(
        (after, packed_after, packed, adjoint)
    )
    packed_second = lax.ppermute(packed_later[:1], "depth", [(2, 0)])
    packed_before = shifted(packed_later, 1)
    adj_after = shifted(adjoint_later, -1)

    window = shape(rows, plan.rows * IMG + LANES)
    second, *msgs = call(
        functools.partial(tau_kernel, plan), [state] + [window] * plan.items,
        [SMEM] + [VMEM] * 4, [buffer, *factors, pltpu.VMEM((rows, width), F32)], 3, "tau",
    )(section_len, after, packed_after, packed_second, diff)
    msgs, before, packed_before = lax.optimization_barrier((msgs, before, packed_before))
    arrived = {plan.first: msgs[plan.first]}
    order = [shift for shift in range(plan.items) if shift != plan.first]
    for k, shift in enumerate(order):
        msg = msgs[shift]
        if k >= AT_ONCE:
            msg, _ = lax.optimization_barrier((msg, arrived[order[k - AT_ONCE]]))
        arrived[shift] = lax.ppermute(msg, "depth", plan.in_pairs(shift))
    msgs = [arrived[shift] for shift in range(plan.items)]

    saved = jax.ShapeDtypeStruct((most, rows, width), BF16)
    point, *states = call(
        point_kernel, [state] + [saved] * 4, [SMEM, ANY] + [VMEM] * 5, [buffer, *factors], 6, "point"
    )(section_len, msgs[plan.first], guess, before, packed, packed_before, diff)
    adjoint_out, grads = call(
        adjoint_kernel, [state, shape(most, rows, rows + 1)],
        [SMEM] + [VMEM] * 10, [buffer, *factors] + [pltpu.VMEM(saved.shape, BF16)] * 2, 10, "adjoint",
    )(section_len, after, adjoint, adj_after, packed, packed_after, diff, *states)

    blocks = call(
        functools.partial(chain_kernel, plan, most), [shape(rows, plan.block * IMG)] * plan.results,
        [SMEM, ANY, VMEM, VMEM] + [ANY] * plan.items,
        [
            pltpu.VMEM((rows, plan.rows * IMG + 2 * LANES), F32),
            pltpu.VMEM((plan.items, *window.shape), F32),
            pltpu.VMEM((plan.results, rows, plan.block * IMG), F32),
            pltpu.SemaphoreType.DMA((plan.items,)),
        ],
        1, "chain",
    )(section_len, grads, second, diff, *msgs)
    received = [lax.ppermute(block, "depth", plan.out_pairs(k)) for k, block in enumerate(blocks)]
    states = call(
        functools.partial(collect_kernel, plan), state, [VMEM] * (2 + plan.results), [], 0.5, "collect"
    )(point, blocks[plan.local], *received)

    _, grads = lax.optimization_barrier((received[0], grads))
    grads = batch_sum(grads)
    return states[None, None], adjoint_out[None, None], grads[:, :, :rows], grads[:, :, rows]


def solution(mesh):
    state = P("depth", "batch", None, None)
    return jax.shard_map(
        body,
        mesh=mesh,
        in_specs=(state, state, P("depth", None, None), P("depth", None), P(), P()),
        out_specs=(state, state, P("depth", None, None), P("depth", None)),
        check_vma=False,
    )
```

```python
import functools

import jax
import jax.numpy as jnp
from jax import lax
from jax.experimental import pallas as pl
from jax.experimental.pallas import tpu as pltpu
from jax.sharding import PartitionSpec as P

IMG = 64
LANES = 128
CHUNK = 256
GRAD_CHUNK = 2048
AT_ONCE = 4
F32 = jnp.float32
BF16 = jnp.bfloat16


def split(x):
    hi = x.astype(BF16)
    lo = (x - hi.astype(F32)).astype(BF16)
    return hi, lo


def stack3(hi, lo):
    return jnp.concatenate([hi, lo, hi], axis=0)


def left_factor(matrix):
    hi = matrix.astype(BF16).astype(F32)
    return jnp.concatenate([hi, hi, matrix - hi], axis=1).astype(BF16)


def mm(a, b):
    return jnp.dot(a, b, preferred_element_type=F32)


def mm_nt(a, b):
    return lax.dot_general(a, b, (((1,), (1,)), ((), ())), preferred_element_type=F32)


def lane_masks(rows):
    lane = lax.broadcasted_iota(jnp.int32, (rows, LANES), 1)
    col = lane % IMG
    return col > 0, col < IMG - 1, lane < IMG


def neighbours(left, mid, right, masks):
    not_first, not_last, upper = masks
    pieces = [left] + [mid[:, k : k + LANES] for k in range(0, mid.shape[1], LANES)] + [right]
    swapped = [pltpu.roll(piece, IMG, 1) for piece in pieces]
    sums = []
    for k in range(1, len(pieces) - 1):
        piece = pieces[k]
        beside = jnp.where(not_first, pltpu.roll(piece, 1, 1), 0.0)
        beside += jnp.where(not_last, pltpu.roll(piece, LANES - 1, 1), 0.0)
        beside += swapped[k] + jnp.where(upper, swapped[k - 1], swapped[k + 1])
        sums.append(beside)
    return jnp.concatenate(sums, axis=1)


def sweep(buf, width, step, chunk=CHUNK):
    rows = buf.shape[0]
    masks = lane_masks(rows)
    before = buf[:, 0:LANES]
    for start in range(0, width, chunk):
        size = min(chunk, width - start)
        at = LANES + start
        mid = buf[:, at : at + size]
        after = buf[:, at + size : at + size + LANES]
        around = neighbours(before, mid, after, masks)
        before = mid[:, size - LANES :]
        buf[:, at : at + size] = step(start, size, mid, around)


def matrix_of(p_ref, slot):
    rows = p_ref.shape[0]
    return p_ref[:, slot * rows : (slot + 1) * rows]


def table_of(p_ref):
    return p_ref[:, p_ref.shape[1] - LANES :]


def bias_of(p_ref, slot):
    table = table_of(p_ref)
    pick = lax.broadcasted_iota(jnp.int32, table.shape, 1) == slot
    return jnp.sum(jnp.where(pick, table, 0.0), axis=1, keepdims=True)


def slots_of(p_ref):
    rows, width = p_ref.shape
    return (width - LANES) // rows


def prepare(p_ref, wl_ref, wt_ref):
    most = slots_of(p_ref)
    factor = 1.0 / most
    for slot in range(most):
        matrix = matrix_of(p_ref, slot)
        wl_ref[slot] = left_factor(matrix)
        wt_ref[slot] = left_factor((factor * matrix).T)
    return factor * table_of(p_ref)[:, most : most + 1], factor


def column(row):
    n = row.shape[1]
    same = lax.broadcasted_iota(jnp.int32, (n, n), 0) == lax.broadcasted_iota(jnp.int32, (n, n), 1)
    return jnp.sum(jnp.where(same, row, 0.0), axis=1, keepdims=True)


def pack_kernel(w_ref, b_ref, diff_ref, guess_ref, p_ref, p0_ref, both_ref):
    most, rows, _ = w_ref.shape
    for slot in range(most):
        p_ref[:, slot * rows : (slot + 1) * rows] = w_ref[slot]
        p_ref[:, most * rows + slot : most * rows + slot + 1] = column(b_ref[slot : slot + 1, :])
    p_ref[:, most * rows + most : most * rows + most + 1] = column(diff_ref[...])
    p0_ref[:, 0:rows] = w_ref[0]
    p0_ref[:, rows : rows + 1] = column(b_ref[0:1, :])
    width = guess_ref.shape[1]
    both_ref[:, 0:width] = guess_ref[...]
    both_ref[:, width:] = p_ref[...]


def forward_layer(buf, width, wl, wt, bias, spread, t_out=None, u_out=None):
    keep = 1.0 - 4.0 * spread

    def step(start, size, mid, around):
        hi, lo = split(mid)
        t_hi, t_lo = split(jnp.tanh(mm(wl, stack3(hi, lo)) + bias))
        if t_out is not None:
            t_out(start, size, t_hi, t_lo)
        if u_out is not None:
            u_out(start, size, hi, lo)
        return mid * keep + around * spread - mm(wt, stack3(t_hi, t_lo))

    sweep(buf, width, step)


def run_forward(buf, width, p_ref, wl_ref, wt_ref, spread, count, t_refs=None, u_refs=None):
    def saver(refs, slot):
        if refs is None:
            return None

        def save(start, size, hi, lo):
            refs[0][slot, :, start : start + size] = hi
            refs[1][slot, :, start : start + size] = lo

        return save

    @pl.loop(0, count)
    def _(slot):
        forward_layer(
            buf, width, wl_ref[slot], wt_ref[slot], bias_of(p_ref, slot), spread,
            saver(t_refs, slot), saver(u_refs, slot),
        )


def run_backward(buf, width, wl_ref, wt_ref, spread, count, t_refs, u_refs=None, grads=None):
    keep = 1.0 - 4.0 * spread

    @pl.loop(0, count)
    def _(passed):
        slot = count - 1 - passed
        wl, wt = wl_ref[slot], wt_ref[slot]
        rows = buf.shape[0]
        total = [None, None]

        def step(start, size, mid, around):
            hi, lo = split(mid)
            t_hi = t_refs[0][slot, :, start : start + size]
            t_lo = t_refs[1][slot, :, start : start + size]
            t = t_hi.astype(F32) + t_lo.astype(F32)
            q = (1.0 - t * t) * mm(wl, stack3(hi, lo))
            q_hi, q_lo = split(q)
            if grads is not None:
                u_hi = u_refs[0][slot, :, start : start + size]
                u_lo = u_refs[1][slot, :, start : start + size]
                left = jnp.concatenate([t_hi, t_lo, q_hi, q_lo], axis=0)
                right = jnp.concatenate([hi, lo, u_hi, u_lo], axis=0)
                part = mm_nt(left, right)
                part_b = sum(q[:, k : k + LANES] for k in range(0, size, LANES))
                total[0] = part if total[0] is None else total[0] + part
                total[1] = part_b if total[1] is None else total[1] + part_b
            return mid * keep + around * spread - mm(wt, stack3(q_hi, q_lo))

        sweep(buf, width, step, CHUNK if grads is None else GRAD_CHUNK)
        if grads is not None:
            g_ref, factor = grads
            g = total[0]
            a, b, c, d = rows, 2 * rows, 3 * rows, 4 * rows
            gw = g[0:a, 0:a] + g[0:a, a:b] + g[a:b, 0:a]
            gw += g[b:c, b:c] + g[b:c, c:d] + g[c:d, b:c]
            g_ref[slot, :, 0:rows] = -factor * gw
            g_ref[slot, :, rows : rows + 1] = -factor * jnp.sum(total[1], axis=1, keepdims=True)


def fill(buf, value):
    rows, width = value.shape
    zero = jnp.zeros((rows, LANES), F32)
    buf[:, 0:LANES] = zero
    buf[:, LANES + width :] = zero
    buf[:, LANES : LANES + width] = value


def inner(buf):
    return buf[:, LANES : buf.shape[1] - LANES]


class Plan:
    def __init__(self, count):
        self.count = count
        self.items = count - 2
        self.hosts = count // 2
        self.first = count // 4
        self.block = IMG // self.hosts
        self.rows = min(IMG, self.block + 2 * (count - 4))
        self.rows += self.rows % 2
        self.results = count - 3
        self.local = (self.first - 3) % self.results

    def window(self, host):
        start = host * self.block - (self.count - 4)
        return jnp.clip(start - start % 2, 0, IMG - self.rows)

    def in_pairs(self, shift):
        return [((h + shift) % self.items, h + self.first) for h in range(self.hosts)]

    def out_pairs(self, shift):
        pairs = [(h + self.first, 3 + (h + shift) % self.results) for h in range(self.hosts)]
        pairs = [(s, d) for s, d in pairs if s != d]
        return pairs + ([(0, 2)] if shift < self.hosts else [])


def lanes(row, size):
    return pl.ds(pl.multiple_of(row * IMG, LANES), size * IMG)


def push_kernel(len_ref, guess_ref, p_ref, out_ref, buf, wl, wt):
    spread, _ = prepare(p_ref, wl, wt)
    fill(buf, guess_ref[...])
    count = len_ref[lax.axis_index("depth")]
    run_forward(buf, guess_ref.shape[1], p_ref, wl, wt, spread, count)
    out_ref[...] = inner(buf)


def tau_kernel(plan, len_ref, point_ref, p_ref, p2_ref, second_ref, *rest):
    msgs, (buf, wl, wt, whole) = rest[:-4], rest[-4:]
    rows, width = point_ref.shape
    own = lax.axis_index("depth")
    count = len_ref[jnp.minimum(own + 1, plan.count - 1)]
    spread, factor = prepare(p_ref, wl, wt)
    fill(buf, point_ref[...])
    run_forward(buf, width, p_ref, wl, wt, spread, count)
    second_ref[...] = inner(buf)

    def coarse(matrix, bias, length):
        scale = length.astype(F32)
        forward_layer(
            buf, width, left_factor(matrix), left_factor((scale * factor * matrix).T), bias, scale * spread
        )

    @pl.when(own > 0)
    def _():
        buf[:, LANES : LANES + width] = point_ref[...]
        coarse(matrix_of(p_ref, 0), bias_of(p_ref, 0), count)
        whole[...] = second_ref[...] - inner(buf)

    @pl.when(own == 0)
    def _():
        coarse(p2_ref[:, 0:rows], p2_ref[:, rows : rows + 1], len_ref[2])
        whole[...] = inner(buf)

    size = plan.rows * IMG
    bias = bias_of(p_ref, 0)
    for shift, msg in enumerate(msgs):
        host = lax.rem(own - shift + 2 * plan.items, plan.items)
        start = plan.window(jnp.minimum(host, plan.hosts - 1))
        msg[:, 0:size] = whole[:, lanes(start, plan.rows)]
        msg[:, size : size + rows] = matrix_of(p_ref, 0)
        msg[:, size + rows : size + rows + 1] = bias


def point_kernel(
    len_ref, _, guess_ref, before_ref, p_ref, point_ref, t_hi, t_lo, u_hi, u_lo, buf, wl, wt
):
    own = lax.axis_index("depth")
    width = guess_ref.shape[1]

    @pl.when(own > 0)
    def _():
        count = len_ref[jnp.maximum(own - 1, 0)]
        p_before_ref = before_ref.at[:, width:]
        spread, _ = prepare(p_before_ref, wl, wt)
        fill(buf, before_ref[:, 0:width])
        run_forward(buf, width, p_before_ref, wl, wt, spread, count)
        point_ref[...] = inner(buf)

    @pl.when(own == 0)
    def _():
        point_ref[...] = guess_ref[...]
        fill(buf, guess_ref[...])

    spread, _ = prepare(p_ref, wl, wt)
    run_forward(buf, width, p_ref, wl, wt, spread, len_ref[own], (t_hi, t_lo), (u_hi, u_lo))


def adjoint_kernel(
    len_ref, after_ref, adj_ref, adj_after_ref, p_ref, p_after_ref, t_hi, t_lo, u_hi, u_lo,
    adj_out_ref, g_ref, buf, wl, wt, t_next_hi, t_next_lo,
):
    own = lax.axis_index("depth")
    last = lax.axis_size("depth") - 1
    width = after_ref.shape[1]
    g_ref[...] = jnp.zeros_like(g_ref)

    @pl.when(own < last)
    def _():
        count = len_ref[jnp.minimum(own + 1, last)]
        spread, _ = prepare(p_after_ref, wl, wt)
        fill(buf, after_ref[...])
        run_forward(buf, width, p_after_ref, wl, wt, spread, count, (t_next_hi, t_next_lo))
        fill(buf, adj_after_ref[...])
        run_backward(buf, width, wl, wt, spread, count, (t_next_hi, t_next_lo))

    @pl.when(own == last)
    def _():
        fill(buf, adj_ref[...])

    spread, factor = prepare(p_ref, wl, wt)
    run_backward(
        buf, width, wl, wt, spread, len_ref[own], (t_hi, t_lo), (u_hi, u_lo), (g_ref, factor)
    )
    adj_out_ref[...] = inner(buf)


def chain_kernel(plan, len_ref, _, second_ref, p_ref, *rest):
    msgs, rest = rest[: plan.items], rest[plan.items :]
    outs, (buf, held, done, sem) = rest[: plan.results], rest[plan.results :]
    own = lax.axis_index("depth")
    host = own - plan.first
    rows = held.shape[1]
    size = plan.rows * IMG
    piece = plan.block * IMG

    @pl.when(jnp.logical_and(host >= 0, host < plan.hosts))
    def _():
        copies = [
            pltpu.make_async_copy(msg, held.at[lax.rem(host + shift, plan.items)], sem.at[shift])
            for shift, msg in enumerate(msgs)
        ]
        for copy in copies:
            copy.start()
        for copy in copies:
            copy.wait()
        offset = host * plan.block - plan.window(host)
        most = slots_of(p_ref)
        diff = table_of(p_ref)[:, most : most + 1]
        fill(buf, held[0, :, 0:size] + held[1, :, 0:size])

        def keep(result):
            done[result] = buf[:, pl.ds(pl.multiple_of(LANES + offset * IMG, LANES), piece)]

        keep(0)

        @pl.loop(2, plan.items)
        def _(item):
            scale = len_ref[item + 1].astype(F32) * (1.0 / most)
            matrix = held[item, :, size : size + rows]
            forward_layer(
                buf, size, left_factor(matrix), left_factor((scale * matrix).T),
                held[item, :, size + rows : size + rows + 1], scale * diff,
            )
            buf[:, LANES : LANES + size] = inner(buf) + held[item, :, 0:size]
            keep(item - 1)

        for shift, out in enumerate(outs):
            out[...] = done[lax.rem(host + shift, plan.results)]

    @pl.when(own == 0)
    def _():
        for shift, out in enumerate(outs):
            if shift < plan.hosts:
                out[...] = second_ref[:, shift * piece : (shift + 1) * piece]


def collect_kernel(plan, point_ref, local_ref, *rest):
    received, out_ref = rest[:-1], rest[-1]
    own = lax.axis_index("depth")
    host = own - plan.first

    @pl.when(own < 2)
    def _():
        out_ref[...] = point_ref[...]

    @pl.when(own == 2)
    def _():
        for shift, block in enumerate(received):
            if shift < plan.hosts:
                out_ref[:, lanes(shift * plan.block, plan.block)] = block[...]

    for shift, block in enumerate(received):
        sender = lax.rem(own - 3 - shift + 2 * plan.results, plan.results)

        @pl.when(jnp.logical_and(own > 2, jnp.logical_and(sender < plan.hosts, sender != host)))
        def _():
            out_ref[:, lanes(sender * plan.block, plan.block)] = block[...]

    @pl.when(jnp.logical_and(own > 2, jnp.logical_and(host >= 0, host < plan.hosts)))
    def _():
        out_ref[:, lanes(host * plan.block, plan.block)] = local_ref[...]


SMEM = pl.BlockSpec(memory_space=pltpu.SMEM)
VMEM = pl.BlockSpec(memory_space=pltpu.VMEM)
ANY = pl.BlockSpec(memory_space=pl.ANY)


def call(kernel, out_shape, in_specs, scratch, micros, name):
    return pl.pallas_call(
        kernel,
        out_shape=out_shape,
        in_specs=in_specs,
        out_specs=jax.tree.map(lambda _: VMEM, out_shape),
        scratch_shapes=scratch,
        compiler_params=pltpu.CompilerParams(vmem_limit_bytes=32 * 2**20),
        cost_estimate=pl.CostEstimate(flops=int(micros * 1e8), bytes_accessed=2**21, transcendentals=0),
        name=name,
    )


def shifted(value, steps):
    count = lax.axis_size("depth")
    first, end = max(0, -steps), min(count, count - steps)
    return lax.ppermute(value, "depth", [(s, s + steps) for s in range(first, end)])


def batch_steps():
    count = lax.axis_size("batch")
    if count & (count - 1):
        return [lambda value: lax.psum(value, "batch")]

    def step(gap):
        return lambda value: value + lax.ppermute(value, "batch", [(s, s ^ gap) for s in range(count)])

    return [step(1 << k) for k in range(count.bit_length() - 1)]


def body(cpoint_guess, adjoint_guess, weights, biases, diffusion, section_len):
    plan = Plan(lax.axis_size("depth"))
    most, rows, _ = weights.shape
    width = cpoint_guess.shape[-1]
    guess, adjoint = cpoint_guess[0, 0], adjoint_guess[0, 0]

    def shape(*dims):
        return jax.ShapeDtypeStruct(dims, F32)

    state = shape(rows, width)
    buffer = pltpu.VMEM((rows, width + 2 * LANES), F32)
    factors = [pltpu.VMEM((most, rows, 3 * rows), BF16)] * 2

    wide = most * rows + LANES
    packed, packed0, both = call(
        pack_kernel, [shape(rows, wide), shape(rows, LANES), shape(rows, width + wide)], [VMEM] * 4, [], 1, "pack"
    )(weights, biases, diffusion[None], guess)
    packed_after = shifted(packed, -1)
    packed_second = lax.ppermute(packed0, "depth", [(2, 0)])
    before = shifted(both, 1)

    after = call(push_kernel, state, [SMEM] + [VMEM] * 2, [buffer, *factors], 40, "push")(
        section_len, guess, packed
    )
    after, packed_after, packed_second, adjoint_later = lax.optimization_barrier(
        (after, packed_after, packed_second, adjoint)
    )
    adj_after = shifted(adjoint_later, -1)

    window = shape(rows, plan.rows * IMG + LANES)
    second, *msgs = call(
        functools.partial(tau_kernel, plan), [state] + [window] * plan.items,
        [SMEM] + [VMEM] * 3, [buffer, *factors, pltpu.VMEM((rows, width), F32)], 3, "tau",
    )(section_len, after, packed_after, packed_second)
    msgs, before = lax.optimization_barrier((msgs, before))
    arrived = {plan.first: msgs[plan.first]}
    order = [shift for shift in range(plan.items) if shift != plan.first]
    for k, shift in enumerate(order):
        msg = msgs[shift]
        if k >= AT_ONCE:
            msg, _ = lax.optimization_barrier((msg, arrived[order[k - AT_ONCE]]))
        arrived[shift] = lax.ppermute(msg, "depth", plan.in_pairs(shift))
    msgs = [arrived[shift] for shift in range(plan.items)]

    saved = jax.ShapeDtypeStruct((most, rows, width), BF16)
    point, *states = call(
        point_kernel, [state] + [saved] * 4, [SMEM, ANY] + [VMEM] * 3, [buffer, *factors], 6, "point"
    )(section_len, msgs[plan.first], guess, before, packed)
    adjoint_out, grads = call(
        adjoint_kernel, [state, shape(most, rows, rows + 1)],
        [SMEM] + [VMEM] * 9, [buffer, *factors] + [pltpu.VMEM(saved.shape, BF16)] * 2, 10, "adjoint",
    )(section_len, after, adjoint, adj_after, packed, packed_after, *states)

    blocks = call(
        functools.partial(chain_kernel, plan), [shape(rows, plan.block * IMG)] * plan.results,
        [SMEM, ANY, VMEM, VMEM] + [ANY] * plan.items,
        [
            pltpu.VMEM((rows, plan.rows * IMG + 2 * LANES), F32),
            pltpu.VMEM((plan.items, *window.shape), F32),
            pltpu.VMEM((plan.results, rows, plan.block * IMG), F32),
            pltpu.SemaphoreType.DMA((plan.items,)),
        ],
        1, "chain",
    )(section_len, grads, second, packed, *msgs)
    steps = batch_steps()
    grads = steps[0](grads)
    grads, blocks = lax.optimization_barrier((grads, blocks))
    for step in steps[1:]:
        grads = step(grads)
    received = [lax.ppermute(block, "depth", plan.out_pairs(k)) for k, block in enumerate(blocks)]
    states = call(
        functools.partial(collect_kernel, plan), state, [VMEM] * (2 + plan.results), [], 0.5, "collect"
    )(point, blocks[plan.local], *received)

    return states[None, None], adjoint_out[None, None], grads[:, :, :rows], grads[:, :, rows]


def solution(mesh):
    state = P("depth", "batch", None, None)
    return jax.shard_map(
        body,
        mesh=mesh,
        in_specs=(state, state, P("depth", None, None), P("depth", None), P(), P()),
        out_specs=(state, state, P("depth", None, None), P("depth", None)),
        check_vma=False,
    )
```

```python
import functools

import jax
import jax.numpy as jnp
from jax import lax
from jax.experimental import pallas as pl
from jax.experimental.pallas import tpu as pltpu
from jax.sharding import PartitionSpec as P

IMG = 64
LANES = 128
CHUNK = 256
AT_ONCE = 3
F32 = jnp.float32
BF16 = jnp.bfloat16


def split(x):
    hi = x.astype(BF16)
    lo = (x - hi.astype(F32)).astype(BF16)
    return hi, lo


def stack3(hi, lo):
    return jnp.concatenate([hi, lo, hi], axis=0)


def left_factor(matrix):
    hi = matrix.astype(BF16).astype(F32)
    return jnp.concatenate([hi, hi, matrix - hi], axis=1).astype(BF16)


def mm(a, b):
    return jnp.dot(a, b, preferred_element_type=F32)


def mm_nt(a, b):
    return lax.dot_general(a, b, (((1,), (1,)), ((), ())), preferred_element_type=F32)


def lane_masks(rows):
    lane = lax.broadcasted_iota(jnp.int32, (rows, LANES), 1)
    col = lane % IMG
    return col > 0, col < IMG - 1, lane < IMG


def neighbours(left, mid, right, masks):
    not_first, not_last, upper = masks
    pieces = [left] + [mid[:, k : k + LANES] for k in range(0, mid.shape[1], LANES)] + [right]
    swapped = [pltpu.roll(piece, IMG, 1) for piece in pieces]
    sums = []
    for k in range(1, len(pieces) - 1):
        piece = pieces[k]
        beside = jnp.where(not_first, pltpu.roll(piece, 1, 1), 0.0)
        beside += jnp.where(not_last, pltpu.roll(piece, LANES - 1, 1), 0.0)
        beside += swapped[k] + jnp.where(upper, swapped[k - 1], swapped[k + 1])
        sums.append(beside)
    return jnp.concatenate(sums, axis=1)


def sweep(buf, width, step):
    rows = buf.shape[0]
    masks = lane_masks(rows)
    before = buf[:, 0:LANES]
    for start in range(0, width, CHUNK):
        size = min(CHUNK, width - start)
        at = LANES + start
        mid = buf[:, at : at + size]
        after = buf[:, at + size : at + size + LANES]
        around = neighbours(before, mid, after, masks)
        before = mid[:, size - LANES :]
        buf[:, at : at + size] = step(start, size, mid, around)


def matrix_of(p_ref, slot):
    rows = p_ref.shape[0]
    return p_ref[:, slot * rows : (slot + 1) * rows]


def table_of(p_ref):
    return p_ref[:, p_ref.shape[1] - LANES :]


def bias_of(p_ref, slot):
    table = table_of(p_ref)
    pick = lax.broadcasted_iota(jnp.int32, table.shape, 1) == slot
    return jnp.sum(jnp.where(pick, table, 0.0), axis=1, keepdims=True)


def slots_of(p_ref):
    rows, width = p_ref.shape
    return (width - LANES) // rows


def prepare(p_ref, wl_ref, wt_ref):
    most = slots_of(p_ref)
    factor = 1.0 / most
    for slot in range(most):
        matrix = matrix_of(p_ref, slot)
        wl_ref[slot] = left_factor(matrix)
        wt_ref[slot] = left_factor((factor * matrix).T)
    return factor * table_of(p_ref)[:, most : most + 1], factor


def column(row):
    n = row.shape[1]
    same = lax.broadcasted_iota(jnp.int32, (n, n), 0) == lax.broadcasted_iota(jnp.int32, (n, n), 1)
    return jnp.sum(jnp.where(same, row, 0.0), axis=1, keepdims=True)


def length_of(p_ref, section):
    row = table_of(p_ref)[0:1, :]
    pick = lax.broadcasted_iota(jnp.int32, row.shape, 1) == slots_of(p_ref) + 1 + section
    return jnp.sum(jnp.where(pick, row, 0.0)).astype(jnp.int32)


def pack_kernel(
    w_any, b_any, diff_any, len_any, guess_any, p_ref, p0_ref, both_ref, w_ref, b_ref, diff_ref, len_ref, sem
):
    most, rows, _ = w_ref.shape
    width = guess_any.shape[1]
    copies = [
        pltpu.make_async_copy(source, target, sem.at[k])
        for k, (source, target) in enumerate(
            [(w_any, w_ref), (b_any, b_ref), (diff_any, diff_ref), (len_any, len_ref),
             (guess_any, both_ref.at[:, 0:width])]
        )
    ]
    for copy in copies:
        copy.start()
    for copy in copies[:-1]:
        copy.wait()
    wide = most * rows
    p_ref[:, wide:] = jnp.zeros((rows, LANES), F32)
    for slot in range(most):
        p_ref[:, slot * rows : (slot + 1) * rows] = w_ref[slot]
        p_ref[:, wide + slot : wide + slot + 1] = column(b_ref[slot : slot + 1, :])
    p_ref[:, wide + most : wide + most + 1] = column(diff_ref[...])
    lengths = len_ref[...].astype(F32)
    first = wide + most + 1
    p_ref[:, first : first + lengths.shape[1]] = jnp.broadcast_to(lengths, (rows, lengths.shape[1]))
    p0_ref[...] = jnp.zeros_like(p0_ref)
    p0_ref[:, 0:rows] = w_ref[0]
    p0_ref[:, rows : rows + 1] = column(b_ref[0:1, :])
    both_ref[:, width:] = p_ref[...]
    copies[-1].wait()


def forward_layer(buf, width, wl, wt, bias, spread, t_out=None, u_out=None):
    keep = 1.0 - 4.0 * spread

    def step(start, size, mid, around):
        hi, lo = split(mid)
        t_hi, t_lo = split(jnp.tanh(mm(wl, stack3(hi, lo)) + bias))
        if t_out is not None:
            t_out(start, size, t_hi, t_lo)
        if u_out is not None:
            u_out(start, size, hi, lo)
        return mid * keep + around * spread - mm(wt, stack3(t_hi, t_lo))

    sweep(buf, width, step)


def run_forward(buf, width, p_ref, wl_ref, wt_ref, spread, count, t_refs=None, u_refs=None):
    def saver(refs, slot):
        if refs is None:
            return None

        def save(start, size, hi, lo):
            refs[0][slot, :, start : start + size] = hi
            refs[1][slot, :, start : start + size] = lo

        return save

    @pl.loop(0, count)
    def _(slot):
        forward_layer(
            buf, width, wl_ref[slot], wt_ref[slot], bias_of(p_ref, slot), spread,
            saver(t_refs, slot), saver(u_refs, slot),
        )


def run_backward(buf, width, wl_ref, wt_ref, spread, count, t_refs, u_refs=None, grads=None):
    keep = 1.0 - 4.0 * spread

    @pl.loop(0, count)
    def _(passed):
        slot = count - 1 - passed
        wl, wt = wl_ref[slot], wt_ref[slot]
        rows = buf.shape[0]
        sums = []

        def step(start, size, mid, around):
            span = slice(start, start + size)
            hi, lo = split(mid)
            t = t_refs[0][slot, :, span].astype(F32) + t_refs[1][slot, :, span].astype(F32)
            q = (1.0 - t * t) * mm(wl, stack3(hi, lo))
            q_hi, q_lo = split(q)
            if grads is not None:
                _, _, lam_ref, q_ref = grads
                lam_ref[0:rows, span], lam_ref[rows:, span] = hi, lo
                q_ref[0:rows, span], q_ref[rows:, span] = q_hi, q_lo
                sums.append(sum(q[:, k : k + LANES] for k in range(0, size, LANES)))
            return mid * keep + around * spread - mm(wt, stack3(q_hi, q_lo))

        sweep(buf, width, step)
        if grads is not None:
            g_ref, factor, lam_ref, q_ref = grads

            def product(left, right):
                g = mm_nt(left, right)
                return g[:rows, :rows] + g[:rows, rows:] + g[rows:, :rows]

            gw = product(jnp.concatenate([ref[slot] for ref in t_refs], axis=0), lam_ref[...])
            gw += product(q_ref[...], jnp.concatenate([ref[slot] for ref in u_refs], axis=0))
            g_ref[slot, :, 0:rows] = -factor * gw
            g_ref[slot, :, rows : rows + 1] = -factor * jnp.sum(sum(sums), axis=1, keepdims=True)


def fill(buf, value):
    rows, width = value.shape
    zero = jnp.zeros((rows, LANES), F32)
    buf[:, 0:LANES] = zero
    buf[:, LANES + width :] = zero
    buf[:, LANES : LANES + width] = value


def inner(buf):
    return buf[:, LANES : buf.shape[1] - LANES]


class Plan:
    def __init__(self, count):
        self.count = count
        self.items = count - 2
        self.hosts = count // 2
        self.first = count // 4
        self.block = IMG // self.hosts
        self.rows = min(IMG, self.block + 2 * (count - 4))
        self.rows += self.rows % 2
        self.results = count - 3
        self.local = (self.first - 3) % self.results

    def window(self, host):
        start = host * self.block - (self.count - 4)
        return jnp.clip(start - start % 2, 0, IMG - self.rows)

    def in_pairs(self, shift):
        return [((h + shift) % self.items, h + self.first) for h in range(self.hosts)]

    def out_pairs(self, shift):
        pairs = [(h + self.first, 3 + (h + shift) % self.results) for h in range(self.hosts)]
        pairs = [(s, d) for s, d in pairs if s != d]
        return pairs + ([(0, 2)] if shift < self.hosts else [])


def lanes(row, size):
    return pl.ds(pl.multiple_of(row * IMG, LANES), size * IMG)


def push_kernel(both_ref, out_ref, buf, wl, wt):
    width = out_ref.shape[1]
    p_ref = both_ref.at[:, width:]
    spread, _ = prepare(p_ref, wl, wt)
    fill(buf, both_ref[:, 0:width])
    run_forward(buf, width, p_ref, wl, wt, spread, length_of(p_ref, lax.axis_index("depth")))
    out_ref[...] = inner(buf)


def tau_kernel(plan, point_ref, p_ref, p2_ref, second_ref, t_hi, t_lo, *rest):
    msgs, (buf, wl, wt, whole) = rest[:-4], rest[-4:]
    rows, width = point_ref.shape
    own = lax.axis_index("depth")
    count = length_of(p_ref, jnp.minimum(own + 1, plan.count - 1))
    spread, factor = prepare(p_ref, wl, wt)
    fill(buf, point_ref[...])
    run_forward(buf, width, p_ref, wl, wt, spread, count, (t_hi, t_lo))
    second_ref[...] = inner(buf)

    def coarse(matrix, bias, length):
        scale = length.astype(F32)
        forward_layer(
            buf, width, left_factor(matrix), left_factor((scale * factor * matrix).T), bias, scale * spread
        )

    @pl.when(own > 0)
    def _():
        buf[:, LANES : LANES + width] = point_ref[...]
        coarse(matrix_of(p_ref, 0), bias_of(p_ref, 0), count)
        whole[...] = second_ref[...] - inner(buf)

    @pl.when(own == 0)
    def _():
        coarse(p2_ref[:, 0:rows], p2_ref[:, rows : rows + 1], length_of(p_ref, 2))
        whole[...] = inner(buf)

    size = plan.rows * IMG
    bias = bias_of(p_ref, 0)
    for shift, msg in enumerate(msgs):
        host = lax.rem(own - shift + 2 * plan.items, plan.items)
        start = plan.window(jnp.minimum(host, plan.hosts - 1))
        msg[:, 0:size] = whole[:, lanes(start, plan.rows)]
        msg[:, size : size + rows] = matrix_of(p_ref, 0)
        msg[:, size + rows : size + rows + 1] = bias


def point_kernel(_, both_ref, before_ref, point_ref, t_hi, t_lo, u_hi, u_lo, buf, wl, wt):
    own = lax.axis_index("depth")
    width = point_ref.shape[1]

    @pl.when(own > 0)
    def _():
        p_before_ref = before_ref.at[:, width:]
        count = length_of(p_before_ref, jnp.maximum(own - 1, 0))
        spread, _ = prepare(p_before_ref, wl, wt)
        fill(buf, before_ref[:, 0:width])
        run_forward(buf, width, p_before_ref, wl, wt, spread, count)
        point_ref[...] = inner(buf)

    @pl.when(own == 0)
    def _():
        point_ref[...] = both_ref[:, 0:width]
        fill(buf, both_ref[:, 0:width])

    p_ref = both_ref.at[:, width:]
    spread, _ = prepare(p_ref, wl, wt)
    run_forward(
        buf, width, p_ref, wl, wt, spread, length_of(p_ref, own), (t_hi, t_lo), (u_hi, u_lo)
    )


def adjoint_kernel(
    _, adj_ref, adj_after_ref, p_ref, p_after_ref, t_next_hi, t_next_lo, t_hi, t_lo, u_hi, u_lo,
    adj_out_ref, g_ref, buf, wl, wt, lam_ref, q_ref,
):
    own = lax.axis_index("depth")
    last = lax.axis_size("depth") - 1
    width = adj_out_ref.shape[1]
    g_ref[...] = jnp.zeros_like(g_ref)

    @pl.when(own < last)
    def _():
        count = length_of(p_after_ref, jnp.minimum(own + 1, last))
        spread, _ = prepare(p_after_ref, wl, wt)
        fill(buf, adj_after_ref[...])
        run_backward(buf, width, wl, wt, spread, count, (t_next_hi, t_next_lo))

    @pl.when(own == last)
    def _():
        fill(buf, adj_ref[...])

    spread, factor = prepare(p_ref, wl, wt)
    run_backward(
        buf, width, wl, wt, spread, length_of(p_ref, own), (t_hi, t_lo), (u_hi, u_lo),
        (g_ref, factor, lam_ref, q_ref),
    )
    adj_out_ref[...] = inner(buf)


def chain_kernel(plan, _, second_ref, p_ref, *rest):
    msgs, rest = rest[: plan.items], rest[plan.items :]
    outs, (buf, held, done, wl, wt, sem) = rest[: plan.results], rest[plan.results :]
    own = lax.axis_index("depth")
    host = own - plan.first
    rows = held.shape[1]
    size = plan.rows * IMG
    piece = plan.block * IMG

    @pl.when(jnp.logical_and(host >= 0, host < plan.hosts))
    def _():
        copies = [
            pltpu.make_async_copy(msg, held.at[lax.rem(host + shift, plan.items)], sem.at[shift])
            for shift, msg in enumerate(msgs)
        ]
        for copy in copies:
            copy.start()
        for copy in copies:
            copy.wait()
        offset = host * plan.block - plan.window(host)
        most = slots_of(p_ref)
        spread = table_of(p_ref)[:, most : most + 1] * (1.0 / most)
        for item in range(2, plan.items):
            matrix = held[item, :, size : size + rows]
            scale = length_of(p_ref, item + 1).astype(F32) * (1.0 / most)
            wl[item] = left_factor(matrix)
            wt[item] = left_factor((scale * matrix).T)
        fill(buf, held[0, :, 0:size] + held[1, :, 0:size])

        def keep(result):
            done[result] = buf[:, pl.ds(pl.multiple_of(LANES + offset * IMG, LANES), piece)]

        keep(0)

        @pl.loop(2, plan.items)
        def _(item):
            forward_layer(
                buf, size, wl[item], wt[item], held[item, :, size + rows : size + rows + 1],
                length_of(p_ref, item + 1).astype(F32) * spread,
            )
            buf[:, LANES : LANES + size] = inner(buf) + held[item, :, 0:size]
            keep(item - 1)

        for shift, out in enumerate(outs):
            out[...] = done[lax.rem(host + shift, plan.results)]

    @pl.when(own == 0)
    def _():
        for shift, out in enumerate(outs):
            if shift < plan.hosts:
                out[...] = second_ref[:, shift * piece : (shift + 1) * piece]


def collect_kernel(plan, point_ref, local_ref, *rest):
    received, out_ref = rest[:-1], rest[-1]
    own = lax.axis_index("depth")
    host = own - plan.first

    @pl.when(own < 2)
    def _():
        out_ref[...] = point_ref[...]

    @pl.when(own == 2)
    def _():
        for shift, block in enumerate(received):
            if shift < plan.hosts:
                out_ref[:, lanes(shift * plan.block, plan.block)] = block[...]

    for shift, block in enumerate(received):
        sender = lax.rem(own - 3 - shift + 2 * plan.results, plan.results)

        @pl.when(jnp.logical_and(own > 2, jnp.logical_and(sender < plan.hosts, sender != host)))
        def _():
            out_ref[:, lanes(sender * plan.block, plan.block)] = block[...]

    @pl.when(jnp.logical_and(own > 2, jnp.logical_and(host >= 0, host < plan.hosts)))
    def _():
        out_ref[:, lanes(host * plan.block, plan.block)] = local_ref[...]


SMEM = pl.BlockSpec(memory_space=pltpu.SMEM)
VMEM = pl.BlockSpec(memory_space=pltpu.VMEM)
ANY = pl.BlockSpec(memory_space=pl.ANY)


def call(kernel, out_shape, in_specs, scratch, micros, name, mebi=32):
    return pl.pallas_call(
        kernel,
        out_shape=out_shape,
        in_specs=in_specs,
        out_specs=jax.tree.map(lambda _: VMEM, out_shape),
        scratch_shapes=scratch,
        compiler_params=pltpu.CompilerParams(vmem_limit_bytes=mebi * 2**20),
        cost_estimate=pl.CostEstimate(flops=int(micros * 1e8), bytes_accessed=2**21, transcendentals=0),
        name=name,
    )


def shifted(value, steps):
    count = lax.axis_size("depth")
    first, end = max(0, -steps), min(count, count - steps)
    return lax.ppermute(value, "depth", [(s, s + steps) for s in range(first, end)])


def batch_steps():
    count = lax.axis_size("batch")
    if count & (count - 1):
        return [lambda value: lax.psum(value, "batch")]

    def step(gap):
        return lambda value: value + lax.ppermute(value, "batch", [(s, s ^ gap) for s in range(count)])

    return [step(1 << k) for k in range(count.bit_length() - 1)]


def body(cpoint_guess, adjoint_guess, weights, biases, diffusion, section_len):
    plan = Plan(lax.axis_size("depth"))
    most, rows, _ = weights.shape
    width = cpoint_guess.shape[-1]
    guess, adjoint = cpoint_guess[0, 0], adjoint_guess[0, 0]

    def shape(*dims):
        return jax.ShapeDtypeStruct(dims, F32)

    state = shape(rows, width)
    buffer = pltpu.VMEM((rows, width + 2 * LANES), F32)
    factors = [pltpu.VMEM((most, rows, 3 * rows), BF16)] * 2

    wide = most * rows + LANES
    packed, packed0, both = call(
        pack_kernel, [shape(rows, wide), shape(rows, LANES), shape(rows, width + wide)], [ANY] * 5,
        [
            pltpu.VMEM(weights.shape, F32), pltpu.VMEM(biases.shape, F32), pltpu.VMEM((1, rows), F32),
            pltpu.VMEM((1, plan.count), jnp.int32), pltpu.SemaphoreType.DMA((5,)),
        ],
        1, "pack", 60,
    )(weights, biases, diffusion[None], section_len[None], guess)
    packed_after = shifted(packed, -1)
    packed_second = lax.ppermute(packed0, "depth", [(2, 0)])
    before = shifted(both, 1)
    after = call(push_kernel, state, [VMEM], [buffer, *factors], 40, "push")(both)
    after, packed_after, packed_second, adjoint_later = lax.optimization_barrier(
        (after, packed_after, packed_second, adjoint)
    )
    adj_after = shifted(adjoint_later, -1)

    saved = jax.ShapeDtypeStruct((most, rows, width), BF16)
    window = shape(rows, plan.rows * IMG + LANES)
    second, *rest = call(
        functools.partial(tau_kernel, plan), [state, saved, saved] + [window] * plan.items,
        [VMEM] * 3, [buffer, *factors, pltpu.VMEM((rows, width), F32)], 3, "tau",
    )(after, packed_after, packed_second)
    t_next, msgs = rest[:2], rest[2:]
    arrived = {plan.first: msgs[plan.first]}
    order = [shift for shift in range(plan.items) if shift != plan.first]
    for k, shift in enumerate(order):
        msg = msgs[shift]
        if k >= AT_ONCE:
            msg, _ = lax.optimization_barrier((msg, arrived[order[k - AT_ONCE]]))
        arrived[shift] = lax.ppermute(msg, "depth", plan.in_pairs(shift))
    msgs = [arrived[shift] for shift in range(plan.items)]

    point, *kept = call(
        point_kernel, [state] + [saved] * 4, [ANY] + [VMEM] * 2, [buffer, *factors], 6, "point"
    )(msgs[plan.first], both, before)

    pair = pltpu.VMEM((2 * rows, width), BF16)
    adjoint_out, grads = call(
        adjoint_kernel, [state, shape(most, rows, rows + 1)],
        [ANY] + [VMEM] * 10, [buffer, *factors, pair, pair], 10, "adjoint",
    )(point, adjoint, adj_after, packed, packed_after, *t_next, *kept)

    piece = shape(rows, plan.block * IMG)
    blocks = call(
        functools.partial(chain_kernel, plan), [piece] * plan.results,
        [ANY, VMEM, VMEM] + [ANY] * plan.items,
        [
            pltpu.VMEM((rows, plan.rows * IMG + 2 * LANES), F32),
            pltpu.VMEM((plan.items, *window.shape), F32),
            pltpu.VMEM((plan.results, *piece.shape), F32),
            pltpu.VMEM((plan.items, rows, 3 * rows), BF16),
            pltpu.VMEM((plan.items, rows, 3 * rows), BF16),
            pltpu.SemaphoreType.DMA((plan.items,)),
        ],
        1, "chain",
    )(grads, second, packed, *msgs)
    steps = batch_steps()
    grads = steps[0](grads)
    grads, blocks = lax.optimization_barrier((grads, blocks))
    for step in steps[1:]:
        grads = step(grads)
    received = [lax.ppermute(block, "depth", plan.out_pairs(k)) for k, block in enumerate(blocks)]

    states = call(
        functools.partial(collect_kernel, plan), state, [VMEM] * (2 + plan.results), [], 0.5, "collect"
    )(point, blocks[plan.local], *received)
    return states[None, None], adjoint_out[None, None], grads[:, :, :rows], grads[:, :, rows]


def solution(mesh):
    state = P("depth", "batch", None, None)
    return jax.shard_map(
        body,
        mesh=mesh,
        in_specs=(state, state, P("depth", None, None), P("depth", None), P(), P()),
        out_specs=(state, state, P("depth", None, None), P("depth", None)),
        check_vma=False,
    )
```

```python
import functools

import jax
import jax.numpy as jnp
from jax import lax
from jax.experimental import pallas as pl
from jax.experimental.pallas import tpu as pltpu
from jax.sharding import PartitionSpec as P

IMG = 64
LANES = 128
CHUNK = 256
AT_ONCE = 4
F32 = jnp.float32
BF16 = jnp.bfloat16


def split(x):
    hi = x.astype(BF16)
    lo = (x - hi.astype(F32)).astype(BF16)
    return hi, lo


def stack3(hi, lo):
    return jnp.concatenate([hi, lo, hi], axis=0)


def left_factor(matrix):
    hi = matrix.astype(BF16).astype(F32)
    return jnp.concatenate([hi, hi, matrix - hi], axis=1).astype(BF16)


def mm(a, b):
    return jnp.dot(a, b, preferred_element_type=F32)


def mm_nt(a, b):
    return lax.dot_general(a, b, (((1,), (1,)), ((), ())), preferred_element_type=F32)


def lane_masks(rows):
    lane = lax.broadcasted_iota(jnp.int32, (rows, LANES), 1)
    col = lane % IMG
    return col > 0, col < IMG - 1, lane < IMG


def neighbours(left, mid, right, masks):
    not_first, not_last, upper = masks
    pieces = [left] + [mid[:, k : k + LANES] for k in range(0, mid.shape[1], LANES)] + [right]
    swapped = [pltpu.roll(piece, IMG, 1) for piece in pieces]
    sums = []
    for k in range(1, len(pieces) - 1):
        piece = pieces[k]
        beside = jnp.where(not_first, pltpu.roll(piece, 1, 1), 0.0)
        beside += jnp.where(not_last, pltpu.roll(piece, LANES - 1, 1), 0.0)
        beside += swapped[k] + jnp.where(upper, swapped[k - 1], swapped[k + 1])
        sums.append(beside)
    return jnp.concatenate(sums, axis=1)


def sweep(buf, width, step):
    rows = buf.shape[0]
    masks = lane_masks(rows)
    before = buf[:, 0:LANES]
    for start in range(0, width, CHUNK):
        size = min(CHUNK, width - start)
        at = LANES + start
        mid = buf[:, at : at + size]
        after = buf[:, at + size : at + size + LANES]
        around = neighbours(before, mid, after, masks)
        before = mid[:, size - LANES :]
        buf[:, at : at + size] = step(start, size, mid, around)


def matrix_of(p_ref, slot):
    rows = p_ref.shape[0]
    return p_ref[:, slot * rows : (slot + 1) * rows]


def table_of(p_ref):
    return p_ref[:, p_ref.shape[1] - LANES :]


def bias_of(p_ref, slot):
    table = table_of(p_ref)
    pick = lax.broadcasted_iota(jnp.int32, table.shape, 1) == slot
    return jnp.sum(jnp.where(pick, table, 0.0), axis=1, keepdims=True)


def slots_of(p_ref):
    rows, width = p_ref.shape
    return (width - LANES) // rows


def prepare(p_ref, wl_ref, wt_ref):
    most = slots_of(p_ref)
    factor = 1.0 / most
    for slot in range(most):
        matrix = matrix_of(p_ref, slot)
        wl_ref[slot] = left_factor(matrix)
        wt_ref[slot] = left_factor((factor * matrix).T)
    return factor * table_of(p_ref)[:, most : most + 1], factor


def column(row):
    n = row.shape[1]
    same = lax.broadcasted_iota(jnp.int32, (n, n), 0) == lax.broadcasted_iota(jnp.int32, (n, n), 1)
    return jnp.sum(jnp.where(same, row, 0.0), axis=1, keepdims=True)


def length_of(p_ref, section):
    row = table_of(p_ref)[0:1, :]
    pick = lax.broadcasted_iota(jnp.int32, row.shape, 1) == slots_of(p_ref) + 1 + section
    return jnp.sum(jnp.where(pick, row, 0.0)).astype(jnp.int32)


def pack_kernel(
    w_any, b_any, diff_any, len_any, guess_any, p_ref, p0_ref, both_ref, w_ref, b_ref, diff_ref, len_ref, sem
):
    most, rows, _ = w_ref.shape
    width = guess_any.shape[1]
    copies = [
        pltpu.make_async_copy(source, target, sem.at[k])
        for k, (source, target) in enumerate(
            [(w_any, w_ref), (b_any, b_ref), (diff_any, diff_ref), (len_any, len_ref),
             (guess_any, both_ref.at[:, 0:width])]
        )
    ]
    for copy in copies:
        copy.start()
    for copy in copies[:-1]:
        copy.wait()
    wide = most * rows
    p_ref[:, wide:] = jnp.zeros((rows, LANES), F32)
    for slot in range(most):
        p_ref[:, slot * rows : (slot + 1) * rows] = w_ref[slot]
        p_ref[:, wide + slot : wide + slot + 1] = column(b_ref[slot : slot + 1, :])
    p_ref[:, wide + most : wide + most + 1] = column(diff_ref[...])
    lengths = len_ref[...].astype(F32)
    first = wide + most + 1
    p_ref[:, first : first + lengths.shape[1]] = jnp.broadcast_to(lengths, (rows, lengths.shape[1]))
    p0_ref[...] = jnp.zeros_like(p0_ref)
    p0_ref[:, 0:rows] = w_ref[0]
    p0_ref[:, rows : rows + 1] = column(b_ref[0:1, :])
    both_ref[:, width:] = p_ref[...]
    copies[-1].wait()


def forward_layer(buf, width, wl, wt, bias, spread, t_out=None, u_out=None):
    keep = 1.0 - 4.0 * spread

    def step(start, size, mid, around):
        hi, lo = split(mid)
        t_hi, t_lo = split(jnp.tanh(mm(wl, stack3(hi, lo)) + bias))
        if t_out is not None:
            t_out(start, size, t_hi, t_lo)
        if u_out is not None:
            u_out(start, size, hi, lo)
        return mid * keep + around * spread - mm(wt, stack3(t_hi, t_lo))

    sweep(buf, width, step)


def run_forward(buf, width, p_ref, wl_ref, wt_ref, spread, count, t_refs=None, u_refs=None):
    def saver(refs, slot):
        if refs is None:
            return None

        def save(start, size, hi, lo):
            refs[0][slot, :, start : start + size] = hi
            refs[1][slot, :, start : start + size] = lo

        return save

    @pl.loop(0, count)
    def _(slot):
        forward_layer(
            buf, width, wl_ref[slot], wt_ref[slot], bias_of(p_ref, slot), spread,
            saver(t_refs, slot), saver(u_refs, slot),
        )


def run_backward(buf, width, wl_ref, wt_ref, spread, count, t_refs, u_refs=None, grads=None):
    keep = 1.0 - 4.0 * spread

    @pl.loop(0, count)
    def _(passed):
        slot = count - 1 - passed
        wl, wt = wl_ref[slot], wt_ref[slot]
        rows = buf.shape[0]
        sums = []

        def step(start, size, mid, around):
            span = slice(start, start + size)
            hi, lo = split(mid)
            t = t_refs[0][slot, :, span].astype(F32) + t_refs[1][slot, :, span].astype(F32)
            q = (1.0 - t * t) * mm(wl, stack3(hi, lo))
            q_hi, q_lo = split(q)
            if grads is not None:
                _, _, lam_ref, q_ref = grads
                lam_ref[0:rows, span], lam_ref[rows:, span] = hi, lo
                q_ref[0:rows, span], q_ref[rows:, span] = q_hi, q_lo
                sums.append(sum(q[:, k : k + LANES] for k in range(0, size, LANES)))
            return mid * keep + around * spread - mm(wt, stack3(q_hi, q_lo))

        sweep(buf, width, step)
        if grads is not None:
            g_ref, factor, lam_ref, q_ref = grads

            def product(left, right):
                g = mm_nt(left, right)
                return g[:rows, :rows] + g[:rows, rows:] + g[rows:, :rows]

            gw = product(jnp.concatenate([ref[slot] for ref in t_refs], axis=0), lam_ref[...])
            gw += product(q_ref[...], jnp.concatenate([ref[slot] for ref in u_refs], axis=0))
            g_ref[slot, :, 0:rows] = -factor * gw
            g_ref[slot, :, rows : rows + 1] = -factor * jnp.sum(sum(sums), axis=1, keepdims=True)


def fill(buf, value):
    rows, width = value.shape
    zero = jnp.zeros((rows, LANES), F32)
    buf[:, 0:LANES] = zero
    buf[:, LANES + width :] = zero
    buf[:, LANES : LANES + width] = value


def inner(buf):
    return buf[:, LANES : buf.shape[1] - LANES]


class Plan:
    def __init__(self, count):
        self.count = count
        self.items = count - 2
        self.hosts = count // 2
        self.first = count // 4
        self.block = IMG // self.hosts
        self.rows = min(IMG, self.block + 2 * (count - 4))
        self.rows += self.rows % 2
        self.results = count - 3
        self.local = (self.first - 3) % self.results

    def window(self, host):
        start = host * self.block - (self.count - 4)
        return jnp.clip(start - start % 2, 0, IMG - self.rows)

    def in_pairs(self, shift):
        return [((h + shift) % self.items, h + self.first) for h in range(self.hosts)]

    def out_pairs(self, shift):
        pairs = [(h + self.first, 3 + (h + shift) % self.results) for h in range(self.hosts)]
        pairs = [(s, d) for s, d in pairs if s != d]
        return pairs + ([(0, 2)] if shift < self.hosts else [])


def lanes(row, size):
    return pl.ds(pl.multiple_of(row * IMG, LANES), size * IMG)


def push_kernel(both_ref, out_ref, buf, wl, wt):
    width = out_ref.shape[1]
    p_ref = both_ref.at[:, width:]
    spread, _ = prepare(p_ref, wl, wt)
    fill(buf, both_ref[:, 0:width])
    run_forward(buf, width, p_ref, wl, wt, spread, length_of(p_ref, lax.axis_index("depth")))
    out_ref[...] = inner(buf)


def tau_kernel(plan, point_ref, p_ref, p2_ref, second_ref, *rest):
    msgs, (buf, wl, wt, whole) = rest[:-4], rest[-4:]
    rows, width = point_ref.shape
    own = lax.axis_index("depth")
    count = length_of(p_ref, jnp.minimum(own + 1, plan.count - 1))
    spread, factor = prepare(p_ref, wl, wt)
    fill(buf, point_ref[...])
    run_forward(buf, width, p_ref, wl, wt, spread, count)
    second_ref[...] = inner(buf)

    def coarse(matrix, bias, length):
        scale = length.astype(F32)
        forward_layer(
            buf, width, left_factor(matrix), left_factor((scale * factor * matrix).T), bias, scale * spread
        )

    @pl.when(own > 0)
    def _():
        buf[:, LANES : LANES + width] = point_ref[...]
        coarse(matrix_of(p_ref, 0), bias_of(p_ref, 0), count)
        whole[...] = second_ref[...] - inner(buf)

    @pl.when(own == 0)
    def _():
        coarse(p2_ref[:, 0:rows], p2_ref[:, rows : rows + 1], length_of(p_ref, 2))
        whole[...] = inner(buf)

    size = plan.rows * IMG
    bias = bias_of(p_ref, 0)
    for shift, msg in enumerate(msgs):
        host = lax.rem(own - shift + 2 * plan.items, plan.items)
        start = plan.window(jnp.minimum(host, plan.hosts - 1))
        msg[:, 0:size] = whole[:, lanes(start, plan.rows)]
        msg[:, size : size + rows] = matrix_of(p_ref, 0)
        msg[:, size + rows : size + rows + 1] = bias


def point_kernel(_, both_ref, before_ref, adj_ref, point_ref, lam_ref, t_hi, t_lo, u_hi, u_lo, buf, wl, wt):
    own = lax.axis_index("depth")
    width = point_ref.shape[1]

    @pl.when(own > 0)
    def _():
        p_before_ref = before_ref.at[:, width:]
        count = length_of(p_before_ref, jnp.maximum(own - 1, 0))
        spread, _ = prepare(p_before_ref, wl, wt)
        fill(buf, before_ref[:, 0:width])
        run_forward(buf, width, p_before_ref, wl, wt, spread, count)
        point_ref[...] = inner(buf)

    @pl.when(own == 0)
    def _():
        point_ref[...] = both_ref[:, 0:width]
        fill(buf, both_ref[:, 0:width])

    p_ref = both_ref.at[:, width:]
    count = length_of(p_ref, own)
    spread, _ = prepare(p_ref, wl, wt)
    run_forward(buf, width, p_ref, wl, wt, spread, count, (t_hi, t_lo), (u_hi, u_lo))

    @pl.when(own > 0)
    def _():
        fill(buf, adj_ref[...])
        run_backward(buf, width, wl, wt, spread, count, (t_hi, t_lo))
        lam_ref[...] = inner(buf)


def adjoint_kernel(
    _, adj_ref, lam_after_ref, p_ref, t_hi, t_lo, u_hi, u_lo, adj_out_ref, g_ref, buf, wl, wt, lam_ref, q_ref, g_all
):
    own = lax.axis_index("depth")
    last = lax.axis_size("depth") - 1
    rows, width = adj_out_ref.shape
    g_all[...] = jnp.zeros_like(g_all)

    @pl.when(own < last)
    def _():
        fill(buf, lam_after_ref[...])

    @pl.when(own == last)
    def _():
        fill(buf, adj_ref[...])

    spread, factor = prepare(p_ref, wl, wt)
    run_backward(
        buf, width, wl, wt, spread, length_of(p_ref, own), (t_hi, t_lo), (u_hi, u_lo),
        (g_all, factor, lam_ref, q_ref),
    )
    adj_out_ref[...] = inner(buf)
    most = g_all.shape[0]
    g_ref[:, most * rows :] = jnp.zeros((rows, LANES), F32)
    for slot in range(most):
        g_ref[:, slot * rows : (slot + 1) * rows] = g_all[slot, :, 0:rows]
        g_ref[:, most * rows + slot : most * rows + slot + 1] = g_all[slot, :, rows : rows + 1]


def sum_kernel(*refs):
    parts, (gw_ref, gb_ref) = refs[:-2], refs[-2:]
    most, rows, _ = gw_ref.shape
    total = sum(part[...] for part in parts)
    for slot in range(most):
        gw_ref[slot] = total[:, slot * rows : (slot + 1) * rows]
    gb_ref[...] = total[:, most * rows :].T[:most, :]


def chain_kernel(plan, _, second_ref, p_ref, *rest):
    msgs, rest = rest[: plan.items], rest[plan.items :]
    outs, (buf, held, done, wl, wt, sem) = rest[: plan.results], rest[plan.results :]
    own = lax.axis_index("depth")
    host = own - plan.first
    rows = held.shape[1]
    size = plan.rows * IMG
    piece = plan.block * IMG

    @pl.when(jnp.logical_and(host >= 0, host < plan.hosts))
    def _():
        copies = [
            pltpu.make_async_copy(msg, held.at[lax.rem(host + shift, plan.items)], sem.at[shift])
            for shift, msg in enumerate(msgs)
        ]
        for copy in copies:
            copy.start()
        for copy in copies:
            copy.wait()
        offset = host * plan.block - plan.window(host)
        most = slots_of(p_ref)
        spread = table_of(p_ref)[:, most : most + 1] * (1.0 / most)
        for item in range(2, plan.items):
            matrix = held[item, :, size : size + rows]
            scale = length_of(p_ref, item + 1).astype(F32) * (1.0 / most)
            wl[item] = left_factor(matrix)
            wt[item] = left_factor((scale * matrix).T)
        fill(buf, held[0, :, 0:size] + held[1, :, 0:size])

        def keep(result):
            done[result] = buf[:, pl.ds(pl.multiple_of(LANES + offset * IMG, LANES), piece)]

        keep(0)

        @pl.loop(2, plan.items)
        def _(item):
            forward_layer(
                buf, size, wl[item], wt[item], held[item, :, size + rows : size + rows + 1],
                length_of(p_ref, item + 1).astype(F32) * spread,
            )
            buf[:, LANES : LANES + size] = inner(buf) + held[item, :, 0:size]
            keep(item - 1)

        for shift, out in enumerate(outs):
            out[...] = done[lax.rem(host + shift, plan.results)]

    @pl.when(own == 0)
    def _():
        for shift, out in enumerate(outs):
            if shift < plan.hosts:
                out[...] = second_ref[:, shift * piece : (shift + 1) * piece]


def collect_kernel(plan, point_ref, local_ref, *rest):
    received, out_ref = rest[:-1], rest[-1]
    own = lax.axis_index("depth")
    host = own - plan.first

    @pl.when(own < 2)
    def _():
        out_ref[...] = point_ref[...]

    @pl.when(own == 2)
    def _():
        for shift, block in enumerate(received):
            if shift < plan.hosts:
                out_ref[:, lanes(shift * plan.block, plan.block)] = block[...]

    for shift, block in enumerate(received):
        sender = lax.rem(own - 3 - shift + 2 * plan.results, plan.results)

        @pl.when(jnp.logical_and(own > 2, jnp.logical_and(sender < plan.hosts, sender != host)))
        def _():
            out_ref[:, lanes(sender * plan.block, plan.block)] = block[...]

    @pl.when(jnp.logical_and(own > 2, jnp.logical_and(host >= 0, host < plan.hosts)))
    def _():
        out_ref[:, lanes(host * plan.block, plan.block)] = local_ref[...]


SMEM = pl.BlockSpec(memory_space=pltpu.SMEM)
VMEM = pl.BlockSpec(memory_space=pltpu.VMEM)
ANY = pl.BlockSpec(memory_space=pl.ANY)


def call(kernel, out_shape, in_specs, scratch, micros, name, mebi=32):
    return pl.pallas_call(
        kernel,
        out_shape=out_shape,
        in_specs=in_specs,
        out_specs=jax.tree.map(lambda _: VMEM, out_shape),
        scratch_shapes=scratch,
        compiler_params=pltpu.CompilerParams(vmem_limit_bytes=mebi * 2**20),
        cost_estimate=pl.CostEstimate(flops=int(micros * 1e8), bytes_accessed=2**21, transcendentals=0),
        name=name,
    )


def shifted(value, steps):
    count = lax.axis_size("depth")
    first, end = max(0, -steps), min(count, count - steps)
    return lax.ppermute(value, "depth", [(s, s + steps) for s in range(first, end)])


def others(value, step):
    count = lax.axis_size("batch")
    xor = count & (count - 1) == 0
    return lax.ppermute(value, "batch", [(s, s ^ step if xor else (s + step) % count) for s in range(count)])


def body(cpoint_guess, adjoint_guess, weights, biases, diffusion, section_len):
    plan = Plan(lax.axis_size("depth"))
    most, rows, _ = weights.shape
    width = cpoint_guess.shape[-1]
    guess, adjoint = cpoint_guess[0, 0], adjoint_guess[0, 0]

    def shape(*dims):
        return jax.ShapeDtypeStruct(dims, F32)

    state = shape(rows, width)
    buffer = pltpu.VMEM((rows, width + 2 * LANES), F32)
    factors = [pltpu.VMEM((most, rows, 3 * rows), BF16)] * 2

    wide = most * rows + LANES
    packed, packed0, both = call(
        pack_kernel, [shape(rows, wide), shape(rows, LANES), shape(rows, width + wide)], [ANY] * 5,
        [
            pltpu.VMEM(weights.shape, F32), pltpu.VMEM(biases.shape, F32), pltpu.VMEM((1, rows), F32),
            pltpu.VMEM((1, plan.count), jnp.int32), pltpu.SemaphoreType.DMA((5,)),
        ],
        1, "pack", 60,
    )(weights, biases, diffusion[None], section_len[None], guess)
    packed_after = shifted(packed, -1)
    packed_second = lax.ppermute(packed0, "depth", [(2, 0)])
    before = shifted(both, 1)
    after = call(push_kernel, state, [VMEM], [buffer, *factors], 40, "push")(both)
    after, packed_after, packed_second = lax.optimization_barrier((after, packed_after, packed_second))

    saved = jax.ShapeDtypeStruct((most, rows, width), BF16)
    window = shape(rows, plan.rows * IMG + LANES)
    second, *msgs = call(
        functools.partial(tau_kernel, plan), [state] + [window] * plan.items,
        [VMEM] * 3, [buffer, *factors, pltpu.VMEM((rows, width), F32)], 3, "tau",
    )(after, packed_after, packed_second)
    arrived = {plan.first: msgs[plan.first]}
    order = [shift for shift in range(plan.items) if shift != plan.first]
    for k, shift in enumerate(order):
        msg = msgs[shift]
        if k >= AT_ONCE:
            msg, _ = lax.optimization_barrier((msg, arrived[order[k - AT_ONCE]]))
        arrived[shift] = lax.ppermute(msg, "depth", plan.in_pairs(shift))
    msgs = [arrived[shift] for shift in range(plan.items)]

    point, lam, *kept = call(
        point_kernel, [state] * 2 + [saved] * 4, [ANY] + [VMEM] * 3, [buffer, *factors], 6, "point"
    )(msgs[plan.first], both, before, adjoint)
    lam, msgs = lax.optimization_barrier((lam, msgs))
    lam_after = shifted(lam, -1)

    piece = shape(rows, plan.block * IMG)
    blocks = call(
        functools.partial(chain_kernel, plan), [piece] * plan.results,
        [ANY, VMEM, VMEM] + [ANY] * plan.items,
        [
            pltpu.VMEM((rows, plan.rows * IMG + 2 * LANES), F32),
            pltpu.VMEM((plan.items, *window.shape), F32),
            pltpu.VMEM((plan.results, *piece.shape), F32),
            pltpu.VMEM((plan.items, rows, 3 * rows), BF16),
            pltpu.VMEM((plan.items, rows, 3 * rows), BF16),
            pltpu.SemaphoreType.DMA((plan.items,)),
        ],
        1, "chain",
    )(lam, second, packed, *msgs)
    received = [lax.ppermute(block, "depth", plan.out_pairs(k)) for k, block in enumerate(blocks)]

    pair = pltpu.VMEM((2 * rows, width), BF16)
    adjoint_out, grads = call(
        adjoint_kernel, [state, shape(rows, wide)], [ANY] + [VMEM] * 7,
        [buffer, *factors, pair, pair, pltpu.VMEM((most, rows, rows + 1), F32)], 10, "adjoint",
    )(blocks[plan.local], adjoint, lam_after, packed, *kept)

    states = call(
        functools.partial(collect_kernel, plan), state, [VMEM] * (2 + plan.results), [], 0.5, "collect"
    )(point, blocks[plan.local], *received)
    grads, *_ = lax.optimization_barrier((grads, *received))
    parts = [grads] + [others(grads, step) for step in range(1, lax.axis_size("batch"))]
    gw, gb = call(
        sum_kernel, [shape(*weights.shape), shape(*biases.shape)], [VMEM] * len(parts), [], 0.5, "sum"
    )(*parts)
    return states[None, None], adjoint_out[None, None], gw, gb


def solution(mesh):
    state = P("depth", "batch", None, None)
    return jax.shard_map(
        body,
        mesh=mesh,
        in_specs=(state, state, P("depth", None, None), P("depth", None), P(), P()),
        out_specs=(state, state, P("depth", None, None), P("depth", None)),
        check_vma=False,
    )
```

```python
import functools

import jax
import jax.numpy as jnp
from jax import lax
from jax.experimental import pallas as pl
from jax.experimental.pallas import tpu as pltpu
from jax.sharding import PartitionSpec as P

IMG = 64
LANES = 128
CHUNK = 256
AT_ONCE = 3
F32 = jnp.float32
BF16 = jnp.bfloat16


def split(x):
    hi = x.astype(BF16)
    lo = (x - hi.astype(F32)).astype(BF16)
    return hi, lo


def stack3(hi, lo):
    return jnp.concatenate([hi, lo, hi], axis=0)


def left_factor(matrix):
    hi = matrix.astype(BF16).astype(F32)
    return jnp.concatenate([hi, hi, matrix - hi], axis=1).astype(BF16)


def mm(a, b):
    return jnp.dot(a, b, preferred_element_type=F32)


def mm_nt(a, b):
    return lax.dot_general(a, b, (((1,), (1,)), ((), ())), preferred_element_type=F32)


def lane_masks(rows):
    lane = lax.broadcasted_iota(jnp.int32, (rows, LANES), 1)
    col = lane % IMG
    return col > 0, col < IMG - 1, lane < IMG


def neighbours(left, mid, right, masks):
    not_first, not_last, upper = masks
    pieces = [left] + [mid[:, k : k + LANES] for k in range(0, mid.shape[1], LANES)] + [right]
    swapped = [pltpu.roll(piece, IMG, 1) for piece in pieces]
    sums = []
    for k in range(1, len(pieces) - 1):
        piece = pieces[k]
        beside = jnp.where(not_first, pltpu.roll(piece, 1, 1), 0.0)
        beside += jnp.where(not_last, pltpu.roll(piece, LANES - 1, 1), 0.0)
        beside += swapped[k] + jnp.where(upper, swapped[k - 1], swapped[k + 1])
        sums.append(beside)
    return jnp.concatenate(sums, axis=1)


def sweep(buf, width, step):
    rows = buf.shape[0]
    masks = lane_masks(rows)
    before = buf[:, 0:LANES]
    for start in range(0, width, CHUNK):
        size = min(CHUNK, width - start)
        at = LANES + start
        mid = buf[:, at : at + size]
        after = buf[:, at + size : at + size + LANES]
        around = neighbours(before, mid, after, masks)
        before = mid[:, size - LANES :]
        buf[:, at : at + size] = step(start, size, mid, around)


def matrix_of(p_ref, slot):
    rows = p_ref.shape[0]
    return p_ref[:, slot * rows : (slot + 1) * rows]


def table_of(p_ref):
    return p_ref[:, p_ref.shape[1] - LANES :]


def bias_of(p_ref, slot):
    table = table_of(p_ref)
    pick = lax.broadcasted_iota(jnp.int32, table.shape, 1) == slot
    return jnp.sum(jnp.where(pick, table, 0.0), axis=1, keepdims=True)


def slots_of(p_ref):
    rows, width = p_ref.shape
    return (width - LANES) // rows


def prepare(p_ref, wl_ref, wt_ref):
    most = slots_of(p_ref)
    factor = 1.0 / most
    for slot in range(most):
        matrix = matrix_of(p_ref, slot)
        wl_ref[slot] = left_factor(matrix)
        wt_ref[slot] = left_factor((factor * matrix).T)
    return factor * table_of(p_ref)[:, most : most + 1], factor


def column(row):
    n = row.shape[1]
    same = lax.broadcasted_iota(jnp.int32, (n, n), 0) == lax.broadcasted_iota(jnp.int32, (n, n), 1)
    return jnp.sum(jnp.where(same, row, 0.0), axis=1, keepdims=True)


def length_of(p_ref, section):
    row = table_of(p_ref)[0:1, :]
    pick = lax.broadcasted_iota(jnp.int32, row.shape, 1) == slots_of(p_ref) + 1 + section
    return jnp.sum(jnp.where(pick, row, 0.0)).astype(jnp.int32)


def pack_kernel(
    w_any, b_any, diff_any, len_any, guess_any, p_ref, p0_ref, both_ref, w_ref, b_ref, diff_ref, len_ref, sem
):
    most, rows, _ = w_ref.shape
    width = guess_any.shape[1]
    copies = [
        pltpu.make_async_copy(source, target, sem.at[k])
        for k, (source, target) in enumerate(
            [(w_any, w_ref), (b_any, b_ref), (diff_any, diff_ref), (len_any, len_ref),
             (guess_any, both_ref.at[:, 0:width])]
        )
    ]
    for copy in copies:
        copy.start()
    for copy in copies[:-1]:
        copy.wait()
    wide = most * rows
    p_ref[:, wide:] = jnp.zeros((rows, LANES), F32)
    for slot in range(most):
        p_ref[:, slot * rows : (slot + 1) * rows] = w_ref[slot]
        p_ref[:, wide + slot : wide + slot + 1] = column(b_ref[slot : slot + 1, :])
    p_ref[:, wide + most : wide + most + 1] = column(diff_ref[...])
    lengths = len_ref[...].astype(F32)
    first = wide + most + 1
    p_ref[:, first : first + lengths.shape[1]] = jnp.broadcast_to(lengths, (rows, lengths.shape[1]))
    p0_ref[...] = jnp.zeros_like(p0_ref)
    p0_ref[:, 0:rows] = w_ref[0]
    p0_ref[:, rows : rows + 1] = column(b_ref[0:1, :])
    both_ref[:, width:] = p_ref[...]
    copies[-1].wait()


def forward_layer(buf, width, wl, wt, bias, spread, t_out=None, u_out=None):
    keep = 1.0 - 4.0 * spread

    def step(start, size, mid, around):
        hi, lo = split(mid)
        t_hi, t_lo = split(jnp.tanh(mm(wl, stack3(hi, lo)) + bias))
        if t_out is not None:
            t_out(start, size, t_hi, t_lo)
        if u_out is not None:
            u_out(start, size, hi, lo)
        return mid * keep + around * spread - mm(wt, stack3(t_hi, t_lo))

    sweep(buf, width, step)


def run_forward(buf, width, p_ref, wl_ref, wt_ref, spread, count, t_refs=None, u_refs=None):
    def saver(refs, slot):
        if refs is None:
            return None

        def save(start, size, hi, lo):
            refs[0][slot, :, start : start + size] = hi
            refs[1][slot, :, start : start + size] = lo

        return save

    @pl.loop(0, count)
    def _(slot):
        forward_layer(
            buf, width, wl_ref[slot], wt_ref[slot], bias_of(p_ref, slot), spread,
            saver(t_refs, slot), saver(u_refs, slot),
        )


def run_backward(buf, width, wl_ref, wt_ref, spread, count, t_refs, u_refs=None, grads=None):
    keep = 1.0 - 4.0 * spread

    @pl.loop(0, count)
    def _(passed):
        slot = count - 1 - passed
        wl, wt = wl_ref[slot], wt_ref[slot]
        rows = buf.shape[0]
        sums = []

        def step(start, size, mid, around):
            span = slice(start, start + size)
            hi, lo = split(mid)
            t = t_refs[0][slot, :, span].astype(F32) + t_refs[1][slot, :, span].astype(F32)
            q = (1.0 - t * t) * mm(wl, stack3(hi, lo))
            q_hi, q_lo = split(q)
            if grads is not None:
                _, _, lam_ref, q_ref = grads
                lam_ref[0:rows, span], lam_ref[rows:, span] = hi, lo
                q_ref[0:rows, span], q_ref[rows:, span] = q_hi, q_lo
                sums.append(sum(q[:, k : k + LANES] for k in range(0, size, LANES)))
            return mid * keep + around * spread - mm(wt, stack3(q_hi, q_lo))

        sweep(buf, width, step)
        if grads is not None:
            g_ref, factor, lam_ref, q_ref = grads

            def product(left, right):
                g = mm_nt(left, right)
                return g[:rows, :rows] + g[:rows, rows:] + g[rows:, :rows]

            gw = product(jnp.concatenate([ref[slot] for ref in t_refs], axis=0), lam_ref[...])
            gw += product(q_ref[...], jnp.concatenate([ref[slot] for ref in u_refs], axis=0))
            g_ref[slot, :, 0:rows] = -factor * gw
            g_ref[slot, :, rows : rows + 1] = -factor * jnp.sum(sum(sums), axis=1, keepdims=True)


def fill(buf, value):
    rows, width = value.shape
    zero = jnp.zeros((rows, LANES), F32)
    buf[:, 0:LANES] = zero
    buf[:, LANES + width :] = zero
    buf[:, LANES : LANES + width] = value


def inner(buf):
    return buf[:, LANES : buf.shape[1] - LANES]


class Plan:
    def __init__(self, count):
        self.count = count
        self.items = count - 2
        self.hosts = count // 2
        self.first = count // 4
        self.block = IMG // self.hosts
        self.rows = min(IMG, self.block + 2 * (count - 4))
        self.rows += self.rows % 2
        self.results = count - 3
        self.local = (self.first - 3) % self.results

    def window(self, host):
        start = host * self.block - (self.count - 4)
        return jnp.clip(start - start % 2, 0, IMG - self.rows)

    def in_order(self):
        shifts = [s for s in range(self.items) if s != self.first]
        return sorted(shifts, key=lambda s: (s - self.first) % 2)

    def in_pairs(self, shift):
        return [((h + shift) % self.items, h + self.first) for h in range(self.hosts)]

    def out_pairs(self, shift):
        pairs = [(h + self.first, 3 + (h + shift) % self.results) for h in range(self.hosts)]
        pairs = [(s, d) for s, d in pairs if s != d]
        return pairs + ([(0, 2)] if shift < self.hosts else [])


def lanes(row, size):
    return pl.ds(pl.multiple_of(row * IMG, LANES), size * IMG)


def push_kernel(both_ref, out_ref, buf, wl, wt):
    width = out_ref.shape[1]
    p_ref = both_ref.at[:, width:]
    spread, _ = prepare(p_ref, wl, wt)
    fill(buf, both_ref[:, 0:width])
    run_forward(buf, width, p_ref, wl, wt, spread, length_of(p_ref, lax.axis_index("depth")))
    out_ref[...] = inner(buf)


def tau_kernel(plan, point_ref, p_ref, p2_ref, second_ref, t_hi, t_lo, *rest):
    msgs, (buf, wl, wt, whole) = rest[:-4], rest[-4:]
    rows, width = point_ref.shape
    own = lax.axis_index("depth")
    count = length_of(p_ref, jnp.minimum(own + 1, plan.count - 1))
    spread, factor = prepare(p_ref, wl, wt)
    fill(buf, point_ref[...])
    run_forward(buf, width, p_ref, wl, wt, spread, count, (t_hi, t_lo))
    second_ref[...] = inner(buf)

    def coarse(matrix, bias, length):
        scale = length.astype(F32)
        forward_layer(
            buf, width, left_factor(matrix), left_factor((scale * factor * matrix).T), bias, scale * spread
        )

    @pl.when(own > 0)
    def _():
        buf[:, LANES : LANES + width] = point_ref[...]
        coarse(matrix_of(p_ref, 0), bias_of(p_ref, 0), count)
        whole[...] = second_ref[...] - inner(buf)

    @pl.when(own == 0)
    def _():
        coarse(p2_ref[:, 0:rows], p2_ref[:, rows : rows + 1], length_of(p_ref, 2))
        whole[...] = inner(buf)

    size = plan.rows * IMG
    bias = bias_of(p_ref, 0)
    for shift, msg in enumerate(msgs):
        host = lax.rem(own - shift + 2 * plan.items, plan.items)
        start = plan.window(jnp.minimum(host, plan.hosts - 1))
        msg[:, 0:size] = whole[:, lanes(start, plan.rows)]
        msg[:, size : size + rows] = matrix_of(p_ref, 0)
        msg[:, size + rows : size + rows + 1] = bias


def point_kernel(
    _, both_ref, before_ref, adj_ref, adj_after_ref, p_after_ref, t_after_hi, t_after_lo,
    point_ref, lam_ref, t_hi, t_lo, u_hi, u_lo, buf, wl, wt,
):
    own = lax.axis_index("depth")
    last = lax.axis_size("depth") - 1
    width = point_ref.shape[1]

    @pl.when(own < last)
    def _():
        count = length_of(p_after_ref, jnp.minimum(own + 1, last))
        spread, _ = prepare(p_after_ref, wl, wt)
        fill(buf, adj_after_ref[...])
        run_backward(buf, width, wl, wt, spread, count, (t_after_hi, t_after_lo))
        lam_ref[...] = inner(buf)

    @pl.when(own == last)
    def _():
        lam_ref[...] = adj_ref[...]

    @pl.when(own > 0)
    def _():
        p_before_ref = before_ref.at[:, width:]
        count = length_of(p_before_ref, jnp.maximum(own - 1, 0))
        spread, _ = prepare(p_before_ref, wl, wt)
        fill(buf, before_ref[:, 0:width])
        run_forward(buf, width, p_before_ref, wl, wt, spread, count)
        point_ref[...] = inner(buf)

    @pl.when(own == 0)
    def _():
        point_ref[...] = both_ref[:, 0:width]
        fill(buf, both_ref[:, 0:width])

    p_ref = both_ref.at[:, width:]
    spread, _ = prepare(p_ref, wl, wt)
    run_forward(
        buf, width, p_ref, wl, wt, spread, length_of(p_ref, own), (t_hi, t_lo), (u_hi, u_lo)
    )


def adjoint_kernel(
    _, lam_end_ref, p_ref, t_hi, t_lo, u_hi, u_lo, adj_out_ref, g_ref, buf, wl, wt, lam_ref, q_ref, g_all
):
    rows, width = adj_out_ref.shape
    g_all[...] = jnp.zeros_like(g_all)
    fill(buf, lam_end_ref[...])
    spread, factor = prepare(p_ref, wl, wt)
    run_backward(
        buf, width, wl, wt, spread, length_of(p_ref, lax.axis_index("depth")), (t_hi, t_lo), (u_hi, u_lo),
        (g_all, factor, lam_ref, q_ref),
    )
    adj_out_ref[...] = inner(buf)
    most = g_all.shape[0]
    g_ref[:, most * rows :] = jnp.zeros((rows, LANES), F32)
    for slot in range(most):
        g_ref[:, slot * rows : (slot + 1) * rows] = g_all[slot, :, 0:rows]
        g_ref[:, most * rows + slot : most * rows + slot + 1] = g_all[slot, :, rows : rows + 1]


def sum_kernel(*refs):
    parts, (gw_ref, gb_ref) = refs[:-2], refs[-2:]
    most, rows, _ = gw_ref.shape
    total = sum(part[...] for part in parts)
    for slot in range(most):
        gw_ref[slot] = total[:, slot * rows : (slot + 1) * rows]
    gb_ref[...] = total[:, most * rows :].T[:most, :]


def chain_kernel(plan, _, second_ref, p_ref, *rest):
    msgs, rest = rest[: plan.items], rest[plan.items :]
    outs, (buf, held, done, wl, wt, sem) = rest[: plan.results], rest[plan.results :]
    own = lax.axis_index("depth")
    host = own - plan.first
    rows = held.shape[1]
    size = plan.rows * IMG
    piece = plan.block * IMG

    @pl.when(jnp.logical_and(host >= 0, host < plan.hosts))
    def _():
        copies = [
            pltpu.make_async_copy(msg, held.at[lax.rem(host + shift, plan.items)], sem.at[shift])
            for shift, msg in enumerate(msgs)
        ]
        for copy in copies:
            copy.start()
        for copy in copies:
            copy.wait()
        offset = host * plan.block - plan.window(host)
        most = slots_of(p_ref)
        spread = table_of(p_ref)[:, most : most + 1] * (1.0 / most)
        for item in range(2, plan.items):
            matrix = held[item, :, size : size + rows]
            scale = length_of(p_ref, item + 1).astype(F32) * (1.0 / most)
            wl[item] = left_factor(matrix)
            wt[item] = left_factor((scale * matrix).T)
        fill(buf, held[0, :, 0:size] + held[1, :, 0:size])

        def keep(result):
            done[result] = buf[:, pl.ds(pl.multiple_of(LANES + offset * IMG, LANES), piece)]

        keep(0)

        @pl.loop(2, plan.items)
        def _(item):
            forward_layer(
                buf, size, wl[item], wt[item], held[item, :, size + rows : size + rows + 1],
                length_of(p_ref, item + 1).astype(F32) * spread,
            )
            buf[:, LANES : LANES + size] = inner(buf) + held[item, :, 0:size]
            keep(item - 1)

        for shift, out in enumerate(outs):
            out[...] = done[lax.rem(host + shift, plan.results)]

    @pl.when(own == 0)
    def _():
        for shift, out in enumerate(outs):
            if shift < plan.hosts:
                out[...] = second_ref[:, shift * piece : (shift + 1) * piece]


def collect_kernel(plan, point_ref, local_ref, *rest):
    received, out_ref = rest[:-1], rest[-1]
    own = lax.axis_index("depth")
    host = own - plan.first

    @pl.when(own < 2)
    def _():
        out_ref[...] = point_ref[...]

    @pl.when(own == 2)
    def _():
        for shift, block in enumerate(received):
            if shift < plan.hosts:
                out_ref[:, lanes(shift * plan.block, plan.block)] = block[...]

    for shift, block in enumerate(received):
        sender = lax.rem(own - 3 - shift + 2 * plan.results, plan.results)

        @pl.when(jnp.logical_and(own > 2, jnp.logical_and(sender < plan.hosts, sender != host)))
        def _():
            out_ref[:, lanes(sender * plan.block, plan.block)] = block[...]

    @pl.when(jnp.logical_and(own > 2, jnp.logical_and(host >= 0, host < plan.hosts)))
    def _():
        out_ref[:, lanes(host * plan.block, plan.block)] = local_ref[...]


SMEM = pl.BlockSpec(memory_space=pltpu.SMEM)
VMEM = pl.BlockSpec(memory_space=pltpu.VMEM)
ANY = pl.BlockSpec(memory_space=pl.ANY)


def call(kernel, out_shape, in_specs, scratch, micros, name, mebi=32):
    return pl.pallas_call(
        kernel,
        out_shape=out_shape,
        in_specs=in_specs,
        out_specs=jax.tree.map(lambda _: VMEM, out_shape),
        scratch_shapes=scratch,
        compiler_params=pltpu.CompilerParams(vmem_limit_bytes=mebi * 2**20),
        cost_estimate=pl.CostEstimate(flops=int(micros * 1e8), bytes_accessed=2**21, transcendentals=0),
        name=name,
    )


def shifted(value, steps):
    count = lax.axis_size("depth")
    first, end = max(0, -steps), min(count, count - steps)
    return lax.ppermute(value, "depth", [(s, s + steps) for s in range(first, end)])


def others(value, step):
    count = lax.axis_size("batch")
    xor = count & (count - 1) == 0
    return lax.ppermute(value, "batch", [(s, s ^ step if xor else (s + step) % count) for s in range(count)])


def body(cpoint_guess, adjoint_guess, weights, biases, diffusion, section_len):
    plan = Plan(lax.axis_size("depth"))
    most, rows, _ = weights.shape
    width = cpoint_guess.shape[-1]
    guess, adjoint = cpoint_guess[0, 0], adjoint_guess[0, 0]

    def shape(*dims):
        return jax.ShapeDtypeStruct(dims, F32)

    state = shape(rows, width)
    buffer = pltpu.VMEM((rows, width + 2 * LANES), F32)
    factors = [pltpu.VMEM((most, rows, 3 * rows), BF16)] * 2

    wide = most * rows + LANES
    packed, packed0, both = call(
        pack_kernel, [shape(rows, wide), shape(rows, LANES), shape(rows, width + wide)], [ANY] * 5,
        [
            pltpu.VMEM(weights.shape, F32), pltpu.VMEM(biases.shape, F32), pltpu.VMEM((1, rows), F32),
            pltpu.VMEM((1, plan.count), jnp.int32), pltpu.SemaphoreType.DMA((5,)),
        ],
        1, "pack", 60,
    )(weights, biases, diffusion[None], section_len[None], guess)
    packed_after = shifted(packed, -1)
    packed_second = lax.ppermute(packed0, "depth", [(2, 0)])
    before = shifted(both, 1)
    after = call(push_kernel, state, [VMEM], [buffer, *factors], 40, "push")(both)
    after, packed_after, packed_second, adjoint_later = lax.optimization_barrier(
        (after, packed_after, packed_second, adjoint)
    )
    adj_after = shifted(adjoint_later, -1)

    saved = jax.ShapeDtypeStruct((most, rows, width), BF16)
    window = shape(rows, plan.rows * IMG + LANES)
    second, t_after_hi, t_after_lo, *msgs = call(
        functools.partial(tau_kernel, plan), [state, saved, saved] + [window] * plan.items,
        [VMEM] * 3, [buffer, *factors, pltpu.VMEM((rows, width), F32)], 3, "tau",
    )(after, packed_after, packed_second)
    arrived = {plan.first: msgs[plan.first]}
    order = plan.in_order()
    for k, shift in enumerate(order):
        msg = msgs[shift]
        if k >= AT_ONCE:
            msg, _ = lax.optimization_barrier((msg, arrived[order[k - AT_ONCE]]))
        arrived[shift] = lax.ppermute(msg, "depth", plan.in_pairs(shift))
    msgs = [arrived[shift] for shift in range(plan.items)]

    point, lam, *kept = call(
        point_kernel, [state] * 2 + [saved] * 4, [ANY] + [VMEM] * 7, [buffer, *factors], 6, "point"
    )(msgs[plan.first], both, before, adjoint, adj_after, packed_after, t_after_hi, t_after_lo)

    piece = shape(rows, plan.block * IMG)
    blocks = call(
        functools.partial(chain_kernel, plan), [piece] * plan.results,
        [ANY, VMEM, VMEM] + [ANY] * plan.items,
        [
            pltpu.VMEM((rows, plan.rows * IMG + 2 * LANES), F32),
            pltpu.VMEM((plan.items, *window.shape), F32),
            pltpu.VMEM((plan.results, *piece.shape), F32),
            pltpu.VMEM((plan.items, rows, 3 * rows), BF16),
            pltpu.VMEM((plan.items, rows, 3 * rows), BF16),
            pltpu.SemaphoreType.DMA((plan.items,)),
        ],
        1, "chain",
    )(lam, second, packed, *msgs)
    received = [lax.ppermute(block, "depth", plan.out_pairs(k)) for k, block in enumerate(blocks)]

    pair = pltpu.VMEM((2 * rows, width), BF16)
    adjoint_out, grads = call(
        adjoint_kernel, [state, shape(rows, wide)], [ANY] + [VMEM] * 6,
        [buffer, *factors, pair, pair, pltpu.VMEM((most, rows, rows + 1), F32)], 10, "adjoint",
    )(blocks[plan.local], lam, packed, *kept)

    states = call(
        functools.partial(collect_kernel, plan), state, [VMEM] * (2 + plan.results), [], 0.5, "collect"
    )(point, blocks[plan.local], *received)
    grads, *_ = lax.optimization_barrier((grads, *received))
    parts = [grads] + [others(grads, step) for step in range(1, lax.axis_size("batch"))]
    gw, gb = call(
        sum_kernel, [shape(*weights.shape), shape(*biases.shape)], [VMEM] * len(parts), [], 0.5, "sum"
    )(*parts)
    return states[None, None], adjoint_out[None, None], gw, gb


def solution(mesh):
    state = P("depth", "batch", None, None)
    return jax.shard_map(
        body,
        mesh=mesh,
        in_specs=(state, state, P("depth", None, None), P("depth", None), P(), P()),
        out_specs=(state, state, P("depth", None, None), P("depth", None)),
        check_vma=False,
    )
```

```python
import functools

import jax
import jax.numpy as jnp
from jax import lax
from jax.experimental import pallas as pl
from jax.experimental.pallas import tpu as pltpu
from jax.sharding import PartitionSpec as P

IMG = 64
LANES = 128
CHUNK = 256
AT_ONCE = 4
F32 = jnp.float32
BF16 = jnp.bfloat16


def split(x):
    hi = x.astype(BF16)
    lo = (x - hi.astype(F32)).astype(BF16)
    return hi, lo


def stack3(hi, lo):
    return jnp.concatenate([hi, lo, hi], axis=0)


def left_factor(matrix):
    hi = matrix.astype(BF16).astype(F32)
    return jnp.concatenate([hi, hi, matrix - hi], axis=1).astype(BF16)


def mm(a, b):
    return jnp.dot(a, b, preferred_element_type=F32)


def mm_nt(a, b):
    return lax.dot_general(a, b, (((1,), (1,)), ((), ())), preferred_element_type=F32)


def lane_masks(rows):
    lane = lax.broadcasted_iota(jnp.int32, (rows, LANES), 1)
    col = lane % IMG
    return col > 0, col < IMG - 1, lane < IMG


def swap(piece):
    return pltpu.roll(piece, IMG, 1)


def pieces_of(x):
    return [x[:, k : k + LANES] for k in range(0, x.shape[1], LANES)]


def to_pairs(x):
    pieces = pieces_of(x)
    half = len(pieces) // 2
    lower = lane_masks(x.shape[0])[2]
    out = []
    for k in range(half):
        out.append(jnp.where(lower, pieces[k], swap(pieces[k + half])))
        out.append(jnp.where(lower, swap(pieces[k]), pieces[k + half]))
    return jnp.concatenate(out, axis=1)


def from_pairs(x):
    pieces = pieces_of(x)
    half = len(pieces) // 2
    lower = lane_masks(x.shape[0])[2]
    first = [jnp.where(lower, pieces[2 * k], swap(pieces[2 * k + 1])) for k in range(half)]
    second = [jnp.where(lower, swap(pieces[2 * k]), pieces[2 * k + 1]) for k in range(half)]
    return jnp.concatenate(first + second, axis=1)


def neighbours(left, mid, right, masks, paired):
    not_first, not_last, lower = masks
    pieces = [left] + pieces_of(mid) + [right]
    swapped = None if paired else [swap(piece) for piece in pieces]
    sums = []
    for k in range(1, len(pieces) - 1):
        piece = pieces[k]
        beside = jnp.where(not_first, pltpu.roll(piece, 1, 1), 0.0)
        beside += jnp.where(not_last, pltpu.roll(piece, LANES - 1, 1), 0.0)
        if paired:
            beside += pieces[k - 1] + pieces[k + 1]
        else:
            beside += swapped[k] + jnp.where(lower, swapped[k - 1], swapped[k + 1])
        sums.append(beside)
    return jnp.concatenate(sums, axis=1)


def sweep(buf, width, step, paired):
    rows = buf.shape[0]
    masks = lane_masks(rows)
    if paired:
        lower = masks[2]
        before = jnp.where(lower, 0.0, swap(buf[:, width : width + LANES]))
        buf[:, width + LANES :] = jnp.where(lower, swap(buf[:, LANES : 2 * LANES]), 0.0)
    else:
        before = buf[:, 0:LANES]
    for start in range(0, width, CHUNK):
        size = min(CHUNK, width - start)
        at = LANES + start
        mid = buf[:, at : at + size]
        after = buf[:, at + size : at + size + LANES]
        around = neighbours(before, mid, after, masks, paired)
        before = mid[:, size - LANES :]
        buf[:, at : at + size] = step(start, size, mid, around)


def matrix_of(p_ref, slot):
    rows = p_ref.shape[0]
    return p_ref[:, slot * rows : (slot + 1) * rows]


def table_of(p_ref):
    return p_ref[:, p_ref.shape[1] - LANES :]


def bias_of(p_ref, slot):
    table = table_of(p_ref)
    pick = lax.broadcasted_iota(jnp.int32, table.shape, 1) == slot
    return jnp.sum(jnp.where(pick, table, 0.0), axis=1, keepdims=True)


def slots_of(p_ref):
    rows, width = p_ref.shape
    return (width - LANES) // rows


def prepare(p_ref, wl_ref, wt_ref):
    most = slots_of(p_ref)
    factor = 1.0 / most
    for slot in range(most):
        matrix = matrix_of(p_ref, slot)
        wl_ref[slot] = left_factor(matrix)
        wt_ref[slot] = left_factor((factor * matrix).T)
    return factor * table_of(p_ref)[:, most : most + 1], factor


def column(row):
    n = row.shape[1]
    same = lax.broadcasted_iota(jnp.int32, (n, n), 0) == lax.broadcasted_iota(jnp.int32, (n, n), 1)
    return jnp.sum(jnp.where(same, row, 0.0), axis=1, keepdims=True)


def length_of(p_ref, section):
    row = table_of(p_ref)[0:1, :]
    pick = lax.broadcasted_iota(jnp.int32, row.shape, 1) == slots_of(p_ref) + 1 + section
    return jnp.sum(jnp.where(pick, row, 0.0)).astype(jnp.int32)


def pack_kernel(
    w_any, b_any, diff_any, len_any, guess_any, p_ref, p0_ref, both_ref, w_ref, b_ref, diff_ref, len_ref, sem
):
    most, rows, _ = w_ref.shape
    width = guess_any.shape[1]
    copies = [
        pltpu.make_async_copy(source, target, sem.at[k])
        for k, (source, target) in enumerate(
            [(w_any, w_ref), (b_any, b_ref), (diff_any, diff_ref), (len_any, len_ref),
             (guess_any, both_ref.at[:, 0:width])]
        )
    ]
    for copy in copies:
        copy.start()
    for copy in copies[:-1]:
        copy.wait()
    wide = most * rows
    p_ref[:, wide:] = jnp.zeros((rows, LANES), F32)
    for slot in range(most):
        p_ref[:, slot * rows : (slot + 1) * rows] = w_ref[slot]
        p_ref[:, wide + slot : wide + slot + 1] = column(b_ref[slot : slot + 1, :])
    p_ref[:, wide + most : wide + most + 1] = column(diff_ref[...])
    lengths = len_ref[...].astype(F32)
    first = wide + most + 1
    p_ref[:, first : first + lengths.shape[1]] = jnp.broadcast_to(lengths, (rows, lengths.shape[1]))
    p0_ref[...] = jnp.zeros_like(p0_ref)
    p0_ref[:, 0:rows] = w_ref[0]
    p0_ref[:, rows : rows + 1] = column(b_ref[0:1, :])
    both_ref[:, width:] = p_ref[...]
    copies[-1].wait()


def forward_layer(buf, width, wl, wt, bias, spread, t_out=None, u_out=None, paired=True):
    keep = 1.0 - 4.0 * spread

    def step(start, size, mid, around):
        hi, lo = split(mid)
        t_hi, t_lo = split(jnp.tanh(mm(wl, stack3(hi, lo)) + bias))
        if t_out is not None:
            t_out(start, size, t_hi, t_lo)
        if u_out is not None:
            u_out(start, size, hi, lo)
        return mid * keep + around * spread - mm(wt, stack3(t_hi, t_lo))

    sweep(buf, width, step, paired)


def run_forward(buf, width, p_ref, wl_ref, wt_ref, spread, count, t_refs=None, u_refs=None):
    def saver(refs, slot):
        if refs is None:
            return None

        def save(start, size, hi, lo):
            refs[0][slot, :, start : start + size] = hi
            refs[1][slot, :, start : start + size] = lo

        return save

    @pl.loop(0, count)
    def _(slot):
        forward_layer(
            buf, width, wl_ref[slot], wt_ref[slot], bias_of(p_ref, slot), spread,
            saver(t_refs, slot), saver(u_refs, slot),
        )


def run_backward(buf, width, wl_ref, wt_ref, spread, count, t_refs, u_refs=None, grads=None):
    keep = 1.0 - 4.0 * spread

    @pl.loop(0, count)
    def _(passed):
        slot = count - 1 - passed
        wl, wt = wl_ref[slot], wt_ref[slot]
        rows = buf.shape[0]
        sums = []

        def step(start, size, mid, around):
            span = slice(start, start + size)
            hi, lo = split(mid)
            t = t_refs[0][slot, :, span].astype(F32) + t_refs[1][slot, :, span].astype(F32)
            q = (1.0 - t * t) * mm(wl, stack3(hi, lo))
            q_hi, q_lo = split(q)
            if grads is not None:
                _, _, lam_ref, q_ref = grads
                lam_ref[0:rows, span], lam_ref[rows:, span] = hi, lo
                q_ref[0:rows, span], q_ref[rows:, span] = q_hi, q_lo
                sums.append(sum(q[:, k : k + LANES] for k in range(0, size, LANES)))
            return mid * keep + around * spread - mm(wt, stack3(q_hi, q_lo))

        sweep(buf, width, step, True)
        if grads is not None:
            g_ref, factor, lam_ref, q_ref = grads

            def product(left, right):
                g = mm_nt(left, right)
                return g[:rows, :rows] + g[:rows, rows:] + g[rows:, :rows]

            gw = product(jnp.concatenate([ref[slot] for ref in t_refs], axis=0), lam_ref[...])
            gw += product(q_ref[...], jnp.concatenate([ref[slot] for ref in u_refs], axis=0))
            g_ref[slot, :, 0:rows] = -factor * gw
            g_ref[slot, :, rows : rows + 1] = -factor * jnp.sum(sum(sums), axis=1, keepdims=True)


def fill(buf, value):
    rows, width = value.shape
    zero = jnp.zeros((rows, LANES), F32)
    buf[:, 0:LANES] = zero
    buf[:, LANES + width :] = zero
    buf[:, LANES : LANES + width] = value


def inner(buf):
    return buf[:, LANES : buf.shape[1] - LANES]


class Plan:
    def __init__(self, count):
        self.count = count
        self.items = count - 2
        self.hosts = count // 2
        self.first = count // 4
        self.block = IMG // self.hosts
        self.rows = min(IMG, self.block + 2 * (count - 4))
        self.rows += self.rows % 2
        self.results = count - 3
        self.local = (self.first - 3) % self.results

    def window(self, host):
        start = host * self.block - (self.count - 4)
        return jnp.clip(start - start % 2, 0, IMG - self.rows)

    def in_pairs(self, shift):
        return [((h + shift) % self.items, h + self.first) for h in range(self.hosts)]

    def out_pairs(self, shift):
        pairs = [(h + self.first, 3 + (h + shift) % self.results) for h in range(self.hosts)]
        pairs = [(s, d) for s, d in pairs if s != d]
        return pairs + ([(0, 2)] if shift < self.hosts else [])


def lanes(row, size):
    return pl.ds(pl.multiple_of(row * IMG, LANES), size * IMG)


def push_kernel(both_ref, out_ref, buf, wl, wt):
    width = out_ref.shape[1]
    p_ref = both_ref.at[:, width:]
    spread, _ = prepare(p_ref, wl, wt)
    fill(buf, to_pairs(both_ref[:, 0:width]))
    run_forward(buf, width, p_ref, wl, wt, spread, length_of(p_ref, lax.axis_index("depth")))
    out_ref[...] = inner(buf)


def tau_kernel(plan, point_ref, p_ref, p2_ref, second_ref, *rest):
    msgs, (buf, wl, wt, whole) = rest[:-4], rest[-4:]
    rows, width = point_ref.shape
    own = lax.axis_index("depth")
    count = length_of(p_ref, jnp.minimum(own + 1, plan.count - 1))
    spread, factor = prepare(p_ref, wl, wt)
    fill(buf, point_ref[...])
    run_forward(buf, width, p_ref, wl, wt, spread, count)
    whole[...] = inner(buf)

    def coarse(matrix, bias, length):
        scale = length.astype(F32)
        forward_layer(
            buf, width, left_factor(matrix), left_factor((scale * factor * matrix).T), bias, scale * spread
        )

    @pl.when(own > 0)
    def _():
        buf[:, LANES : LANES + width] = point_ref[...]
        coarse(matrix_of(p_ref, 0), bias_of(p_ref, 0), count)
        whole[...] = from_pairs(whole[...] - inner(buf))

    @pl.when(own == 0)
    def _():
        second_ref[...] = from_pairs(whole[...])
        coarse(p2_ref[:, 0:rows], p2_ref[:, rows : rows + 1], length_of(p_ref, 2))
        whole[...] = from_pairs(inner(buf))

    size = plan.rows * IMG
    bias = bias_of(p_ref, 0)
    for shift, msg in enumerate(msgs):
        host = lax.rem(own - shift + 2 * plan.items, plan.items)
        start = plan.window(jnp.minimum(host, plan.hosts - 1))
        msg[:, 0:size] = whole[:, lanes(start, plan.rows)]
        msg[:, size : size + rows] = matrix_of(p_ref, 0)
        msg[:, size + rows : size + rows + 1] = bias


def point_kernel(_, both_ref, before_ref, adj_ref, point_ref, lam_ref, t_hi, t_lo, u_hi, u_lo, buf, wl, wt):
    own = lax.axis_index("depth")
    width = point_ref.shape[1]

    @pl.when(own > 0)
    def _():
        p_before_ref = before_ref.at[:, width:]
        count = length_of(p_before_ref, jnp.maximum(own - 1, 0))
        spread, _ = prepare(p_before_ref, wl, wt)
        fill(buf, to_pairs(before_ref[:, 0:width]))
        run_forward(buf, width, p_before_ref, wl, wt, spread, count)

    @pl.when(own == 1)
    def _():
        point_ref[...] = from_pairs(inner(buf))

    @pl.when(own == 0)
    def _():
        point_ref[...] = both_ref[:, 0:width]
        fill(buf, to_pairs(both_ref[:, 0:width]))

    p_ref = both_ref.at[:, width:]
    count = length_of(p_ref, own)
    spread, _ = prepare(p_ref, wl, wt)
    run_forward(buf, width, p_ref, wl, wt, spread, count, (t_hi, t_lo), (u_hi, u_lo))

    @pl.when(own > 0)
    def _():
        fill(buf, to_pairs(adj_ref[...]))
        run_backward(buf, width, wl, wt, spread, count, (t_hi, t_lo))
        lam_ref[...] = inner(buf)


def adjoint_kernel(
    _, adj_ref, lam_after_ref, p_ref, t_hi, t_lo, u_hi, u_lo, adj_out_ref, g_ref, buf, wl, wt, lam_ref, q_ref, g_all
):
    own = lax.axis_index("depth")
    last = lax.axis_size("depth") - 1
    rows, width = adj_out_ref.shape
    g_all[...] = jnp.zeros_like(g_all)

    @pl.when(own < last)
    def _():
        fill(buf, lam_after_ref[...])

    @pl.when(own == last)
    def _():
        fill(buf, to_pairs(adj_ref[...]))

    spread, factor = prepare(p_ref, wl, wt)
    run_backward(
        buf, width, wl, wt, spread, length_of(p_ref, own), (t_hi, t_lo), (u_hi, u_lo),
        (g_all, factor, lam_ref, q_ref),
    )
    adj_out_ref[...] = from_pairs(inner(buf))
    most = g_all.shape[0]
    g_ref[:, most * rows :] = jnp.zeros((rows, LANES), F32)
    for slot in range(most):
        g_ref[:, slot * rows : (slot + 1) * rows] = g_all[slot, :, 0:rows]
        g_ref[:, most * rows + slot : most * rows + slot + 1] = g_all[slot, :, rows : rows + 1]


def sum_kernel(*refs):
    parts, (gw_ref, gb_ref) = refs[:-2], refs[-2:]
    most, rows, _ = gw_ref.shape
    total = sum(part[...] for part in parts)
    for slot in range(most):
        gw_ref[slot] = total[:, slot * rows : (slot + 1) * rows]
    gb_ref[...] = total[:, most * rows :].T[:most, :]


def chain_kernel(plan, _, second_ref, p_ref, *rest):
    msgs, rest = rest[: plan.items], rest[plan.items :]
    outs, (buf, held, done, wl, wt, sem) = rest[: plan.results], rest[plan.results :]
    own = lax.axis_index("depth")
    host = own - plan.first
    rows = held.shape[1]
    size = plan.rows * IMG
    piece = plan.block * IMG

    @pl.when(jnp.logical_and(host >= 0, host < plan.hosts))
    def _():
        copies = [
            pltpu.make_async_copy(msg, held.at[lax.rem(host + shift, plan.items)], sem.at[shift])
            for shift, msg in enumerate(msgs)
        ]
        for copy in copies:
            copy.start()
        for copy in copies:
            copy.wait()
        offset = host * plan.block - plan.window(host)
        most = slots_of(p_ref)
        spread = table_of(p_ref)[:, most : most + 1] * (1.0 / most)
        for item in range(2, plan.items):
            matrix = held[item, :, size : size + rows]
            scale = length_of(p_ref, item + 1).astype(F32) * (1.0 / most)
            wl[item] = left_factor(matrix)
            wt[item] = left_factor((scale * matrix).T)
        fill(buf, held[0, :, 0:size] + held[1, :, 0:size])

        def keep(result):
            done[result] = buf[:, pl.ds(pl.multiple_of(LANES + offset * IMG, LANES), piece)]

        keep(0)

        @pl.loop(2, plan.items)
        def _(item):
            forward_layer(
                buf, size, wl[item], wt[item], held[item, :, size + rows : size + rows + 1],
                length_of(p_ref, item + 1).astype(F32) * spread, paired=False,
            )
            buf[:, LANES : LANES + size] = inner(buf) + held[item, :, 0:size]
            keep(item - 1)

        for shift, out in enumerate(outs):
            out[...] = done[lax.rem(host + shift, plan.results)]

    @pl.when(own == 0)
    def _():
        for shift, out in enumerate(outs):
            if shift < plan.hosts:
                out[...] = second_ref[:, shift * piece : (shift + 1) * piece]


def collect_kernel(plan, point_ref, local_ref, *rest):
    received, out_ref = rest[:-1], rest[-1]
    own = lax.axis_index("depth")
    host = own - plan.first

    @pl.when(own < 2)
    def _():
        out_ref[...] = point_ref[...]

    @pl.when(own == 2)
    def _():
        for shift, block in enumerate(received):
            if shift < plan.hosts:
                out_ref[:, lanes(shift * plan.block, plan.block)] = block[...]

    for shift, block in enumerate(received):
        sender = lax.rem(own - 3 - shift + 2 * plan.results, plan.results)

        @pl.when(jnp.logical_and(own > 2, jnp.logical_and(sender < plan.hosts, sender != host)))
        def _():
            out_ref[:, lanes(sender * plan.block, plan.block)] = block[...]

    @pl.when(jnp.logical_and(own > 2, jnp.logical_and(host >= 0, host < plan.hosts)))
    def _():
        out_ref[:, lanes(host * plan.block, plan.block)] = local_ref[...]


SMEM = pl.BlockSpec(memory_space=pltpu.SMEM)
VMEM = pl.BlockSpec(memory_space=pltpu.VMEM)
ANY = pl.BlockSpec(memory_space=pl.ANY)


def call(kernel, out_shape, in_specs, scratch, micros, name, mebi=32):
    return pl.pallas_call(
        kernel,
        out_shape=out_shape,
        in_specs=in_specs,
        out_specs=jax.tree.map(lambda _: VMEM, out_shape),
        scratch_shapes=scratch,
        compiler_params=pltpu.CompilerParams(vmem_limit_bytes=mebi * 2**20),
        cost_estimate=pl.CostEstimate(flops=int(micros * 1e8), bytes_accessed=2**21, transcendentals=0),
        name=name,
    )


def shifted(value, steps):
    count = lax.axis_size("depth")
    first, end = max(0, -steps), min(count, count - steps)
    return lax.ppermute(value, "depth", [(s, s + steps) for s in range(first, end)])


def others(value, step):
    count = lax.axis_size("batch")
    xor = count & (count - 1) == 0
    return lax.ppermute(value, "batch", [(s, s ^ step if xor else (s + step) % count) for s in range(count)])


def body(cpoint_guess, adjoint_guess, weights, biases, diffusion, section_len):
    plan = Plan(lax.axis_size("depth"))
    most, rows, _ = weights.shape
    width = cpoint_guess.shape[-1]
    guess, adjoint = cpoint_guess[0, 0], adjoint_guess[0, 0]

    def shape(*dims):
        return jax.ShapeDtypeStruct(dims, F32)

    state = shape(rows, width)
    buffer = pltpu.VMEM((rows, width + 2 * LANES), F32)
    factors = [pltpu.VMEM((most, rows, 3 * rows), BF16)] * 2

    wide = most * rows + LANES
    packed, packed0, both = call(
        pack_kernel, [shape(rows, wide), shape(rows, LANES), shape(rows, width + wide)], [ANY] * 5,
        [
            pltpu.VMEM(weights.shape, F32), pltpu.VMEM(biases.shape, F32), pltpu.VMEM((1, rows), F32),
            pltpu.VMEM((1, plan.count), jnp.int32), pltpu.SemaphoreType.DMA((5,)),
        ],
        1, "pack", 60,
    )(weights, biases, diffusion[None], section_len[None], guess)
    packed_after = shifted(packed, -1)
    packed_second = lax.ppermute(packed0, "depth", [(2, 0)])
    before = shifted(both, 1)
    after = call(push_kernel, state, [VMEM], [buffer, *factors], 40, "push")(both)
    after, packed_after, packed_second = lax.optimization_barrier((after, packed_after, packed_second))

    saved = jax.ShapeDtypeStruct((most, rows, width), BF16)
    window = shape(rows, plan.rows * IMG + LANES)
    second, *msgs = call(
        functools.partial(tau_kernel, plan), [state] + [window] * plan.items,
        [VMEM] * 3, [buffer, *factors, pltpu.VMEM((rows, width), F32)], 3, "tau",
    )(after, packed_after, packed_second)
    arrived = {plan.first: msgs[plan.first]}
    order = [shift for shift in range(plan.items) if shift != plan.first]
    for k, shift in enumerate(order):
        msg = msgs[shift]
        if k >= AT_ONCE:
            msg, _ = lax.optimization_barrier((msg, arrived[order[k - AT_ONCE]]))
        arrived[shift] = lax.ppermute(msg, "depth", plan.in_pairs(shift))
    msgs = [arrived[shift] for shift in range(plan.items)]

    point, lam, *kept = call(
        point_kernel, [state] * 2 + [saved] * 4, [ANY] + [VMEM] * 3, [buffer, *factors], 6, "point"
    )(msgs[plan.first], both, before, adjoint)
    lam_after = shifted(lam, -1)

    piece = shape(rows, plan.block * IMG)
    blocks = call(
        functools.partial(chain_kernel, plan), [piece] * plan.results,
        [ANY, VMEM, VMEM] + [ANY] * plan.items,
        [
            pltpu.VMEM((rows, plan.rows * IMG + 2 * LANES), F32),
            pltpu.VMEM((plan.items, *window.shape), F32),
            pltpu.VMEM((plan.results, *piece.shape), F32),
            pltpu.VMEM((plan.items, rows, 3 * rows), BF16),
            pltpu.VMEM((plan.items, rows, 3 * rows), BF16),
            pltpu.SemaphoreType.DMA((plan.items,)),
        ],
        40, "chain",
    )(lam, second, packed, *msgs)
    received = [lax.ppermute(block, "depth", plan.out_pairs(k)) for k, block in enumerate(blocks)]

    pair = pltpu.VMEM((2 * rows, width), BF16)
    adjoint_out, grads = call(
        adjoint_kernel, [state, shape(rows, wide)], [ANY] + [VMEM] * 7,
        [buffer, *factors, pair, pair, pltpu.VMEM((most, rows, rows + 1), F32)], 10, "adjoint",
    )(blocks[plan.local], adjoint, lam_after, packed, *kept)

    states = call(
        functools.partial(collect_kernel, plan), state, [VMEM] * (2 + plan.results), [], 0.5, "collect"
    )(point, blocks[plan.local], *received)
    grads, *_ = lax.optimization_barrier((grads, *received))
    parts = [grads] + [others(grads, step) for step in range(1, lax.axis_size("batch"))]
    gw, gb = call(
        sum_kernel, [shape(*weights.shape), shape(*biases.shape)], [VMEM] * len(parts), [], 0.5, "sum"
    )(*parts)
    return states[None, None], adjoint_out[None, None], gw, gb


def solution(mesh):
    state = P("depth", "batch", None, None)
    return jax.shard_map(
        body,
        mesh=mesh,
        in_specs=(state, state, P("depth", None, None), P("depth", None), P(), P()),
        out_specs=(state, state, P("depth", None, None), P("depth", None)),
        check_vma=False,
    )
```

```python
import functools

import jax
import jax.numpy as jnp
from jax import lax
from jax.experimental import pallas as pl
from jax.experimental.pallas import tpu as pltpu
from jax.sharding import PartitionSpec as P

IMG = 64
LANES = 128
CHUNK = 256
AT_ONCE = 4
F32 = jnp.float32
BF16 = jnp.bfloat16


def split(x):
    hi = x.astype(BF16)
    lo = (x - hi.astype(F32)).astype(BF16)
    return hi, lo


def stack3(hi, lo):
    return jnp.concatenate([hi, lo, hi], axis=0)


def left_factor(matrix):
    hi = matrix.astype(BF16).astype(F32)
    return jnp.concatenate([hi, hi, matrix - hi], axis=1).astype(BF16)


def mm(a, b):
    return jnp.dot(a, b, preferred_element_type=F32)


def mm_nt(a, b):
    return lax.dot_general(a, b, (((1,), (1,)), ((), ())), preferred_element_type=F32)


def lane_masks(rows):
    lane = lax.broadcasted_iota(jnp.int32, (rows, LANES), 1)
    col = lane % IMG
    return col > 0, col < IMG - 1, lane < IMG


def swap(piece):
    return pltpu.roll(piece, IMG, 1)


def pieces_of(x):
    return [x[:, k : k + LANES] for k in range(0, x.shape[1], LANES)]


def to_pairs(x):
    pieces = pieces_of(x)
    half = len(pieces) // 2
    lower = lane_masks(x.shape[0])[2]
    out = []
    for k in range(half):
        out.append(jnp.where(lower, pieces[k], swap(pieces[k + half])))
        out.append(jnp.where(lower, swap(pieces[k]), pieces[k + half]))
    return jnp.concatenate(out, axis=1)


def from_pairs(x):
    pieces = pieces_of(x)
    half = len(pieces) // 2
    lower = lane_masks(x.shape[0])[2]
    first = [jnp.where(lower, pieces[2 * k], swap(pieces[2 * k + 1])) for k in range(half)]
    second = [jnp.where(lower, swap(pieces[2 * k]), pieces[2 * k + 1]) for k in range(half)]
    return jnp.concatenate(first + second, axis=1)


def neighbours(left, mid, right, masks, paired):
    not_first, not_last, lower = masks
    pieces = [left] + pieces_of(mid) + [right]
    swapped = None if paired else [swap(piece) for piece in pieces]
    sums = []
    for k in range(1, len(pieces) - 1):
        piece = pieces[k]
        beside = jnp.where(not_first, pltpu.roll(piece, 1, 1), 0.0)
        beside += jnp.where(not_last, pltpu.roll(piece, LANES - 1, 1), 0.0)
        if paired:
            beside += pieces[k - 1] + pieces[k + 1]
        else:
            beside += swapped[k] + jnp.where(lower, swapped[k - 1], swapped[k + 1])
        sums.append(beside)
    return jnp.concatenate(sums, axis=1)


def sweep(buf, width, step, paired):
    rows = buf.shape[0]
    masks = lane_masks(rows)
    if paired:
        lower = masks[2]
        before = jnp.where(lower, 0.0, swap(buf[:, width : width + LANES]))
        buf[:, width + LANES :] = jnp.where(lower, swap(buf[:, LANES : 2 * LANES]), 0.0)
    else:
        before = buf[:, 0:LANES]
    for start in range(0, width, CHUNK):
        size = min(CHUNK, width - start)
        at = LANES + start
        mid = buf[:, at : at + size]
        after = buf[:, at + size : at + size + LANES]
        around = neighbours(before, mid, after, masks, paired)
        before = mid[:, size - LANES :]
        buf[:, at : at + size] = step(start, size, mid, around)


def matrix_of(p_ref, slot):
    rows = p_ref.shape[0]
    return p_ref[:, slot * rows : (slot + 1) * rows]


def table_of(p_ref):
    return p_ref[:, p_ref.shape[1] - LANES :]


def bias_of(p_ref, slot):
    table = table_of(p_ref)
    pick = lax.broadcasted_iota(jnp.int32, table.shape, 1) == slot
    return jnp.sum(jnp.where(pick, table, 0.0), axis=1, keepdims=True)


def slots_of(p_ref):
    rows, width = p_ref.shape
    return (width - LANES) // rows


def scales_of(p_ref):
    most = slots_of(p_ref)
    return (1.0 / most) * table_of(p_ref)[:, most : most + 1], 1.0 / most


def prepare(p_ref, wl_ref, wt_ref):
    spread, factor = scales_of(p_ref)
    for slot in range(slots_of(p_ref)):
        matrix = matrix_of(p_ref, slot)
        wl_ref[slot] = left_factor(matrix)
        wt_ref[slot] = left_factor((factor * matrix).T)
    return spread, factor


def column(row):
    n = row.shape[1]
    same = lax.broadcasted_iota(jnp.int32, (n, n), 0) == lax.broadcasted_iota(jnp.int32, (n, n), 1)
    return jnp.sum(jnp.where(same, row, 0.0), axis=1, keepdims=True)


def length_of(p_ref, section):
    row = table_of(p_ref)[0:1, :]
    pick = lax.broadcasted_iota(jnp.int32, row.shape, 1) == slots_of(p_ref) + 1 + section
    return jnp.sum(jnp.where(pick, row, 0.0)).astype(jnp.int32)


def pack_kernel(
    w_any, b_any, diff_any, len_any, guess_any, p_ref, p0_ref, both_ref, w_ref, b_ref, diff_ref, len_ref, sem
):
    most, rows, _ = w_ref.shape
    width = guess_any.shape[1]
    copies = [
        pltpu.make_async_copy(source, target, sem.at[k])
        for k, (source, target) in enumerate(
            [(w_any, w_ref), (b_any, b_ref), (diff_any, diff_ref), (len_any, len_ref),
             (guess_any, both_ref.at[:, 0:width])]
        )
    ]
    for copy in copies:
        copy.start()
    for copy in copies[:-1]:
        copy.wait()
    wide = most * rows
    p_ref[:, wide:] = jnp.zeros((rows, LANES), F32)
    for slot in range(most):
        p_ref[:, slot * rows : (slot + 1) * rows] = w_ref[slot]
        p_ref[:, wide + slot : wide + slot + 1] = column(b_ref[slot : slot + 1, :])
    p_ref[:, wide + most : wide + most + 1] = column(diff_ref[...])
    lengths = len_ref[...].astype(F32)
    first = wide + most + 1
    p_ref[:, first : first + lengths.shape[1]] = jnp.broadcast_to(lengths, (rows, lengths.shape[1]))
    p0_ref[...] = jnp.zeros_like(p0_ref)
    p0_ref[:, 0:rows] = w_ref[0]
    p0_ref[:, rows : rows + 1] = column(b_ref[0:1, :])
    both_ref[:, width:] = p_ref[...]
    copies[-1].wait()


def forward_layer(buf, width, wl, wt, bias, spread, t_out=None, u_out=None, paired=True):
    keep = 1.0 - 4.0 * spread

    def step(start, size, mid, around):
        hi, lo = split(mid)
        t_hi, t_lo = split(jnp.tanh(mm(wl, stack3(hi, lo)) + bias))
        if t_out is not None:
            t_out(start, size, t_hi, t_lo)
        if u_out is not None:
            u_out(start, size, hi, lo)
        return mid * keep + around * spread - mm(wt, stack3(t_hi, t_lo))

    sweep(buf, width, step, paired)


def run_forward(buf, width, p_ref, wl_ref, wt_ref, spread, count, t_refs=None, u_refs=None):
    def saver(refs, slot):
        if refs is None:
            return None

        def save(start, size, hi, lo):
            refs[0][slot, :, start : start + size] = hi
            refs[1][slot, :, start : start + size] = lo

        return save

    @pl.loop(0, count)
    def _(slot):
        forward_layer(
            buf, width, wl_ref[slot], wt_ref[slot], bias_of(p_ref, slot), spread,
            saver(t_refs, slot), saver(u_refs, slot),
        )


def run_backward(buf, width, wl_ref, wt_ref, spread, count, t_refs, u_refs=None, grads=None):
    keep = 1.0 - 4.0 * spread

    @pl.loop(0, count)
    def _(passed):
        slot = count - 1 - passed
        wl, wt = wl_ref[slot], wt_ref[slot]
        rows = buf.shape[0]
        sums = []

        def step(start, size, mid, around):
            span = slice(start, start + size)
            hi, lo = split(mid)
            t = t_refs[0][slot, :, span].astype(F32) + t_refs[1][slot, :, span].astype(F32)
            q = (1.0 - t * t) * mm(wl, stack3(hi, lo))
            q_hi, q_lo = split(q)
            if grads is not None:
                _, _, lam_ref, q_ref = grads
                lam_ref[0:rows, span], lam_ref[rows:, span] = hi, lo
                q_ref[0:rows, span], q_ref[rows:, span] = q_hi, q_lo
                sums.append(sum(q[:, k : k + LANES] for k in range(0, size, LANES)))
            return mid * keep + around * spread - mm(wt, stack3(q_hi, q_lo))

        sweep(buf, width, step, True)
        if grads is not None:
            g_ref, factor, lam_ref, q_ref = grads

            def product(left, right):
                g = mm_nt(left, right)
                return g[:rows, :rows] + g[:rows, rows:] + g[rows:, :rows]

            gw = product(jnp.concatenate([ref[slot] for ref in t_refs], axis=0), lam_ref[...])
            gw += product(q_ref[...], jnp.concatenate([ref[slot] for ref in u_refs], axis=0))
            g_ref[slot, :, 0:rows] = -factor * gw
            g_ref[slot, :, rows : rows + 1] = -factor * jnp.sum(sum(sums), axis=1, keepdims=True)


def fill(buf, value):
    rows, width = value.shape
    zero = jnp.zeros((rows, LANES), F32)
    buf[:, 0:LANES] = zero
    buf[:, LANES + width :] = zero
    buf[:, LANES : LANES + width] = value


def inner(buf):
    return buf[:, LANES : buf.shape[1] - LANES]


class Plan:
    def __init__(self, count):
        self.count = count
        self.items = count - 2
        self.hosts = count // 2
        self.first = count // 4
        self.block = IMG // self.hosts
        self.rows = min(IMG, self.block + 2 * (count - 4))
        self.rows += self.rows % 2
        self.results = count - 3
        self.local = (self.first - 3) % self.results

    def window(self, host):
        start = host * self.block - (self.count - 4)
        return jnp.clip(start - start % 2, 0, IMG - self.rows)

    def in_pairs(self, shift):
        return [((h + shift) % self.items, h + self.first) for h in range(self.hosts)]

    def out_pairs(self, shift):
        pairs = [(h + self.first, 3 + (h + shift) % self.results) for h in range(self.hosts)]
        pairs = [(s, d) for s, d in pairs if s != d]
        return pairs + ([(0, 2)] if shift < self.hosts else [])


def lanes(row, size):
    return pl.ds(pl.multiple_of(row * IMG, LANES), size * IMG)


def front_kernel(plan, both_ref, p_ref, p2_ref, second_ref, own_wl, own_wt, *rest):
    msgs, (buf, wl, wt, whole, start_state) = rest[:-5], rest[-5:]
    rows, width = second_ref.shape
    own = lax.axis_index("depth")
    own_p_ref = both_ref.at[:, width:]
    spread, factor = prepare(own_p_ref, own_wl, own_wt)
    fill(buf, to_pairs(both_ref[:, 0:width]))
    run_forward(buf, width, own_p_ref, own_wl, own_wt, spread, length_of(own_p_ref, own))
    start_state[...] = inner(buf)

    count = length_of(own_p_ref, jnp.minimum(own + 1, plan.count - 1))
    prepare(p_ref, wl, wt)
    run_forward(buf, width, p_ref, wl, wt, spread, count)
    whole[...] = inner(buf)

    def coarse(matrix, bias, length):
        scale = length.astype(F32)
        forward_layer(
            buf, width, left_factor(matrix), left_factor((scale * factor * matrix).T), bias, scale * spread
        )

    @pl.when(own > 0)
    def _():
        buf[:, LANES : LANES + width] = start_state[...]
        coarse(matrix_of(p_ref, 0), bias_of(p_ref, 0), count)
        whole[...] = from_pairs(whole[...] - inner(buf))

    @pl.when(own == 0)
    def _():
        second_ref[...] = from_pairs(whole[...])
        coarse(p2_ref[:, 0:rows], p2_ref[:, rows : rows + 1], length_of(own_p_ref, 2))
        whole[...] = from_pairs(inner(buf))

    size = plan.rows * IMG
    bias = bias_of(p_ref, 0)
    for shift, msg in enumerate(msgs):
        host = lax.rem(own - shift + 2 * plan.items, plan.items)
        start = plan.window(jnp.minimum(host, plan.hosts - 1))
        msg[...] = whole[:, lanes(start, plan.rows)]
        for at, here in ((size - IMG, start == 0), (0, start > 0)):

            @pl.when(jnp.logical_and(own > 1, here))
            def _():
                msg[:, at : at + rows] = matrix_of(p_ref, 0)
                msg[:, at + rows : at + rows + 1] = bias


def point_kernel(
    _, both_ref, before_ref, adj_ref, own_wl, own_wt, point_ref, lam_ref, t_hi, t_lo, u_hi, u_lo, buf, wl, wt
):
    own = lax.axis_index("depth")
    width = point_ref.shape[1]

    @pl.when(own > 0)
    def _():
        p_before_ref = before_ref.at[:, width:]
        count = length_of(p_before_ref, jnp.maximum(own - 1, 0))
        spread, _ = prepare(p_before_ref, wl, wt)
        fill(buf, to_pairs(before_ref[:, 0:width]))
        run_forward(buf, width, p_before_ref, wl, wt, spread, count)

    @pl.when(own == 1)
    def _():
        point_ref[...] = from_pairs(inner(buf))

    @pl.when(own == 0)
    def _():
        point_ref[...] = both_ref[:, 0:width]
        fill(buf, to_pairs(both_ref[:, 0:width]))

    p_ref = both_ref.at[:, width:]
    count = length_of(p_ref, own)
    spread, _ = scales_of(p_ref)
    run_forward(buf, width, p_ref, own_wl, own_wt, spread, count, (t_hi, t_lo), (u_hi, u_lo))

    @pl.when(own > 0)
    def _():
        fill(buf, to_pairs(adj_ref[...]))
        run_backward(buf, width, own_wl, own_wt, spread, count, (t_hi, t_lo))
        lam_ref[...] = inner(buf)


def adjoint_kernel(
    _, adj_ref, lam_after_ref, p_ref, wl, wt, t_hi, t_lo, u_hi, u_lo, adj_out_ref, g_ref, buf, lam_ref, q_ref, g_all
):
    own = lax.axis_index("depth")
    last = lax.axis_size("depth") - 1
    rows, width = adj_out_ref.shape
    g_all[...] = jnp.zeros_like(g_all)

    @pl.when(own < last)
    def _():
        fill(buf, lam_after_ref[...])

    @pl.when(own == last)
    def _():
        fill(buf, to_pairs(adj_ref[...]))

    spread, factor = scales_of(p_ref)
    run_backward(
        buf, width, wl, wt, spread, length_of(p_ref, own), (t_hi, t_lo), (u_hi, u_lo),
        (g_all, factor, lam_ref, q_ref),
    )
    adj_out_ref[...] = from_pairs(inner(buf))
    most = g_all.shape[0]
    g_ref[:, most * rows :] = jnp.zeros((rows, LANES), F32)
    for slot in range(most):
        g_ref[:, slot * rows : (slot + 1) * rows] = g_all[slot, :, 0:rows]
        g_ref[:, most * rows + slot : most * rows + slot + 1] = g_all[slot, :, rows : rows + 1]


def sum_kernel(*refs):
    parts, (gw_ref, gb_ref) = refs[:-2], refs[-2:]
    most, rows, _ = gw_ref.shape
    total = sum(part[...] for part in parts)
    for slot in range(most):
        gw_ref[slot] = total[:, slot * rows : (slot + 1) * rows]
    gb_ref[...] = total[:, most * rows :].T[:most, :]


def chain_kernel(plan, _, second_ref, p_ref, *rest):
    msgs, rest = rest[: plan.items], rest[plan.items :]
    outs, (buf, held, done, wl, wt, bias, sem) = rest[: plan.results], rest[plan.results :]
    own = lax.axis_index("depth")
    host = own - plan.first
    rows = held.shape[1]
    size = plan.rows * IMG
    piece = plan.block * IMG

    @pl.when(jnp.logical_and(host >= 0, host < plan.hosts))
    def _():
        if plan.hosts > 4:
            copies = [
                pltpu.make_async_copy(msg, held.at[lax.rem(host + shift, plan.items)], sem.at[shift])
                for shift, msg in enumerate(msgs)
            ]
            for copy in copies:
                copy.start()
            for copy in copies:
                copy.wait()
        for h in range(plan.hosts if plan.hosts <= 4 else 0):

            @pl.when(host == h)
            def _():
                for shift, msg in enumerate(msgs):
                    held[(h + shift) % plan.items] = msg[...]

        start = plan.window(host)
        offset = host * plan.block - start
        most = slots_of(p_ref)
        spread = table_of(p_ref)[:, most : most + 1] * (1.0 / most)
        for item in range(2, plan.items):
            ends = held[item, :, 0:LANES], held[item, :, size - LANES :]
            tile = jnp.where(start == 0, ends[1][:, IMG:], ends[0][:, :IMG])
            matrix = tile[:, 0:rows]
            scale = length_of(p_ref, item + 1).astype(F32) * (1.0 / most)
            wl[item] = left_factor(matrix)
            wt[item] = left_factor((scale * matrix).T)
            bias[item] = tile[:, rows : rows + 1]
        fill(buf, held[0] + held[1])

        def keep(result):
            done[result] = buf[:, pl.ds(pl.multiple_of(LANES + offset * IMG, LANES), piece)]

        keep(0)

        @pl.loop(2, plan.items)
        def _(item):
            forward_layer(
                buf, size, wl[item], wt[item], bias[item],
                length_of(p_ref, item + 1).astype(F32) * spread, paired=False,
            )
            buf[:, LANES : LANES + size] = inner(buf) + held[item]
            keep(item - 1)

        for shift, out in enumerate(outs):
            out[...] = done[lax.rem(host + shift, plan.results)]

    @pl.when(own == 0)
    def _():
        for shift, out in enumerate(outs):
            if shift < plan.hosts:
                out[...] = second_ref[:, shift * piece : (shift + 1) * piece]


def collect_kernel(plan, point_ref, local_ref, *rest):
    received, out_ref = rest[:-1], rest[-1]
    own = lax.axis_index("depth")
    host = own - plan.first

    @pl.when(own < 2)
    def _():
        out_ref[...] = point_ref[...]

    @pl.when(own == 2)
    def _():
        for shift, block in enumerate(received):
            if shift < plan.hosts:
                out_ref[:, lanes(shift * plan.block, plan.block)] = block[...]

    for shift, block in enumerate(received):
        sender = lax.rem(own - 3 - shift + 2 * plan.results, plan.results)

        @pl.when(jnp.logical_and(own > 2, jnp.logical_and(sender < plan.hosts, sender != host)))
        def _():
            out_ref[:, lanes(sender * plan.block, plan.block)] = block[...]

    @pl.when(jnp.logical_and(own > 2, jnp.logical_and(host >= 0, host < plan.hosts)))
    def _():
        out_ref[:, lanes(host * plan.block, plan.block)] = local_ref[...]


SMEM = pl.BlockSpec(memory_space=pltpu.SMEM)
VMEM = pl.BlockSpec(memory_space=pltpu.VMEM)
ANY = pl.BlockSpec(memory_space=pl.ANY)


def call(kernel, out_shape, in_specs, scratch, micros, name, mebi=32):
    return pl.pallas_call(
        kernel,
        out_shape=out_shape,
        in_specs=in_specs,
        out_specs=jax.tree.map(lambda _: VMEM, out_shape),
        scratch_shapes=scratch,
        compiler_params=pltpu.CompilerParams(vmem_limit_bytes=mebi * 2**20),
        cost_estimate=pl.CostEstimate(flops=int(micros * 1e8), bytes_accessed=2**21, transcendentals=0),
        name=name,
    )


def shifted(value, steps):
    count = lax.axis_size("depth")
    first, end = max(0, -steps), min(count, count - steps)
    return lax.ppermute(value, "depth", [(s, s + steps) for s in range(first, end)])


def others(value, step):
    count = lax.axis_size("batch")
    xor = count & (count - 1) == 0
    return lax.ppermute(value, "batch", [(s, s ^ step if xor else (s + step) % count) for s in range(count)])


def body(cpoint_guess, adjoint_guess, weights, biases, diffusion, section_len):
    plan = Plan(lax.axis_size("depth"))
    most, rows, _ = weights.shape
    width = cpoint_guess.shape[-1]
    guess, adjoint = cpoint_guess[0, 0], adjoint_guess[0, 0]

    def shape(*dims):
        return jax.ShapeDtypeStruct(dims, F32)

    state = shape(rows, width)
    buffer = pltpu.VMEM((rows, width + 2 * LANES), F32)
    factors = [pltpu.VMEM((most, rows, 3 * rows), BF16)] * 2

    wide = most * rows + LANES
    packed, packed0, both = call(
        pack_kernel, [shape(rows, wide), shape(rows, LANES), shape(rows, width + wide)], [ANY] * 5,
        [
            pltpu.VMEM(weights.shape, F32), pltpu.VMEM(biases.shape, F32), pltpu.VMEM((1, rows), F32),
            pltpu.VMEM((1, plan.count), jnp.int32), pltpu.SemaphoreType.DMA((5,)),
        ],
        1, "pack", 60,
    )(weights, biases, diffusion[None], section_len[None], guess)
    packed_after = shifted(packed, -1)
    packed_second = lax.ppermute(packed0, "depth", [(2, 0)])
    before = shifted(both, 1)
    saved = jax.ShapeDtypeStruct((most, rows, width), BF16)
    factor_shape = jax.ShapeDtypeStruct((most, rows, 3 * rows), BF16)
    window = shape(rows, plan.rows * IMG)
    second, own_wl, own_wt, *msgs = call(
        functools.partial(front_kernel, plan), [state, factor_shape, factor_shape] + [window] * plan.items,
        [VMEM] * 3, [buffer, *factors, pltpu.VMEM(state.shape, F32), pltpu.VMEM(state.shape, F32)], 40, "front",
    )(both, packed_after, packed_second)
    arrived = {plan.first: msgs[plan.first]}
    order = [shift for shift in range(plan.items) if shift != plan.first]
    for k, shift in enumerate(order):
        msg = msgs[shift]
        if k >= AT_ONCE:
            msg, _ = lax.optimization_barrier((msg, arrived[order[k - AT_ONCE]]))
        arrived[shift] = lax.ppermute(msg, "depth", plan.in_pairs(shift))
    msgs = [arrived[shift] for shift in range(plan.items)]

    point, lam, *kept = call(
        point_kernel, [state] * 2 + [saved] * 4, [ANY] + [VMEM] * 5, [buffer, *factors], 6, "point"
    )(msgs[plan.first], both, before, adjoint, own_wl, own_wt)
    lam_after = shifted(lam, -1)

    piece = shape(rows, plan.block * IMG)
    blocks = call(
        functools.partial(chain_kernel, plan), [piece] * plan.results,
        [ANY, VMEM, VMEM] + [VMEM if plan.hosts <= 4 else ANY] * plan.items,
        [
            pltpu.VMEM((rows, plan.rows * IMG + 2 * LANES), F32),
            pltpu.VMEM((plan.items, *window.shape), F32),
            pltpu.VMEM((plan.results, *piece.shape), F32),
            pltpu.VMEM((plan.items, rows, 3 * rows), BF16),
            pltpu.VMEM((plan.items, rows, 3 * rows), BF16),
            pltpu.VMEM((plan.items, rows, 1), F32),
            pltpu.SemaphoreType.DMA((plan.items,)),
        ],
        40, "chain",
    )(lam, second, packed, *msgs)
    received = [lax.ppermute(block, "depth", plan.out_pairs(k)) for k, block in enumerate(blocks)]

    pair = pltpu.VMEM((2 * rows, width), BF16)
    adjoint_out, grads = call(
        adjoint_kernel, [state, shape(rows, wide)], [ANY] + [VMEM] * 9,
        [buffer, pair, pair, pltpu.VMEM((most, rows, rows + 1), F32)], 10, "adjoint",
    )(blocks[plan.local], adjoint, lam_after, packed, own_wl, own_wt, *kept)

    states = call(
        functools.partial(collect_kernel, plan), state, [VMEM] * (2 + plan.results), [], 0.5, "collect"
    )(point, blocks[plan.local], *received)
    grads, *_ = lax.optimization_barrier((grads, *received))
    parts = [grads] + [others(grads, step) for step in range(1, lax.axis_size("batch"))]
    gw, gb = call(
        sum_kernel, [shape(*weights.shape), shape(*biases.shape)], [VMEM] * len(parts), [], 0.5, "sum"
    )(*parts)
    return states[None, None], adjoint_out[None, None], gw, gb


def solution(mesh):
    state = P("depth", "batch", None, None)
    return jax.shard_map(
        body,
        mesh=mesh,
        in_specs=(state, state, P("depth", None, None), P("depth", None), P(), P()),
        out_specs=(state, state, P("depth", None, None), P("depth", None)),
        check_vma=False,
    )
```

```python
import functools

import jax
import jax.numpy as jnp
from jax import lax
from jax.experimental import pallas as pl
from jax.experimental.pallas import tpu as pltpu
from jax.sharding import PartitionSpec as P

IMG = 64
LANES = 128
CHUNK = 256
AT_ONCE = 4
F32 = jnp.float32
BF16 = jnp.bfloat16


def split(x):
    hi = x.astype(BF16)
    lo = (x - hi.astype(F32)).astype(BF16)
    return hi, lo


def stack3(hi, lo):
    return jnp.concatenate([hi, lo, hi], axis=0)


def left_factor(matrix):
    hi = matrix.astype(BF16).astype(F32)
    return jnp.concatenate([hi, hi, matrix - hi], axis=1).astype(BF16)


def mm(a, b):
    return jnp.dot(a, b, preferred_element_type=F32)


def mm_nt(a, b):
    return lax.dot_general(a, b, (((1,), (1,)), ((), ())), preferred_element_type=F32)


def lane_masks(rows):
    lane = lax.broadcasted_iota(jnp.int32, (rows, LANES), 1)
    col = lane % IMG
    return col > 0, col < IMG - 1, lane < IMG


def swap(piece):
    return pltpu.roll(piece, IMG, 1)


def pieces_of(x):
    return [x[:, k : k + LANES] for k in range(0, x.shape[1], LANES)]


def to_pairs(x):
    pieces = pieces_of(x)
    half = len(pieces) // 2
    lower = lane_masks(x.shape[0])[2]
    out = []
    for k in range(half):
        out.append(jnp.where(lower, pieces[k], swap(pieces[k + half])))
        out.append(jnp.where(lower, swap(pieces[k]), pieces[k + half]))
    return jnp.concatenate(out, axis=1)


def from_pairs(x):
    pieces = pieces_of(x)
    half = len(pieces) // 2
    lower = lane_masks(x.shape[0])[2]
    first = [jnp.where(lower, pieces[2 * k], swap(pieces[2 * k + 1])) for k in range(half)]
    second = [jnp.where(lower, swap(pieces[2 * k]), pieces[2 * k + 1]) for k in range(half)]
    return jnp.concatenate(first + second, axis=1)


def neighbours(left, mid, right, masks, paired):
    not_first, not_last, lower = masks
    pieces = [left] + pieces_of(mid) + [right]
    swapped = None if paired else [swap(piece) for piece in pieces]
    sums = []
    for k in range(1, len(pieces) - 1):
        piece = pieces[k]
        beside = jnp.where(not_first, pltpu.roll(piece, 1, 1), 0.0)
        beside += jnp.where(not_last, pltpu.roll(piece, LANES - 1, 1), 0.0)
        if paired:
            beside += pieces[k - 1] + pieces[k + 1]
        else:
            beside += swapped[k] + jnp.where(lower, swapped[k - 1], swapped[k + 1])
        sums.append(beside)
    return jnp.concatenate(sums, axis=1)


def sweep(buf, width, step, paired):
    rows = buf.shape[0]
    masks = lane_masks(rows)
    if paired:
        lower = masks[2]
        before = jnp.where(lower, 0.0, swap(buf[:, width : width + LANES]))
        buf[:, width + LANES :] = jnp.where(lower, swap(buf[:, LANES : 2 * LANES]), 0.0)
    else:
        before = buf[:, 0:LANES]
    for start in range(0, width, CHUNK):
        size = min(CHUNK, width - start)
        at = LANES + start
        mid = buf[:, at : at + size]
        after = buf[:, at + size : at + size + LANES]
        around = neighbours(before, mid, after, masks, paired)
        before = mid[:, size - LANES :]
        buf[:, at : at + size] = step(start, size, mid, around)


def matrix_of(p_ref, slot):
    rows = p_ref.shape[0]
    return p_ref[:, slot * rows : (slot + 1) * rows]


def table_of(p_ref):
    return p_ref[:, p_ref.shape[1] - LANES :]


def bias_of(p_ref, slot):
    table = table_of(p_ref)
    pick = lax.broadcasted_iota(jnp.int32, table.shape, 1) == slot
    return jnp.sum(jnp.where(pick, table, 0.0), axis=1, keepdims=True)


def slots_of(p_ref):
    rows, width = p_ref.shape
    return (width - LANES) // rows


def scales_of(p_ref):
    most = slots_of(p_ref)
    return (1.0 / most) * table_of(p_ref)[:, most : most + 1], 1.0 / most


def prepare(p_ref, wl_ref, wt_ref):
    spread, factor = scales_of(p_ref)
    for slot in range(slots_of(p_ref)):
        matrix = matrix_of(p_ref, slot)
        wl_ref[slot] = left_factor(matrix)
        wt_ref[slot] = left_factor((factor * matrix).T)
    return spread, factor


def column(row):
    n = row.shape[1]
    same = lax.broadcasted_iota(jnp.int32, (n, n), 0) == lax.broadcasted_iota(jnp.int32, (n, n), 1)
    return jnp.sum(jnp.where(same, row, 0.0), axis=1, keepdims=True)


def length_of(p_ref, section):
    row = table_of(p_ref)[0:1, :]
    pick = lax.broadcasted_iota(jnp.int32, row.shape, 1) == slots_of(p_ref) + 1 + section
    return jnp.sum(jnp.where(pick, row, 0.0)).astype(jnp.int32)


def pack_kernel(
    w_any, b_any, diff_any, len_any, guess_any, p_ref, p0_ref, both_ref, w_ref, b_ref, diff_ref, len_ref, sem
):
    most, rows, _ = w_ref.shape
    width = guess_any.shape[1]
    copies = [
        pltpu.make_async_copy(source, target, sem.at[k])
        for k, (source, target) in enumerate(
            [(w_any, w_ref), (b_any, b_ref), (diff_any, diff_ref), (len_any, len_ref),
             (guess_any, both_ref.at[:, 0:width])]
        )
    ]
    for copy in copies:
        copy.start()
    for copy in copies[:-1]:
        copy.wait()
    wide = most * rows
    p_ref[:, wide:] = jnp.zeros((rows, LANES), F32)
    for slot in range(most):
        p_ref[:, slot * rows : (slot + 1) * rows] = w_ref[slot]
        p_ref[:, wide + slot : wide + slot + 1] = column(b_ref[slot : slot + 1, :])
    p_ref[:, wide + most : wide + most + 1] = column(diff_ref[...])
    lengths = len_ref[...].astype(F32)
    first = wide + most + 1
    p_ref[:, first : first + lengths.shape[1]] = jnp.broadcast_to(lengths, (rows, lengths.shape[1]))
    p0_ref[...] = jnp.zeros_like(p0_ref)
    p0_ref[:, 0:rows] = w_ref[0]
    p0_ref[:, rows : rows + 1] = column(b_ref[0:1, :])
    both_ref[:, width:] = p_ref[...]
    copies[-1].wait()


def forward_layer(buf, width, wl, wt, bias, spread, t_out=None, u_out=None, paired=True):
    keep = 1.0 - 4.0 * spread

    def step(start, size, mid, around):
        hi, lo = split(mid)
        t_hi, t_lo = split(jnp.tanh(mm(wl, stack3(hi, lo)) + bias))
        if t_out is not None:
            t_out(start, size, t_hi, t_lo)
        if u_out is not None:
            u_out(start, size, hi, lo)
        return mid * keep + around * spread - mm(wt, stack3(t_hi, t_lo))

    sweep(buf, width, step, paired)


def run_forward(buf, width, p_ref, wl_ref, wt_ref, spread, count, t_refs=None, u_refs=None):
    def saver(refs, slot):
        if refs is None:
            return None

        def save(start, size, hi, lo):
            refs[0][slot, :, start : start + size] = hi
            refs[1][slot, :, start : start + size] = lo

        return save

    @pl.loop(0, count)
    def _(slot):
        forward_layer(
            buf, width, wl_ref[slot], wt_ref[slot], bias_of(p_ref, slot), spread,
            saver(t_refs, slot), saver(u_refs, slot),
        )


def run_backward(buf, width, wl_ref, wt_ref, spread, count, t_refs, u_refs=None, grads=None):
    keep = 1.0 - 4.0 * spread

    @pl.loop(0, count)
    def _(passed):
        slot = count - 1 - passed
        wl, wt = wl_ref[slot], wt_ref[slot]
        rows = buf.shape[0]
        sums = []

        def step(start, size, mid, around):
            span = slice(start, start + size)
            hi, lo = split(mid)
            t = t_refs[0][slot, :, span].astype(F32) + t_refs[1][slot, :, span].astype(F32)
            q = (1.0 - t * t) * mm(wl, stack3(hi, lo))
            q_hi, q_lo = split(q)
            if grads is not None:
                _, _, lam_ref, q_ref = grads
                lam_ref[0:rows, span], lam_ref[rows:, span] = hi, lo
                q_ref[0:rows, span], q_ref[rows:, span] = q_hi, q_lo
                sums.append(sum(q[:, k : k + LANES] for k in range(0, size, LANES)))
            return mid * keep + around * spread - mm(wt, stack3(q_hi, q_lo))

        sweep(buf, width, step, True)
        if grads is not None:
            g_ref, factor, lam_ref, q_ref = grads

            def product(left, right):
                g = mm_nt(left, right)
                return g[:rows, :rows] + g[:rows, rows:] + g[rows:, :rows]

            gw = product(jnp.concatenate([ref[slot] for ref in t_refs], axis=0), lam_ref[...])
            gw += product(q_ref[...], jnp.concatenate([ref[slot] for ref in u_refs], axis=0))
            g_ref[slot, :, 0:rows] = -factor * gw
            g_ref[slot, :, rows : rows + 1] = -factor * jnp.sum(sum(sums), axis=1, keepdims=True)


def fill(buf, value):
    rows, width = value.shape
    zero = jnp.zeros((rows, LANES), F32)
    buf[:, 0:LANES] = zero
    buf[:, LANES + width :] = zero
    buf[:, LANES : LANES + width] = value


def inner(buf):
    return buf[:, LANES : buf.shape[1] - LANES]


class Plan:
    def __init__(self, count):
        self.count = count
        self.items = count - 2
        self.hosts = count // 2
        self.first = count // 4
        self.block = IMG // self.hosts
        self.rows = min(IMG, self.block + 2 * (count - 4))
        self.rows += self.rows % 2
        self.results = count - 3
        self.local = (self.first - 3) % self.results

    def window(self, host):
        start = host * self.block - (self.count - 4)
        return jnp.clip(start - start % 2, 0, IMG - self.rows)

    def in_order(self):
        shifts = [s for s in range(self.items) if s != self.first]
        return shifts[:1] + shifts[-1:] + shifts[1:-1]

    def in_pairs(self, shift):
        return [((h + shift) % self.items, h + self.first) for h in range(self.hosts)]

    def out_pairs(self, shift):
        pairs = [(h + self.first, 3 + (h + shift) % self.results) for h in range(self.hosts)]
        return [(s, d) for s, d in pairs if s != d]


def lanes(row, size):
    return pl.ds(pl.multiple_of(row * IMG, LANES), size * IMG)


def front_kernel(plan, both_ref, p_ref, p2_ref, second_ref, own_wl, own_wt, wl, wt, t_hi, t_lo, *rest):
    msgs, (buf, whole, start_state) = rest[:-3], rest[-3:]
    rows, width = second_ref.shape
    own = lax.axis_index("depth")
    own_p_ref = both_ref.at[:, width:]
    spread, factor = prepare(own_p_ref, own_wl, own_wt)
    fill(buf, to_pairs(both_ref[:, 0:width]))
    run_forward(buf, width, own_p_ref, own_wl, own_wt, spread, length_of(own_p_ref, own))
    start_state[...] = inner(buf)

    count = length_of(own_p_ref, jnp.minimum(own + 1, plan.count - 1))
    prepare(p_ref, wl, wt)
    run_forward(buf, width, p_ref, wl, wt, spread, count, (t_hi, t_lo))
    whole[...] = inner(buf)

    def coarse(matrix, bias, length):
        scale = length.astype(F32)
        forward_layer(
            buf, width, left_factor(matrix), left_factor((scale * factor * matrix).T), bias, scale * spread
        )

    @pl.when(own > 0)
    def _():
        buf[:, LANES : LANES + width] = start_state[...]
        coarse(matrix_of(p_ref, 0), bias_of(p_ref, 0), count)
        whole[...] = from_pairs(whole[...] - inner(buf))

    @pl.when(own == 0)
    def _():
        second_ref[...] = from_pairs(whole[...])
        coarse(p2_ref[:, 0:rows], p2_ref[:, rows : rows + 1], length_of(own_p_ref, 2))
        whole[...] = from_pairs(inner(buf))

    size = plan.rows * IMG
    bias = bias_of(p_ref, 0)
    for shift, msg in enumerate(msgs):
        host = lax.rem(own - shift + 2 * plan.items, plan.items)
        start = plan.window(jnp.minimum(host, plan.hosts - 1))
        msg[...] = whole[:, lanes(start, plan.rows)]
        for at, here in ((size - IMG, start == 0), (0, start > 0)):

            @pl.when(jnp.logical_and(own > 1, here))
            def _():
                msg[:, at : at + rows] = matrix_of(p_ref, 0)
                msg[:, at + rows : at + rows + 1] = bias


def point_kernel(
    _, both_ref, before_ref, own_wl, own_wt, point_ref, t_hi, t_lo, u_hi, u_lo, buf, wl, wt
):
    own = lax.axis_index("depth")
    width = point_ref.shape[1]

    @pl.when(own > 0)
    def _():
        p_before_ref = before_ref.at[:, width:]
        count = length_of(p_before_ref, jnp.maximum(own - 1, 0))
        spread, _ = prepare(p_before_ref, wl, wt)
        fill(buf, to_pairs(before_ref[:, 0:width]))
        run_forward(buf, width, p_before_ref, wl, wt, spread, count)

    @pl.when(own == 1)
    def _():
        point_ref[...] = from_pairs(inner(buf))

    @pl.when(own == 0)
    def _():
        point_ref[...] = both_ref[:, 0:width]
        fill(buf, to_pairs(both_ref[:, 0:width]))

    p_ref = both_ref.at[:, width:]
    count = length_of(p_ref, own)
    spread, _ = scales_of(p_ref)
    run_forward(buf, width, p_ref, own_wl, own_wt, spread, count, (t_hi, t_lo), (u_hi, u_lo))


def adjoint_kernel(
    _, adj_ref, adj_after_ref, p_ref, wl, wt, wl_after, wt_after, t_after_hi, t_after_lo, t_hi, t_lo, u_hi, u_lo,
    adj_out_ref, g_ref, buf, lam_ref, q_ref, g_all,
):
    own = lax.axis_index("depth")
    last = lax.axis_size("depth") - 1
    rows, width = adj_out_ref.shape
    g_all[...] = jnp.zeros_like(g_all)

    @pl.when(own < last)
    def _():
        count = length_of(p_ref, jnp.minimum(own + 1, last))
        spread, _ = scales_of(p_ref)
        fill(buf, to_pairs(adj_after_ref[...]))
        run_backward(buf, width, wl_after, wt_after, spread, count, (t_after_hi, t_after_lo))

    @pl.when(own == last)
    def _():
        fill(buf, to_pairs(adj_ref[...]))

    spread, factor = scales_of(p_ref)
    run_backward(
        buf, width, wl, wt, spread, length_of(p_ref, own), (t_hi, t_lo), (u_hi, u_lo),
        (g_all, factor, lam_ref, q_ref),
    )
    adj_out_ref[...] = from_pairs(inner(buf))
    most = g_all.shape[0]
    g_ref[:, most * rows :] = jnp.zeros((rows, LANES), F32)
    for slot in range(most):
        g_ref[:, slot * rows : (slot + 1) * rows] = g_all[slot, :, 0:rows]
        g_ref[:, most * rows + slot : most * rows + slot + 1] = g_all[slot, :, rows : rows + 1]


def sum_kernel(*refs):
    parts, (gw_ref, gb_ref) = refs[:-2], refs[-2:]
    most, rows, _ = gw_ref.shape
    total = sum(part[...] for part in parts)
    for slot in range(most):
        gw_ref[slot] = total[:, slot * rows : (slot + 1) * rows]
    gb_ref[...] = total[:, most * rows :].T[:most, :]


def chain_kernel(plan, _, p_ref, *rest):
    msgs, rest = rest[: plan.items], rest[plan.items :]
    outs, (buf, held, done, wl, wt, bias, sem) = rest[: plan.results], rest[plan.results :]
    own = lax.axis_index("depth")
    host = own - plan.first
    rows = held.shape[1]
    size = plan.rows * IMG
    piece = plan.block * IMG

    @pl.when(jnp.logical_and(host >= 0, host < plan.hosts))
    def _():
        if plan.hosts > 4:
            copies = [
                pltpu.make_async_copy(msg, held.at[lax.rem(host + shift, plan.items)], sem.at[shift])
                for shift, msg in enumerate(msgs)
            ]
            for copy in copies:
                copy.start()
            for copy in copies:
                copy.wait()
        for h in range(plan.hosts if plan.hosts <= 4 else 0):

            @pl.when(host == h)
            def _():
                for shift, msg in enumerate(msgs):
                    held[(h + shift) % plan.items] = msg[...]

        start = plan.window(host)
        offset = host * plan.block - start
        most = slots_of(p_ref)
        spread = table_of(p_ref)[:, most : most + 1] * (1.0 / most)
        for item in range(2, plan.items):
            ends = held[item, :, 0:LANES], held[item, :, size - LANES :]
            tile = jnp.where(start == 0, ends[1][:, IMG:], ends[0][:, :IMG])
            matrix = tile[:, 0:rows]
            scale = length_of(p_ref, item + 1).astype(F32) * (1.0 / most)
            wl[item] = left_factor(matrix)
            wt[item] = left_factor((scale * matrix).T)
            bias[item] = tile[:, rows : rows + 1]
        fill(buf, held[0] + held[1])

        def keep(result):
            done[result] = buf[:, pl.ds(pl.multiple_of(LANES + offset * IMG, LANES), piece)]

        keep(0)

        @pl.loop(2, plan.items)
        def _(item):
            forward_layer(
                buf, size, wl[item], wt[item], bias[item],
                length_of(p_ref, item + 1).astype(F32) * spread, paired=False,
            )
            buf[:, LANES : LANES + size] = inner(buf) + held[item]
            keep(item - 1)

        for shift, out in enumerate(outs):
            out[...] = done[lax.rem(host + shift, plan.results)]


def collect_kernel(plan, point_ref, second_ref, local_ref, *rest):
    received, out_ref = rest[:-1], rest[-1]
    own = lax.axis_index("depth")
    host = own - plan.first

    @pl.when(own < 2)
    def _():
        out_ref[...] = point_ref[...]

    @pl.when(own == 2)
    def _():
        out_ref[...] = second_ref[...]

    for shift, block in enumerate(received):
        sender = lax.rem(own - 3 - shift + 2 * plan.results, plan.results)

        @pl.when(jnp.logical_and(own > 2, jnp.logical_and(sender < plan.hosts, sender != host)))
        def _():
            out_ref[:, lanes(sender * plan.block, plan.block)] = block[...]

    @pl.when(jnp.logical_and(own > 2, jnp.logical_and(host >= 0, host < plan.hosts)))
    def _():
        out_ref[:, lanes(host * plan.block, plan.block)] = local_ref[...]


SMEM = pl.BlockSpec(memory_space=pltpu.SMEM)
VMEM = pl.BlockSpec(memory_space=pltpu.VMEM)
ANY = pl.BlockSpec(memory_space=pl.ANY)


def call(kernel, out_shape, in_specs, scratch, micros, name, mebi=32, moved=2**21):
    return pl.pallas_call(
        kernel,
        out_shape=out_shape,
        in_specs=in_specs,
        out_specs=jax.tree.map(lambda _: VMEM, out_shape),
        scratch_shapes=scratch,
        compiler_params=pltpu.CompilerParams(vmem_limit_bytes=mebi * 2**20),
        cost_estimate=pl.CostEstimate(flops=int(micros * 1e8), bytes_accessed=moved, transcendentals=0),
        name=name,
    )


def shifted(value, steps):
    count = lax.axis_size("depth")
    first, end = max(0, -steps), min(count, count - steps)
    return lax.ppermute(value, "depth", [(s, s + steps) for s in range(first, end)])


def others(value, step):
    count = lax.axis_size("batch")
    xor = count & (count - 1) == 0
    return lax.ppermute(value, "batch", [(s, s ^ step if xor else (s + step) % count) for s in range(count)])


def body(cpoint_guess, adjoint_guess, weights, biases, diffusion, section_len):
    plan = Plan(lax.axis_size("depth"))
    most, rows, _ = weights.shape
    width = cpoint_guess.shape[-1]
    guess, adjoint = cpoint_guess[0, 0], adjoint_guess[0, 0]

    def shape(*dims):
        return jax.ShapeDtypeStruct(dims, F32)

    state = shape(rows, width)
    buffer = pltpu.VMEM((rows, width + 2 * LANES), F32)
    factors = [pltpu.VMEM((most, rows, 3 * rows), BF16)] * 2

    wide = most * rows + LANES
    packed, packed0, both = call(
        pack_kernel, [shape(rows, wide), shape(rows, LANES), shape(rows, width + wide)], [ANY] * 5,
        [
            pltpu.VMEM(weights.shape, F32), pltpu.VMEM(biases.shape, F32), pltpu.VMEM((1, rows), F32),
            pltpu.VMEM((1, plan.count), jnp.int32), pltpu.SemaphoreType.DMA((5,)),
        ],
        1, "pack", 60,
    )(weights, biases, diffusion[None], section_len[None], guess)
    packed_after = shifted(packed, -1)
    packed_second = lax.ppermute(packed0, "depth", [(2, 0)])
    before = shifted(both, 1)
    saved = jax.ShapeDtypeStruct((most, rows, width), BF16)
    factor_shape = jax.ShapeDtypeStruct((most, rows, 3 * rows), BF16)
    window = shape(rows, plan.rows * IMG)
    second, own_wl, own_wt, wl, wt, t_after_hi, t_after_lo, *msgs = call(
        functools.partial(front_kernel, plan), [state] + [factor_shape] * 4 + [saved] * 2 + [window] * plan.items,
        [VMEM] * 3, [buffer, pltpu.VMEM(state.shape, F32), pltpu.VMEM(state.shape, F32)], 40, "front",
    )(both, packed_after, packed_second)
    arrived = {plan.first: msgs[plan.first]}
    order = plan.in_order()
    for k, shift in enumerate(order):
        msg = msgs[shift]
        if k >= AT_ONCE:
            msg, _ = lax.optimization_barrier((msg, arrived[order[k - AT_ONCE]]))
        arrived[shift] = lax.ppermute(msg, "depth", plan.in_pairs(shift))
    msgs = [arrived[shift] for shift in range(plan.items)]

    point, *kept = call(
        point_kernel, [state] + [saved] * 4, [ANY] + [VMEM] * 4, [buffer, *factors], 6, "point"
    )(msgs[plan.first], both, before, own_wl, own_wt)
    adjoint_later, _ = lax.optimization_barrier((adjoint, point))
    adj_after = shifted(adjoint_later, -1)

    piece = shape(rows, plan.block * IMG)
    blocks = call(
        functools.partial(chain_kernel, plan), [piece] * plan.results,
        [ANY, VMEM] + [VMEM if plan.hosts <= 4 else ANY] * plan.items,
        [
            pltpu.VMEM((rows, plan.rows * IMG + 2 * LANES), F32),
            pltpu.VMEM((plan.items, *window.shape), F32),
            pltpu.VMEM((plan.results, *piece.shape), F32),
            pltpu.VMEM((plan.items, rows, 3 * rows), BF16),
            pltpu.VMEM((plan.items, rows, 3 * rows), BF16),
            pltpu.VMEM((plan.items, rows, 1), F32),
            pltpu.SemaphoreType.DMA((plan.items,)),
        ],
        40, "chain",
    )(point, packed, *msgs)
    second, *_ = lax.optimization_barrier((second, blocks[0]))
    second_arrived = lax.ppermute(second, "depth", [(0, 2)])
    blocks = list(blocks)
    blocks[3], blocks[4], adj_after = lax.optimization_barrier((blocks[3], blocks[4], adj_after))
    received = [lax.ppermute(block, "depth", plan.out_pairs(k)) for k, block in enumerate(blocks)]

    pair = pltpu.VMEM((2 * rows, width), BF16)
    adjoint_out, grads = call(
        adjoint_kernel, [state, shape(rows, wide)], [ANY] + [VMEM] * 13,
        [buffer, pair, pair, pltpu.VMEM((most, rows, rows + 1), F32)], 10, "adjoint",
    )(
        blocks[plan.local], adjoint, adj_after, packed, own_wl, own_wt, wl, wt, t_after_hi, t_after_lo, *kept
    )

    states = call(
        functools.partial(collect_kernel, plan), state, [VMEM] * (3 + plan.results), [], 0.5, "collect"
    )(point, second_arrived, blocks[plan.local], *received)
    grads, *_ = lax.optimization_barrier((grads, *received))
    parts = [grads] + [others(grads, step) for step in range(1, lax.axis_size("batch"))]
    gw, gb = call(
        sum_kernel, [shape(*weights.shape), shape(*biases.shape)], [VMEM] * len(parts), [], 0.5, "sum"
    )(*parts)
    return states[None, None], adjoint_out[None, None], gw, gb


def solution(mesh):
    state = P("depth", "batch", None, None)
    return jax.shard_map(
        body,
        mesh=mesh,
        in_specs=(state, state, P("depth", None, None), P("depth", None), P(), P()),
        out_specs=(state, state, P("depth", None, None), P("depth", None)),
        check_vma=False,
    )
```

```python
import functools

import jax
import jax.numpy as jnp
from jax import lax
from jax.experimental import pallas as pl
from jax.experimental.pallas import tpu as pltpu
from jax.sharding import PartitionSpec as P

IMG = 64
LANES = 128
CHUNK = 256
AT_ONCE = 4
F32 = jnp.float32
BF16 = jnp.bfloat16


def split(x):
    hi = x.astype(BF16)
    lo = (x - hi.astype(F32)).astype(BF16)
    return hi, lo


def stack3(hi, lo):
    return jnp.concatenate([hi, lo, hi], axis=0)


def left_factor(matrix):
    hi = matrix.astype(BF16).astype(F32)
    return jnp.concatenate([hi, hi, matrix - hi], axis=1).astype(BF16)


def mm(a, b):
    return jnp.dot(a, b, preferred_element_type=F32)


def mm_nt(a, b):
    return lax.dot_general(a, b, (((1,), (1,)), ((), ())), preferred_element_type=F32)


def lane_masks(rows):
    lane = lax.broadcasted_iota(jnp.int32, (rows, LANES), 1)
    col = lane % IMG
    return col > 0, col < IMG - 1, lane < IMG


def swap(piece):
    return pltpu.roll(piece, IMG, 1)


def pieces_of(x):
    return [x[:, k : k + LANES] for k in range(0, x.shape[1], LANES)]


def to_pairs(x):
    pieces = pieces_of(x)
    half = len(pieces) // 2
    lower = lane_masks(x.shape[0])[2]
    out = []
    for k in range(half):
        out.append(jnp.where(lower, pieces[k], swap(pieces[k + half])))
        out.append(jnp.where(lower, swap(pieces[k]), pieces[k + half]))
    return jnp.concatenate(out, axis=1)


def from_pairs(x):
    pieces = pieces_of(x)
    half = len(pieces) // 2
    lower = lane_masks(x.shape[0])[2]
    first = [jnp.where(lower, pieces[2 * k], swap(pieces[2 * k + 1])) for k in range(half)]
    second = [jnp.where(lower, swap(pieces[2 * k]), pieces[2 * k + 1]) for k in range(half)]
    return jnp.concatenate(first + second, axis=1)


def neighbours(left, mid, right, masks, paired):
    not_first, not_last, lower = masks
    pieces = [left] + pieces_of(mid) + [right]
    swapped = None if paired else [swap(piece) for piece in pieces]
    sums = []
    for k in range(1, len(pieces) - 1):
        piece = pieces[k]
        beside = jnp.where(not_first, pltpu.roll(piece, 1, 1), 0.0)
        beside += jnp.where(not_last, pltpu.roll(piece, LANES - 1, 1), 0.0)
        if paired:
            beside += pieces[k - 1] + pieces[k + 1]
        else:
            beside += swapped[k] + jnp.where(lower, swapped[k - 1], swapped[k + 1])
        sums.append(beside)
    return jnp.concatenate(sums, axis=1)


def sweep(buf, width, step, paired):
    rows = buf.shape[0]
    masks = lane_masks(rows)
    if paired:
        lower = masks[2]
        before = jnp.where(lower, 0.0, swap(buf[:, width : width + LANES]))
        buf[:, width + LANES :] = jnp.where(lower, swap(buf[:, LANES : 2 * LANES]), 0.0)
    else:
        before = buf[:, 0:LANES]
    for start in range(0, width, CHUNK):
        size = min(CHUNK, width - start)
        at = LANES + start
        mid = buf[:, at : at + size]
        after = buf[:, at + size : at + size + LANES]
        around = neighbours(before, mid, after, masks, paired)
        before = mid[:, size - LANES :]
        buf[:, at : at + size] = step(start, size, mid, around)


def matrix_of(p_ref, slot):
    rows = p_ref.shape[0]
    return p_ref[:, slot * rows : (slot + 1) * rows]


def table_of(p_ref):
    return p_ref[:, p_ref.shape[1] - LANES :]


def bias_of(p_ref, slot):
    table = table_of(p_ref)
    pick = lax.broadcasted_iota(jnp.int32, table.shape, 1) == slot
    return jnp.sum(jnp.where(pick, table, 0.0), axis=1, keepdims=True)


def slots_of(p_ref):
    rows, width = p_ref.shape
    return (width - LANES) // rows


def scales_of(p_ref):
    most = slots_of(p_ref)
    return (1.0 / most) * table_of(p_ref)[:, most : most + 1], 1.0 / most


def prepare(p_ref, wl_ref, wt_ref):
    spread, factor = scales_of(p_ref)
    for slot in range(slots_of(p_ref)):
        matrix = matrix_of(p_ref, slot)
        wl_ref[slot] = left_factor(matrix)
        wt_ref[slot] = left_factor((factor * matrix).T)
    return spread, factor


def column(row):
    n = row.shape[1]
    same = lax.broadcasted_iota(jnp.int32, (n, n), 0) == lax.broadcasted_iota(jnp.int32, (n, n), 1)
    return jnp.sum(jnp.where(same, row, 0.0), axis=1, keepdims=True)


def length_of(p_ref, section):
    row = table_of(p_ref)[0:1, :]
    pick = lax.broadcasted_iota(jnp.int32, row.shape, 1) == slots_of(p_ref) + 1 + section
    return jnp.sum(jnp.where(pick, row, 0.0)).astype(jnp.int32)


def pack_kernel(
    w_any, b_any, diff_any, len_any, guess_any, p_ref, p0_ref, both_ref, w_ref, b_ref, diff_ref, len_ref, sem
):
    most, rows, _ = w_ref.shape
    width = guess_any.shape[1]
    copies = [
        pltpu.make_async_copy(source, target, sem.at[k])
        for k, (source, target) in enumerate(
            [(w_any, w_ref), (b_any, b_ref), (diff_any, diff_ref), (len_any, len_ref),
             (guess_any, both_ref.at[:, 0:width])]
        )
    ]
    for copy in copies:
        copy.start()
    for copy in copies[:-1]:
        copy.wait()
    wide = most * rows
    p_ref[:, wide:] = jnp.zeros((rows, LANES), F32)
    for slot in range(most):
        p_ref[:, slot * rows : (slot + 1) * rows] = w_ref[slot]
        p_ref[:, wide + slot : wide + slot + 1] = column(b_ref[slot : slot + 1, :])
    p_ref[:, wide + most : wide + most + 1] = column(diff_ref[...])
    lengths = len_ref[...].astype(F32)
    first = wide + most + 1
    p_ref[:, first : first + lengths.shape[1]] = jnp.broadcast_to(lengths, (rows, lengths.shape[1]))
    p0_ref[...] = jnp.zeros_like(p0_ref)
    p0_ref[:, 0:rows] = w_ref[0]
    p0_ref[:, rows : rows + 1] = column(b_ref[0:1, :])
    both_ref[:, width:] = p_ref[...]
    copies[-1].wait()


def forward_layer(buf, width, wl, wt, bias, spread, t_out=None, u_out=None, paired=True):
    keep = 1.0 - 4.0 * spread

    def step(start, size, mid, around):
        hi, lo = split(mid)
        t_hi, t_lo = split(jnp.tanh(mm(wl, stack3(hi, lo)) + bias))
        if t_out is not None:
            t_out(start, size, t_hi, t_lo)
        if u_out is not None:
            u_out(start, size, hi, lo)
        return mid * keep + around * spread - mm(wt, stack3(t_hi, t_lo))

    sweep(buf, width, step, paired)


def run_forward(buf, width, p_ref, wl_ref, wt_ref, spread, count, t_refs=None, u_refs=None):
    def saver(refs, slot):
        if refs is None:
            return None

        def save(start, size, hi, lo):
            refs[0][slot, :, start : start + size] = hi
            refs[1][slot, :, start : start + size] = lo

        return save

    @pl.loop(0, count)
    def _(slot):
        forward_layer(
            buf, width, wl_ref[slot], wt_ref[slot], bias_of(p_ref, slot), spread,
            saver(t_refs, slot), saver(u_refs, slot),
        )


def run_backward(buf, width, wl_ref, wt_ref, spread, count, t_refs, u_refs=None, grads=None):
    keep = 1.0 - 4.0 * spread

    @pl.loop(0, count)
    def _(passed):
        slot = count - 1 - passed
        wl, wt = wl_ref[slot], wt_ref[slot]
        rows = buf.shape[0]
        sums = []

        def step(start, size, mid, around):
            span = slice(start, start + size)
            hi, lo = split(mid)
            t = t_refs[0][slot, :, span].astype(F32) + t_refs[1][slot, :, span].astype(F32)
            q = (1.0 - t * t) * mm(wl, stack3(hi, lo))
            q_hi, q_lo = split(q)
            if grads is not None:
                _, _, lam_ref, q_ref = grads
                lam_ref[0:rows, span], lam_ref[rows:, span] = hi, lo
                q_ref[0:rows, span], q_ref[rows:, span] = q_hi, q_lo
                sums.append(sum(q[:, k : k + LANES] for k in range(0, size, LANES)))
            return mid * keep + around * spread - mm(wt, stack3(q_hi, q_lo))

        sweep(buf, width, step, True)
        if grads is not None:
            g_ref, factor, lam_ref, q_ref = grads

            def product(left, right):
                g = mm_nt(left, right)
                return g[:rows, :rows] + g[:rows, rows:] + g[rows:, :rows]

            gw = product(jnp.concatenate([ref[slot] for ref in t_refs], axis=0), lam_ref[...])
            gw += product(q_ref[...], jnp.concatenate([ref[slot] for ref in u_refs], axis=0))
            g_ref[slot, :, 0:rows] = -factor * gw
            g_ref[slot, :, rows : rows + 1] = -factor * jnp.sum(sum(sums), axis=1, keepdims=True)


def fill(buf, value):
    rows, width = value.shape
    zero = jnp.zeros((rows, LANES), F32)
    buf[:, 0:LANES] = zero
    buf[:, LANES + width :] = zero
    buf[:, LANES : LANES + width] = value


def inner(buf):
    return buf[:, LANES : buf.shape[1] - LANES]


class Plan:
    def __init__(self, count):
        self.count = count
        self.items = count - 2
        self.hosts = count // 2
        self.first = count // 4
        self.block = IMG // self.hosts
        self.rows = min(IMG, self.block + 2 * (count - 4))
        self.rows += self.rows % 2
        self.results = count - 3
        self.local = (self.first - 3) % self.results

    def window(self, host):
        start = host * self.block - (self.count - 4)
        return jnp.clip(start - start % 2, 0, IMG - self.rows)

    def in_order(self):
        shifts = [s for s in range(self.items) if s != self.first]
        return shifts[:1] + shifts[-1:] + shifts[1:-1]

    def in_pairs(self, shift):
        return [((h + shift) % self.items, h + self.first) for h in range(self.hosts)]

    def out_pairs(self, shift):
        pairs = [(h + self.first, 3 + (h + shift) % self.results) for h in range(self.hosts)]
        pairs = [(s, d) for s, d in pairs if s != d]
        return pairs + ([(0, 2)] if shift < self.hosts else [])


def lanes(row, size):
    return pl.ds(pl.multiple_of(row * IMG, LANES), size * IMG)


def front_kernel(plan, both_ref, p_ref, p2_ref, second_ref, own_wl, own_wt, wl, wt, t_hi, t_lo, *rest):
    msgs, (buf, whole, start_state) = rest[:-3], rest[-3:]
    rows, width = second_ref.shape
    own = lax.axis_index("depth")
    own_p_ref = both_ref.at[:, width:]
    spread, factor = prepare(own_p_ref, own_wl, own_wt)
    fill(buf, to_pairs(both_ref[:, 0:width]))
    run_forward(buf, width, own_p_ref, own_wl, own_wt, spread, length_of(own_p_ref, own))
    start_state[...] = inner(buf)

    count = length_of(own_p_ref, jnp.minimum(own + 1, plan.count - 1))
    prepare(p_ref, wl, wt)
    run_forward(buf, width, p_ref, wl, wt, spread, count, (t_hi, t_lo))
    whole[...] = inner(buf)

    def coarse(matrix, bias, length):
        scale = length.astype(F32)
        forward_layer(
            buf, width, left_factor(matrix), left_factor((scale * factor * matrix).T), bias, scale * spread
        )

    @pl.when(own > 0)
    def _():
        buf[:, LANES : LANES + width] = start_state[...]
        coarse(matrix_of(p_ref, 0), bias_of(p_ref, 0), count)
        whole[...] = from_pairs(whole[...] - inner(buf))

    @pl.when(own == 0)
    def _():
        second_ref[...] = from_pairs(whole[...])
        coarse(p2_ref[:, 0:rows], p2_ref[:, rows : rows + 1], length_of(own_p_ref, 2))
        whole[...] = from_pairs(inner(buf))

    size = plan.rows * IMG
    bias = bias_of(p_ref, 0)
    for shift, msg in enumerate(msgs):
        host = lax.rem(own - shift + 2 * plan.items, plan.items)
        start = plan.window(jnp.minimum(host, plan.hosts - 1))
        msg[...] = whole[:, lanes(start, plan.rows)]
        for at, here in ((size - IMG, start == 0), (0, start > 0)):

            @pl.when(jnp.logical_and(own > 1, here))
            def _():
                msg[:, at : at + rows] = matrix_of(p_ref, 0)
                msg[:, at + rows : at + rows + 1] = bias


def point_kernel(
    _, both_ref, before_ref, own_wl, own_wt, point_ref, t_hi, t_lo, u_hi, u_lo, buf, wl, wt
):
    own = lax.axis_index("depth")
    width = point_ref.shape[1]

    @pl.when(own > 0)
    def _():
        p_before_ref = before_ref.at[:, width:]
        count = length_of(p_before_ref, jnp.maximum(own - 1, 0))
        spread, _ = prepare(p_before_ref, wl, wt)
        fill(buf, to_pairs(before_ref[:, 0:width]))
        run_forward(buf, width, p_before_ref, wl, wt, spread, count)

    @pl.when(own == 1)
    def _():
        point_ref[...] = from_pairs(inner(buf))

    @pl.when(own == 0)
    def _():
        point_ref[...] = both_ref[:, 0:width]
        fill(buf, to_pairs(both_ref[:, 0:width]))

    p_ref = both_ref.at[:, width:]
    count = length_of(p_ref, own)
    spread, _ = scales_of(p_ref)
    run_forward(buf, width, p_ref, own_wl, own_wt, spread, count, (t_hi, t_lo), (u_hi, u_lo))


def adjoint_kernel(
    _, adj_ref, adj_after_ref, p_ref, wl, wt, wl_after, wt_after, t_after_hi, t_after_lo, t_hi, t_lo, u_hi, u_lo,
    adj_out_ref, g_ref, buf, lam_ref, q_ref, g_all,
):
    own = lax.axis_index("depth")
    last = lax.axis_size("depth") - 1
    rows, width = adj_out_ref.shape
    g_all[...] = jnp.zeros_like(g_all)

    @pl.when(own < last)
    def _():
        count = length_of(p_ref, jnp.minimum(own + 1, last))
        spread, _ = scales_of(p_ref)
        fill(buf, to_pairs(adj_after_ref[...]))
        run_backward(buf, width, wl_after, wt_after, spread, count, (t_after_hi, t_after_lo))

    @pl.when(own == last)
    def _():
        fill(buf, to_pairs(adj_ref[...]))

    spread, factor = scales_of(p_ref)
    run_backward(
        buf, width, wl, wt, spread, length_of(p_ref, own), (t_hi, t_lo), (u_hi, u_lo),
        (g_all, factor, lam_ref, q_ref),
    )
    adj_out_ref[...] = from_pairs(inner(buf))
    most = g_all.shape[0]
    g_ref[:, most * rows :] = jnp.zeros((rows, LANES), F32)
    for slot in range(most):
        g_ref[:, slot * rows : (slot + 1) * rows] = g_all[slot, :, 0:rows]
        g_ref[:, most * rows + slot : most * rows + slot + 1] = g_all[slot, :, rows : rows + 1]


def sum_kernel(*refs):
    parts, (gw_ref, gb_ref) = refs[:-2], refs[-2:]
    most, rows, _ = gw_ref.shape
    total = sum(part[...] for part in parts)
    for slot in range(most):
        gw_ref[slot] = total[:, slot * rows : (slot + 1) * rows]
    gb_ref[...] = total[:, most * rows :].T[:most, :]


def chain_kernel(plan, _, second_ref, p_ref, *rest):
    msgs, rest = rest[: plan.items], rest[plan.items :]
    outs, (buf, held, done, wl, wt, bias, sem) = rest[: plan.results], rest[plan.results :]
    own = lax.axis_index("depth")
    host = own - plan.first
    rows = held.shape[1]
    size = plan.rows * IMG
    piece = plan.block * IMG

    @pl.when(jnp.logical_and(host >= 0, host < plan.hosts))
    def _():
        if plan.hosts > 4:
            copies = [
                pltpu.make_async_copy(msg, held.at[lax.rem(host + shift, plan.items)], sem.at[shift])
                for shift, msg in enumerate(msgs)
            ]
            for copy in copies:
                copy.start()
            for copy in copies:
                copy.wait()
        for h in range(plan.hosts if plan.hosts <= 4 else 0):

            @pl.when(host == h)
            def _():
                for shift, msg in enumerate(msgs):
                    held[(h + shift) % plan.items] = msg[...]

        start = plan.window(host)
        offset = host * plan.block - start
        most = slots_of(p_ref)
        spread = table_of(p_ref)[:, most : most + 1] * (1.0 / most)
        for item in range(2, plan.items):
            ends = held[item, :, 0:LANES], held[item, :, size - LANES :]
            tile = jnp.where(start == 0, ends[1][:, IMG:], ends[0][:, :IMG])
            matrix = tile[:, 0:rows]
            scale = length_of(p_ref, item + 1).astype(F32) * (1.0 / most)
            wl[item] = left_factor(matrix)
            wt[item] = left_factor((scale * matrix).T)
            bias[item] = tile[:, rows : rows + 1]
        fill(buf, held[0] + held[1])

        def keep(result):
            done[result] = buf[:, pl.ds(pl.multiple_of(LANES + offset * IMG, LANES), piece)]

        keep(0)

        @pl.loop(2, plan.items)
        def _(item):
            forward_layer(
                buf, size, wl[item], wt[item], bias[item],
                length_of(p_ref, item + 1).astype(F32) * spread, paired=False,
            )
            buf[:, LANES : LANES + size] = inner(buf) + held[item]
            keep(item - 1)

        for shift, out in enumerate(outs):
            out[...] = done[lax.rem(host + shift, plan.results)]

    @pl.when(own == 0)
    def _():
        for shift, out in enumerate(outs):
            if shift < plan.hosts:
                out[...] = second_ref[:, shift * piece : (shift + 1) * piece]


def collect_kernel(plan, point_ref, local_ref, *rest):
    received, out_ref = rest[:-1], rest[-1]
    own = lax.axis_index("depth")
    host = own - plan.first

    @pl.when(own < 2)
    def _():
        out_ref[...] = point_ref[...]

    @pl.when(own == 2)
    def _():
        for shift, block in enumerate(received):
            if shift < plan.hosts:
                out_ref[:, lanes(shift * plan.block, plan.block)] = block[...]

    for shift, block in enumerate(received):
        sender = lax.rem(own - 3 - shift + 2 * plan.results, plan.results)

        @pl.when(jnp.logical_and(own > 2, jnp.logical_and(sender < plan.hosts, sender != host)))
        def _():
            out_ref[:, lanes(sender * plan.block, plan.block)] = block[...]

    @pl.when(jnp.logical_and(own > 2, jnp.logical_and(host >= 0, host < plan.hosts)))
    def _():
        out_ref[:, lanes(host * plan.block, plan.block)] = local_ref[...]


SMEM = pl.BlockSpec(memory_space=pltpu.SMEM)
VMEM = pl.BlockSpec(memory_space=pltpu.VMEM)
ANY = pl.BlockSpec(memory_space=pl.ANY)


def call(kernel, out_shape, in_specs, scratch, micros, name, mebi=32, moved=2**21):
    return pl.pallas_call(
        kernel,
        out_shape=out_shape,
        in_specs=in_specs,
        out_specs=jax.tree.map(lambda _: VMEM, out_shape),
        scratch_shapes=scratch,
        compiler_params=pltpu.CompilerParams(vmem_limit_bytes=mebi * 2**20),
        cost_estimate=pl.CostEstimate(flops=int(micros * 1e8), bytes_accessed=moved, transcendentals=0),
        name=name,
    )


def shifted(value, steps):
    count = lax.axis_size("depth")
    first, end = max(0, -steps), min(count, count - steps)
    return lax.ppermute(value, "depth", [(s, s + steps) for s in range(first, end)])


def others(value, step):
    count = lax.axis_size("batch")
    xor = count & (count - 1) == 0
    return lax.ppermute(value, "batch", [(s, s ^ step if xor else (s + step) % count) for s in range(count)])


def body(cpoint_guess, adjoint_guess, weights, biases, diffusion, section_len):
    plan = Plan(lax.axis_size("depth"))
    most, rows, _ = weights.shape
    width = cpoint_guess.shape[-1]
    guess, adjoint = cpoint_guess[0, 0], adjoint_guess[0, 0]

    def shape(*dims):
        return jax.ShapeDtypeStruct(dims, F32)

    state = shape(rows, width)
    buffer = pltpu.VMEM((rows, width + 2 * LANES), F32)
    factors = [pltpu.VMEM((most, rows, 3 * rows), BF16)] * 2

    wide = most * rows + LANES
    packed, packed0, both = call(
        pack_kernel, [shape(rows, wide), shape(rows, LANES), shape(rows, width + wide)], [ANY] * 5,
        [
            pltpu.VMEM(weights.shape, F32), pltpu.VMEM(biases.shape, F32), pltpu.VMEM((1, rows), F32),
            pltpu.VMEM((1, plan.count), jnp.int32), pltpu.SemaphoreType.DMA((5,)),
        ],
        1, "pack", 60,
    )(weights, biases, diffusion[None], section_len[None], guess)
    packed_after = shifted(packed, -1)
    packed_second = lax.ppermute(packed0, "depth", [(2, 0)])
    before = shifted(both, 1)
    saved = jax.ShapeDtypeStruct((most, rows, width), BF16)
    factor_shape = jax.ShapeDtypeStruct((most, rows, 3 * rows), BF16)
    window = shape(rows, plan.rows * IMG)
    second, own_wl, own_wt, wl, wt, t_after_hi, t_after_lo, *msgs = call(
        functools.partial(front_kernel, plan), [state] + [factor_shape] * 4 + [saved] * 2 + [window] * plan.items,
        [VMEM] * 3, [buffer, pltpu.VMEM(state.shape, F32), pltpu.VMEM(state.shape, F32)], 40, "front",
    )(both, packed_after, packed_second)
    arrived = {plan.first: msgs[plan.first]}
    order = plan.in_order()
    for k, shift in enumerate(order):
        msg = msgs[shift]
        if k >= AT_ONCE:
            msg, _ = lax.optimization_barrier((msg, arrived[order[k - AT_ONCE]]))
        arrived[shift] = lax.ppermute(msg, "depth", plan.in_pairs(shift))
    msgs = [arrived[shift] for shift in range(plan.items)]

    point, *kept = call(
        point_kernel, [state] + [saved] * 4, [ANY] + [VMEM] * 4, [buffer, *factors], 6, "point"
    )(msgs[plan.first], both, before, own_wl, own_wt)
    adjoint_later, _ = lax.optimization_barrier((adjoint, point))
    adj_after = shifted(adjoint_later, -1)

    piece = shape(rows, plan.block * IMG)
    blocks = call(
        functools.partial(chain_kernel, plan), [piece] * plan.results,
        [ANY, VMEM, VMEM] + [VMEM if plan.hosts <= 4 else ANY] * plan.items,
        [
            pltpu.VMEM((rows, plan.rows * IMG + 2 * LANES), F32),
            pltpu.VMEM((plan.items, *window.shape), F32),
            pltpu.VMEM((plan.results, *piece.shape), F32),
            pltpu.VMEM((plan.items, rows, 3 * rows), BF16),
            pltpu.VMEM((plan.items, rows, 3 * rows), BF16),
            pltpu.VMEM((plan.items, rows, 1), F32),
            pltpu.SemaphoreType.DMA((plan.items,)),
        ],
        40, "chain",
    )(point, second, packed, *msgs)
    received = {}
    for k in reversed(range(plan.results)):
        received[k] = lax.ppermute(blocks[k], "depth", plan.out_pairs(k))
    received = [received[k] for k in range(plan.results)]

    pair = pltpu.VMEM((2 * rows, width), BF16)
    adjoint_out, grads = call(
        adjoint_kernel, [state, shape(rows, wide)], [ANY] + [VMEM] * 13,
        [buffer, pair, pair, pltpu.VMEM((most, rows, rows + 1), F32)], 10, "adjoint",
    )(
        blocks[plan.local], adjoint, adj_after, packed, own_wl, own_wt, wl, wt, t_after_hi, t_after_lo, *kept
    )

    states = call(
        functools.partial(collect_kernel, plan), state, [VMEM] * (2 + plan.results), [], 0.5, "collect"
    )(point, blocks[plan.local], *received)
    grads, *_ = lax.optimization_barrier((grads, *received))
    parts = [grads] + [others(grads, step) for step in range(1, lax.axis_size("batch"))]
    gw, gb = call(
        sum_kernel, [shape(*weights.shape), shape(*biases.shape)], [VMEM] * len(parts), [], 0.5, "sum"
    )(*parts)
    return states[None, None], adjoint_out[None, None], gw, gb


def solution(mesh):
    state = P("depth", "batch", None, None)
    return jax.shard_map(
        body,
        mesh=mesh,
        in_specs=(state, state, P("depth", None, None), P("depth", None), P(), P()),
        out_specs=(state, state, P("depth", None, None), P("depth", None)),
        check_vma=False,
    )
```
